32 devices in a mesh: ctx: 8 (over z, x), tp: 4 (over y, core).
Axes of the slice: x: 2, y: 2, z: 4, core: 2. Of those that a mesh axis runs over, the one named last changes fastest.
Arguments:
- tokens: int32 [2048], P('ctx'), may hold values from 0 to 3
- rc_map: int32 [4], replicated, may hold values from 0 to 3, each once
- embedding: bfloat16 [4, 2048], replicated, may hold values from -6 to 6
- norm_gain: float32 [2048], replicated, may hold values from 0.5 to 1.5
- w_values: bfloat16 [2048, 4096], P(None, 'tp'), may hold values from -0.125 to 0.125
- w_gates: bfloat16 [2048, 4096], P(None, 'tp'), may hold values from -0.125 to 0.125
- w_states: bfloat16 [2048, 256], replicated, may hold values from -0.125 to 0.125
- w_steps: bfloat16 [2048, 32], P(None, 'tp'), may hold values from -0.125 to 0.125
- conv_values: float32 [4, 4096], P(None, 'tp'), may hold values from -0.5 to 0.5
- conv_states: float32 [4, 256], replicated, may hold values from -0.5 to 0.5
- step_bias: float32 [32], P('tp'), may hold values from -1 to 1
- log_rate: float32 [32], P('tp'), as said below
- skip_gain: float32 [32], P('tp'), may hold values from 0.5 to 1.5
- head_gain: float32 [4096], P('tp'), may hold values from 0.5 to 1.5
- cotangent: bfloat16 [2048, 4096], P('ctx', 'tp'), may hold values from -6 to 6
Outputs:
- encoded: bfloat16 [2048, 4096], P('ctx', 'tp')
- grad_log_rate: float32 [32], replicated
- grad_step_bias: float32 [32], replicated
- grad_conv_states: float32 [4, 256], replicated
The draws below stay inside these ranges and needn't reach their ends.
Inputs may be any that keep to these rules, and one draw needn't show every extreme that they name: `rc_map`: a permutation of the four ids. exp(log_rate) lies between 0.3 / 2048 and 0.1.
All inputs are finite; a program needn't handle non-finite values.
Results may differ from the reference program's by a relative error of at most 0.001.
The reference program's roundings to bfloat16 on the way (of `normed`) count: a program that leaves them out, or rounds other values in their place, can miss the bound.
Values sent between devices are 32-bit elements; how exact they have to be, the bound alone decides.
No kernel may reach another device: no remote copies, remote signals or barrier semaphores. Data moves between devices by JAX's collectives and lax.ppermute only.
A program may use at most 128 MiB of HBM per device.

```python
import math
import jax
import jax.numpy as jnp
from jax import lax

D = 2048
H = 32
HEAD = 128
STATE = 128
GROUP = 256
CONV = 4
DI = 4096
TOKENS = 2048


def draw_log_rate(key, part):
    key_kind, key_slow, key_fast = jax.random.split(jax.random.fold_in(key, 11), 3)
    slow_share = 0.5
    slow_mask = jax.random.uniform(key_kind, (H,)) < slow_share
    slow_logs = jax.random.uniform(key_slow, (H,), minval=jnp.log(0.3), maxval=jnp.log(2.0)) - jnp.log(1.0 * TOKENS)
    fast_logs = jax.random.uniform(key_fast, (H,), minval=jnp.log(0.03), maxval=jnp.log(0.1))
    return jnp.where(slow_mask, slow_logs, fast_logs).astype(jnp.float32)


def set_ends(drawn, own_key, low, high):
    dims = drawn.shape
    index_at = [jax.random.randint(jax.random.fold_in(own_key, axis), (), 0, dims[axis]) for axis in range(len(dims))]
    drawn = drawn.at[tuple(index_at)].set(low)
    longest = dims.index(max(dims))
    index_at[longest] = (index_at[longest] + 1) % dims[longest]
    return drawn.at[tuple(index_at)].set(high)


def levels(key, dims, pieces, smallest, largest):
    gain = 1.0
    for dim, parts in pieces:
        steps = jax.random.uniform(jax.random.fold_in(jax.random.fold_in(key, 6), dim), (parts,), jnp.float32, smallest / len(pieces), largest / len(pieces))
        gain = gain * jnp.repeat(jnp.exp(steps), dims[dim] // parts).reshape((-1,) + (1,) * (len(dims) - 1 - dim))
    return gain


def normal_values(rng, shape, spread, most, shards=(), kind=jnp.bfloat16):
    entries = jax.random.normal(rng, shape, jnp.float32) * spread
    if len(shards) > 0:
        entries = levels(rng, shape, shards, -0.22, 0.18) * entries
    return jnp.clip(entries, min=-most, max=most).astype(kind)


def setup_inputs(seed: int = 0) -> dict:
    splits = jax.random.split(jax.random.key(seed), 16)
    tokens = set_ends(jax.random.randint(splits[0], (TOKENS,), 0, 4), jax.random.fold_in(splits[0], 1), 0, 3).astype(jnp.int32)
    rc_map = jax.random.permutation(splits[1], 4).astype(jnp.int32)
    embedding = normal_values(splits[2], (4, D), 1.0, 6.0)
    norm_gain = jnp.clip(1.0 + 0.1 * jax.random.normal(splits[3], (D,), jnp.float32), 0.5, 1.5)
    w_values = normal_values(splits[4], (D, DI), D ** -0.5, 0.125, ((1, 4),))
    w_gates = normal_values(splits[5], (D, DI), D ** -0.5, 0.125, ((1, 4),))
    w_states = normal_values(splits[6], (D, 2 * STATE), D ** -0.5, 0.125)
    w_steps = normal_values(splits[7], (D, H), D ** -0.5, 0.125, ((1, 4),))
    conv_values = jnp.clip(jax.random.uniform(splits[8], (CONV, DI), jnp.float32, -0.5, 0.5) * levels(splits[8], (CONV, DI), ((1, 4),), -0.4, 0.0), -0.5, 0.5)
    conv_states = jnp.clip(jax.random.uniform(splits[9], (CONV, 2 * STATE), jnp.float32, -0.5, 0.5), -0.5, 0.5)
    step_bias = jnp.clip(jax.random.uniform(splits[10], (H,), jnp.float32, -1.0, 1.0) * levels(splits[10], (H,), ((0, 4),), -0.4, 0.0), -1.0, 1.0)
    log_rate = draw_log_rate(jax.random.fold_in(splits[15], 71), 0)
    skip_gain = jnp.clip(0.5 + 1.0 * jax.random.uniform(splits[12], (H,), jnp.float32) ** levels(splits[12], (H,), ((0, 4),), -0.2, 0.2), 0.5, 1.5)
    head_gain = jnp.clip(1.0 + 0.1 * jax.random.normal(splits[13], (DI,), jnp.float32), 0.5, 1.5)
    cotangent = normal_values(splits[14], (TOKENS, DI), 1.0, 6.0, ((0, 8), (1, 4)))
    return {"tokens": tokens, "rc_map": rc_map, "embedding": embedding, "norm_gain": norm_gain, "w_values": w_values, "w_gates": w_gates, "w_states": w_states, "w_steps": w_steps, "conv_values": conv_values, "conv_states": conv_states, "step_bias": step_bias, "log_rate": log_rate, "skip_gain": skip_gain, "head_gain": head_gain, "cotangent": cotangent}


epsilon = 1e-05
highest = lax.Precision.HIGHEST

def lookup(token_ids, lookup_table):
    onehot = (token_ids[:, None] == jnp.arange(4, dtype=jnp.int32)[None, :]).astype(jnp.float32)
    return jnp.dot(onehot, lookup_table, precision=highest, preferred_element_type=jnp.float32)

def group_step(carry_state, inputs):
    values, keys_b, queries_c, steps_dt, log_decay = inputs
    cumulative = jnp.cumsum(log_decay, axis=0)
    length = log_decay.shape[0]
    causal = (jnp.arange(length)[:, None] >= jnp.arange(length)[None, :])[:, :, None]
    differences = cumulative[:, None, :] - cumulative[None, :, :]
    decays = jnp.where(causal, jnp.exp(jnp.where(causal, differences, 0.0)), 0.0)
    scores = jnp.dot(queries_c, keys_b.T, precision=highest)
    mixing = scores[:, :, None] * decays * steps_dt[None, :, :]
    within = jnp.einsum('tsh,shp->thp', mixing, values, precision=highest)
    carried = jnp.exp(cumulative)[:, :, None] * jnp.einsum('tn,hnp->thp', queries_c, carry_state, precision=highest)
    end_weights = jnp.exp(cumulative[-1][None, :] - cumulative) * steps_dt
    fresh_state = jnp.einsum('sh,sn,shp->hnp', end_weights, keys_b, values, precision=highest)
    new_state = jnp.exp(cumulative[-1])[:, None, None] * carry_state + fresh_state
    return (new_state, within + carried)

def gate_norm(outputs, gate_rows, head_gain):
    own_count, head_count, head_size = outputs.shape
    gated_rows = outputs * jax.nn.silu(gate_rows).reshape(own_count, head_count, head_size)
    scaled = gated_rows * lax.rsqrt(lax.optimization_barrier(jnp.mean(gated_rows * gated_rows, axis=2, keepdims=True)) + epsilon)
    return scaled.reshape(own_count, head_count * head_size) * head_gain

def strand_output(rate_in, bias_in, conv_in, token_ids, tables, conv_values, skip_gain, head_gain):
    table_vs, table_z, table_dt = tables
    own_count = token_ids.shape[0]
    projected = lookup(token_ids, table_vs)
    padded = jnp.concatenate([jnp.zeros((CONV - 1, projected.shape[1]), jnp.float32), projected], axis=0)
    conv_weights = jnp.concatenate([conv_values, conv_in], axis=1)
    summed = sum((conv_weights[shift_tap] * padded[shift_tap:shift_tap + own_count] for shift_tap in range(CONV)))
    activated = jax.nn.silu(summed)
    inner_width = conv_values.shape[1]
    head_count = inner_width // HEAD
    values = activated[:, :inner_width].reshape(own_count, head_count, HEAD)
    keys_b = activated[:, inner_width:inner_width + STATE]
    queries_c = activated[:, inner_width + STATE:]
    steps_dt = jax.nn.softplus(lookup(token_ids, table_dt) + bias_in)
    log_decay = -jnp.exp(rate_in) * steps_dt
    blocks = own_count // GROUP

    def to_blocks(member):
        return member.reshape((blocks, GROUP) + member.shape[1:])
    zero_state = jnp.zeros((head_count, STATE, HEAD), jnp.float32)
    grouped = tuple((to_blocks(member) for member in (values, keys_b, queries_c, steps_dt, log_decay)))
    _, rows_out = lax.scan(jax.checkpoint(group_step), zero_state, grouped)
    outputs = rows_out.reshape(own_count, head_count, HEAD) + skip_gain[None, :, None] * values
    return gate_norm(outputs, lookup(token_ids, table_z), head_gain)

def reference(tokens, rc_map, embedding, norm_gain, w_values, w_gates, w_states, w_steps, conv_values, conv_states, step_bias, log_rate, skip_gain, head_gain, cotangent):
    embedded = embedding.astype(jnp.float32)
    normed = (embedded * lax.rsqrt(lax.optimization_barrier(jnp.mean(embedded * embedded, axis=1, keepdims=True)) + epsilon) * norm_gain).astype(jnp.bfloat16)
    table_vs = jnp.concatenate([jnp.dot(normed, w_values, preferred_element_type=jnp.float32), jnp.dot(normed, w_states, preferred_element_type=jnp.float32)], axis=1)
    table_z = jnp.dot(normed, w_gates, preferred_element_type=jnp.float32)
    table_dt = jnp.dot(normed, w_steps, preferred_element_type=jnp.float32)
    tables = (table_vs, table_z, table_dt)
    rc_tokens = lax.optimization_barrier(jnp.sum(jnp.where(tokens[:, None] == jnp.arange(4, dtype=jnp.int32)[None, :], rc_map[None, :], 0), axis=1)).astype(jnp.int32)

    def both_strands(rate_in, bias_in, conv_in):
        forward_rows = strand_output(rate_in, bias_in, conv_in, tokens, tables, conv_values, skip_gain, head_gain)
        reverse_rows = strand_output(rate_in, bias_in, conv_in, rc_tokens[::-1], tables, conv_values, skip_gain, head_gain)
        return forward_rows + reverse_rows[::-1]
    summed, pullback = jax.vjp(both_strands, log_rate, step_bias, conv_states)
    loss_scale = 1.0 / math.sqrt(TOKENS * HEAD)
    grads = pullback(cotangent.astype(jnp.float32) * loss_scale)
    return (summed.astype(jnp.bfloat16), grads[0], grads[1], grads[2])
```

```python
import functools
import math

import jax
import jax.numpy as jnp
from jax import lax
from jax.experimental import pallas as pl
from jax.experimental.pallas import tpu as pltpu
from jax.sharding import PartitionSpec as P

HEAD = 128
STATE = 128
CONV = 4
IDS = 4
WINDOWS = IDS**CONV
ROWS = WINDOWS + 16
EPSILON = 1e-05

f32 = jnp.float32
bf16 = jnp.bfloat16
NN = (((1,), (0,)), ((), ()))
NT = (((1,), (1,)), ((), ()))
TN = (((0,), (0,)), ((), ()))


def iota(shape, dim):
    return lax.broadcasted_iota(jnp.int32, shape, dim)


def mm(a, b, dims=NN):
    return lax.dot_general(a, b, dims, preferred_element_type=f32)


def split(x):
    high = x.astype(bf16)
    return high, (x - high.astype(f32)).astype(bf16)


def mm3(a, b, dims=NN):
    return mm(a[0], b[0], dims) + (mm(a[0], b[1], dims) + mm(a[1], b[0], dims))


def sigmoid(v):
    return 1.0 / (1.0 + jnp.exp(-v))


def tables_kernel(emb_ref, gain_ref, wv_ref, wg_ref, ws_ref, wt_ref, tv_ref, tz_ref, tbc_ref, dt_ref):
    embedded = emb_ref[...].astype(f32)
    mean = jnp.mean(embedded * embedded, axis=1, keepdims=True)
    normed = (embedded * lax.rsqrt(mean + EPSILON) * gain_ref[...]).astype(bf16)
    for out, weights in ((tv_ref, wv_ref), (tz_ref, wg_ref), (tbc_ref, ws_ref)):
        out[0:IDS, :] = mm(normed, weights[...])
        out[IDS:, :] = jnp.zeros((8 - IDS, out.shape[1]), f32)
    dt_ref[...] = mm(wt_ref[...], normed, NT)


def tables(embedding, norm_gain, w_values, w_gates, w_states, w_steps):
    depth, width = w_values.shape
    heads = w_steps.shape[1]
    steps = width // 256
    state_blocks = w_states.shape[1] // 128
    whole = lambda shape: pl.BlockSpec(shape, lambda i: (0, 0))
    columns = lambda rows, size: pl.BlockSpec((rows, size), lambda i: (0, i))
    states = lambda rows: pl.BlockSpec((rows, 128), lambda i: (0, jnp.minimum(i, state_blocks - 1)))
    return pl.pallas_call(
        tables_kernel,
        grid=(steps,),
        in_specs=[
            whole(embedding.shape),
            whole((1, depth)),
            columns(depth, 256),
            columns(depth, 256),
            states(depth),
            whole((heads, depth)),
        ],
        out_specs=[columns(8, 256), columns(8, 256), states(8), whole((heads, IDS))],
        out_shape=[
            jax.ShapeDtypeStruct((8, width), f32),
            jax.ShapeDtypeStruct((8, width), f32),
            jax.ShapeDtypeStruct((8, w_states.shape[1]), f32),
            jax.ShapeDtypeStruct((heads, IDS), f32),
        ],
        compiler_params=pltpu.CompilerParams(vmem_limit_bytes=24 * 2**20),
        name="tables",
    )(embedding, norm_gain.reshape(1, depth), w_values, w_gates, w_states, w_steps.T)


def mixer_kernel(
    scale,
    tok_ref,
    rc_ref,
    place_ref,
    skip_ref,
    tv_ref,
    tbc_ref,
    tz_ref,
    dt_ref,
    cv_ref,
    cs_ref,
    bias_ref,
    rate_ref,
    gain_ref,
    cot_ref,
    enc_ref,
    grad_ref,
    tok_s,
    ids_s,
    count_s,
    onehot_s,
    weight_s,
    x_s,
    xh_s,
    xl_s,
    wh_s,
    wl_s,
    lh_s,
    ll_s,
    far_s,
    dh_s,
    dl_s,
    row_s,
    lcol_s,
    acol_s,
    tcol_s,
    gate_s,
    score_s,
    q_s,
    acc_s,
):
    devices, count = tok_ref.shape
    width = tv_ref.shape[1]
    heads = width // HEAD
    here = place_ref[0]
    tp_place = place_ref[1]

    for r in range(devices):
        tok_s[pl.ds(jnp.bitwise_xor(here, r), 1), :] = tok_ref[r : r + 1, :]
    tok = tok_s[...]
    rc = [rc_ref[t] for t in range(IDS)]
    rtok = jnp.zeros_like(tok)
    for t in range(IDS):
        rtok = jnp.where(tok == t, rc[t], rtok)
    lane = iota((devices, count), 1)
    row = iota((devices, count), 0)

    def before(ids, shift):
        turned = pltpu.roll(ids, shift, 1)
        return jnp.where(lane < shift, pltpu.roll(turned, 1, 0), turned)

    def after(ids, shift):
        turned = pltpu.roll(ids, count - shift, 1)
        return jnp.where(lane >= count - shift, pltpu.roll(turned, devices - 1, 0), turned)

    kf = before(tok, 3) + IDS * before(tok, 2) + IDS**2 * before(tok, 1) + IDS**3 * tok
    kr = after(rtok, 3) + IDS * after(rtok, 2) + IDS**2 * after(rtok, 1) + IDS**3 * rtok
    first = row * count + lane
    last = devices * count - 1 - first
    kf = jnp.where(first < CONV - 1, WINDOWS + first, kf)
    kr = jnp.where(last < CONV - 1, WINDOWS + CONV - 1 + last, kr)
    ids_s[0] = kf
    ids_s[1] = kr

    eye = iota((heads, heads), 0) == iota((heads, heads), 1)
    column = lambda ref: jnp.sum(jnp.where(eye, ref[...], 0.0), axis=1, keepdims=True)
    raw = dt_ref[...] + column(bias_ref)
    rate = jnp.exp(column(rate_ref))
    step = jnp.maximum(raw, 0.0) + jnp.log1p(jnp.exp(-jnp.abs(raw)))
    slope = sigmoid(raw)
    ratio = jnp.where(step > 1e-37, slope / jnp.maximum(step, 1e-37), 1.0)

    def per_strand(table):
        own = [table[:, t : t + 1] for t in range(IDS)]
        mapped = []
        for t in range(IDS):
            picked = own[0]
            for other in range(1, IDS):
                picked = jnp.where(rc[t] == other, own[other], picked)
            mapped.append(picked)
        return own, mapped

    step_of, slope_of, ratio_of = per_strand(step), per_strand(slope), per_strand(ratio)
    log_of, alog_of = per_strand(-rate * step), per_strand(-rate * slope)

    masks = [(tok == t).astype(f32) for t in range(IDS)]
    upper = (iota((count, count), 0) <= iota((count, count), 1)).astype(bf16)
    for t in range(IDS):
        count_s[t] = mm(masks[t].astype(bf16), upper)
    totals = [jnp.sum(m, axis=1, keepdims=True) for m in masks]
    row1 = iota((devices, 1), 0)
    far_counts = []
    for t in range(IDS):
        between = jnp.zeros((devices, 1), f32)
        for j in range(devices):
            inside = ((row1 < j) & (j < here)) | ((row1 > j) & (j > here))
            between = between + jnp.where(inside, totals[t][j : j + 1, :], 0.0)
        inclusive = count_s[t]
        far_counts.append(
            jnp.where(row < here, totals[t] - inclusive, inclusive - masks[t]) + between
        )

    window_rows = iota((ROWS, count), 0)
    for j in range(devices):
        forward = j < here
        reverse = j > here
        choose = lambda pair, t: jnp.where(forward, pair[0][t], pair[1][t])
        tok_j = tok[j : j + 1, :]
        log_sum = jnp.zeros((heads, count), f32)
        alog_sum = jnp.zeros((heads, count), f32)
        step_j = jnp.zeros((heads, count), f32)
        slope_j = jnp.zeros((heads, count), f32)
        for t in range(IDS):
            number = far_counts[t][j : j + 1, :]
            log_sum = log_sum + choose(log_of, t) * number
            alog_sum = alog_sum + choose(alog_of, t) * number
            step_j = jnp.where(tok_j == t, choose(step_of, t), step_j)
            slope_j = jnp.where(tok_j == t, choose(slope_of, t), slope_j)
        decay = jnp.exp(log_sum)
        weight = decay * step_j
        terms = jnp.concatenate([weight, weight * log_sum, decay * (slope_j + step_j * alog_sum)], axis=0)
        both = jnp.concatenate(
            [
                jnp.where(forward, terms, 0.0),
                jnp.where(reverse, terms, 0.0),
                jnp.zeros((64 - 6 * heads, count), f32),
            ],
            axis=0,
        )
        high, low = split(both)
        weight_s[0:64, j * count : (j + 1) * count] = high
        weight_s[64:128, j * count : (j + 1) * count] = low
        window_j = jnp.where(forward, kf[j : j + 1, :], kr[j : j + 1, :])
        onehot_s[:, j * count : (j + 1) * count] = (window_rows == window_j).astype(bf16)
    weights = mm(onehot_s[...], weight_s[...], NT)
    weights = weights + pltpu.roll(weights, 64, 1)

    lane_w = iota((WINDOWS, 128), 1)
    tap_w = (lane_w >> 3) & 3
    digit = (iota((WINDOWS, 128), 0) >> (2 * tap_w)) & 3
    lane_e = iota((16, 128), 1)
    row_e = iota((16, 128), 0)
    tap_e = (lane_e >> 3) & 3
    edge = jnp.full((16, 128), IDS, jnp.int32)
    for u in range(CONV - 1):
        for k in range(CONV - 1 - u, CONV):
            at = u - (CONV - 1) + k
            edge = jnp.where((row_e == u) & (tap_e == k), tok[0:1, at : at + 1], edge)
            edge = jnp.where(
                (row_e == CONV - 1 + u) & (tap_e == k),
                rtok[devices - 1 : devices, count - 1 - at : count - at],
                edge,
            )
    chosen = jnp.concatenate([digit, edge], axis=0)
    lane_r = iota((ROWS, 128), 1)
    pick = ((chosen == (lane_r & 7)) & (lane_r < 96)).astype(f32).astype(bf16)

    def windows(table, taps_ref):
        product = jnp.concatenate([taps_ref[k : k + 1, :] * table for k in range(CONV)], axis=0)
        p1 = product.astype(bf16)
        rest = product - p1.astype(f32)
        p2 = rest.astype(bf16)
        p3 = (rest - p2.astype(f32)).astype(bf16)
        return mm(pick, jnp.concatenate([p1, p2, p3, jnp.zeros_like(p1)], axis=0))

    summed = windows(tv_ref[...], cv_ref)
    x_all = summed * sigmoid(summed)
    x_s[...] = x_all
    xh_s[...], xl_s[...] = split(x_all)
    table_bc = tbc_ref[...]
    summed = windows(table_bc, cs_ref)
    sig = sigmoid(summed)
    bc_all = summed * sig
    bc_slope = sig * (1.0 + summed * (1.0 - sig))
    bc = split(bc_all)
    b_all = (bc[0][:, :STATE], bc[1][:, :STATE])

    own_tok = tok_s[pl.ds(here, 1), :]
    own_masks = [(own_tok == t).astype(f32) for t in range(IDS)]
    own_counts = [[], []]
    for t in range(IDS):
        inclusive = count_s[t, pl.ds(here, 1), :]
        total = jnp.sum(own_masks[t], axis=1, keepdims=True)
        own_counts[0].append(inclusive)
        own_counts[1].append(total - inclusive + own_masks[t])
    turned = []
    for s in range(2):
        logs = sum(log_of[s][t] * own_counts[s][t] for t in range(IDS))
        alogs = sum(alog_of[s][t] * own_counts[s][t] for t in range(IDS))
        row_s[s, 0] = logs
        row_s[s, 1] = sum(step_of[s][t] * own_masks[t] for t in range(IDS))
        row_s[s, 2] = sum(ratio_of[s][t] * own_masks[t] for t in range(IDS)) - alogs
        turned += [logs, alogs]
    own_ids = [ids_s[s, pl.ds(here, 1), :] for s in range(2)]
    extra = jnp.concatenate(
        [own_ids[0].astype(f32), own_ids[1].astype(f32), own_tok.astype(f32), jnp.zeros((5, count), f32)],
        axis=0,
    )
    turned = jnp.concatenate(turned + [extra, jnp.zeros((120 - 4 * heads, count), f32)], axis=0).T
    for s in range(2):
        for h in range(heads):
            at = 2 * s * heads + h
            lcol_s[s, h] = jnp.broadcast_to(turned[:, at : at + 1], (count, 128))
            acol_s[s, h] = jnp.broadcast_to(turned[:, at + heads : at + heads + 1], (count, 128))
    base = 4 * heads
    tcol_s[...] = jnp.broadcast_to(turned[:, base + 2 : base + 3], (count, 128))
    gates = tz_ref[...]
    gates = gates * sigmoid(gates)
    gate_s[0] = gates
    for t in range(IDS):
        picked = gates[0:1, :]
        for other in range(1, IDS):
            picked = jnp.where(rc[t] == other, gates[other : other + 1, :], picked)
        gate_s[1, t : t + 1, :] = picked

    own_onehot = []
    own_bc = []
    states = []
    lane_k = iota((count, ROWS), 1).astype(f32)
    for s in range(2):
        picks = (lane_k == turned[:, base + s : base + s + 1]).astype(f32).astype(bf16)
        own_onehot.append((window_rows == own_ids[s]).astype(f32).astype(bf16))
        lh_s[s] = mm(picks, xh_s[...]).astype(bf16)
        ll_s[s] = mm(picks, xl_s[...]).astype(bf16)
        own_bc.append((mm(picks, bc[0]).astype(bf16), mm(picks, bc[1]).astype(bf16)))
        own_b = tuple(part[:, :STATE] for part in own_bc[s])
        own_c = tuple(part[:, STATE:] for part in own_bc[s])
        score_s[s] = mm3(own_c, own_b, NT)
        for h in range(heads):
            at = 3 * s * heads + h
            columns = slice(h * HEAD, (h + 1) * HEAD)
            weighted = split(x_s[:, columns] * weights[:, at : at + 1])
            wh_s[s, :, columns], wl_s[s, :, columns] = weighted
        states.append(split(mm3(b_all, (wh_s[s], wl_s[s]), TN)))
        far_s[s] = mm3(own_c, states[s])

    q_s[...] = jnp.zeros_like(q_s)
    sub = iota((count, count), 0)
    lan = iota((count, count), 1)

    def one_head(h, _):
        columns = pl.ds(pl.multiple_of(h * HEAD, HEAD), HEAD)
        gain = gain_ref[:, columns]
        cot = cot_ref[:, columns].astype(f32) * scale * gain
        tcol = tcol_s[...]
        total_out = jnp.zeros((count, HEAD), f32)
        rate_row = jnp.zeros((1, 128), f32)
        bias_row = jnp.zeros((1, 128), f32)
        for s in range(2):
            lcol = lcol_s[s, h]
            log_row = row_s[s, 0, pl.ds(h, 1), :]
            step_row = row_s[s, 1, pl.ds(h, 1), :]
            mixed_row = row_s[s, 2, pl.ds(h, 1), :]
            causal = (sub >= lan) if s == 0 else (sub <= lan)
            wide = jnp.concatenate([lcol] * (count // 128), axis=1)
            factor = jnp.exp(jnp.where(causal, wide - log_row, -1e30)) * step_row
            mixing = score_s[s] * factor
            x = (lh_s[s, :, columns], ll_s[s, :, columns])
            grown = jnp.exp(lcol)
            y = mm3(split(mixing), x) + grown * far_s[s, :, columns]
            gate = gate_s[s, 0:1, columns]
            for t in range(1, IDS):
                gate = jnp.where(tcol == t, gate_s[s, t : t + 1, columns], gate)
            gated = (y + skip_ref[h] * (x[0].astype(f32) + x[1].astype(f32))) * gate
            inverse = lax.rsqrt(jnp.mean(gated * gated, axis=1, keepdims=True) + EPSILON)
            total_out = total_out + gated * inverse * gain
            shared = jnp.mean(cot * gated, axis=1, keepdims=True) * (inverse * inverse)
            dy = (cot - gated * shared) * inverse * gate
            e = mm3(split(dy), x, NT)
            q_s[s] += e * factor
            column_sum = jnp.sum(e * mixing, axis=0, keepdims=True)
            row_terms = dy * y
            fold = lambda v: sum(v[:, i * 128 : (i + 1) * 128] for i in range(count // 128))
            rate_row += jnp.sum(lcol * row_terms, axis=0, keepdims=True) - fold(log_row * column_sum)
            bias_row += jnp.sum(acol_s[s, h] * row_terms, axis=0, keepdims=True) + fold(mixed_row * column_sum)
            dh_s[s, :, columns], dl_s[s, :, columns] = split(grown * dy)
        enc_ref[:, columns] = total_out.astype(enc_ref.dtype)
        acc_s[0, pl.ds(h, 1), :] = rate_row
        acc_s[1, pl.ds(h, 1), :] = bias_row
        return 0

    lax.fori_loop(0, heads, one_head, 0)

    db_all = jnp.zeros((ROWS, STATE), f32)
    dc_all = jnp.zeros((ROWS, STATE), f32)
    for s in range(2):
        own_b = tuple(part[:, :STATE] for part in own_bc[s])
        own_c = tuple(part[:, STATE:] for part in own_bc[s])
        q = split(q_s[s])
        grown = (dh_s[s], dl_s[s])
        dc_own = split(mm3(q, own_b) + mm3(grown, states[s], NT))
        db_own = split(mm3(q, own_c, TN))
        back = split(mm3(own_c, grown, TN))
        dc_all = dc_all + (mm(own_onehot[s], dc_own[0]) + mm(own_onehot[s], dc_own[1]))
        db_all = db_all + (mm(own_onehot[s], db_own[0]) + mm(own_onehot[s], db_own[1]))
        db_all = db_all + mm3((wh_s[s], wl_s[s]), back, NT)
        reach = mm3(b_all, back)
        for h in range(heads):
            at = 3 * s * heads + heads + h
            columns = slice(h * HEAD, (h + 1) * HEAD)
            terms = reach[:, columns] * x_s[:, columns]
            acc_s[0, h : h + 1, :] += jnp.sum(terms * weights[:, at : at + 1], axis=0, keepdims=True)
            acc_s[1, h : h + 1, :] += jnp.sum(
                terms * weights[:, at + heads : at + heads + 1], axis=0, keepdims=True
            )
    d_summed = split(jnp.concatenate([db_all, dc_all], axis=1) * bc_slope)
    by_tap = mm(pick, d_summed[0], TN) + mm(pick, d_summed[1], TN)
    grad_ref[...] = jnp.zeros_like(grad_ref)
    for k in range(CONV):
        grad_ref[k : k + 1, :] = jnp.sum(by_tap[8 * k : 8 * k + 8, :] * table_bc, axis=0, keepdims=True)
    place = iota((heads, 128), 1) == iota((heads, 128), 0) + tp_place * heads
    for i in range(2):
        sums = jnp.sum(acc_s[i], axis=1, keepdims=True)
        grad_ref[CONV + i : CONV + i + 1, 0:128] = jnp.sum(jnp.where(place, sums, 0.0), axis=0, keepdims=True)


def mixer(tokens, rc_map, place, skip, tabs, conv_values, conv_states, bias, rate, gain, cotangent, scale):
    devices, count = tokens.shape
    width = conv_values.shape[1]
    heads = width // HEAD
    tv, tz, tbc, dt = tabs
    vmem = pl.BlockSpec(memory_space=pltpu.VMEM)
    smem = pl.BlockSpec(memory_space=pltpu.SMEM)
    scratch = [
        ((devices, count), jnp.int32),
        ((2, devices, count), jnp.int32),
        ((IDS, devices, count), f32),
        ((ROWS, devices * count), bf16),
        ((128, devices * count), bf16),
        ((ROWS, width), f32),
        ((ROWS, width), bf16),
        ((ROWS, width), bf16),
        ((2, ROWS, width), bf16),
        ((2, ROWS, width), bf16),
        ((2, count, width), bf16),
        ((2, count, width), bf16),
        ((2, count, width), f32),
        ((2, count, width), bf16),
        ((2, count, width), bf16),
        ((2, 3, heads, count), f32),
        ((2, heads, count, 128), f32),
        ((2, heads, count, 128), f32),
        ((count, 128), f32),
        ((2, 8, width), f32),
        ((2, count, count), f32),
        ((2, count, count), f32),
        ((2, heads, 128), f32),
    ]
    return pl.pallas_call(
        functools.partial(mixer_kernel, scale),
        in_specs=[vmem, smem, smem, smem] + [vmem] * 10,
        out_specs=[vmem, vmem],
        out_shape=[
            jax.ShapeDtypeStruct((count, width), bf16),
            jax.ShapeDtypeStruct((8, 2 * STATE), f32),
        ],
        scratch_shapes=[pltpu.VMEM(shape, kind) for shape, kind in scratch],
        compiler_params=pltpu.CompilerParams(vmem_limit_bytes=52 * 2**20),
        name="mixer",
    )(
        tokens,
        rc_map,
        place,
        skip,
        tv,
        tbc,
        tz,
        dt,
        conv_values,
        conv_states,
        bias.reshape(1, heads),
        rate.reshape(1, heads),
        gain.reshape(1, width),
        cotangent,
    )


def exchange(value, axis, distance):
    size = lax.axis_size(axis)
    return lax.ppermute(value, axis, [(i, i ^ distance) for i in range(size)])


def on_device(
    tokens,
    rc_map,
    embedding,
    norm_gain,
    w_values,
    w_gates,
    w_states,
    w_steps,
    conv_values,
    conv_states,
    step_bias,
    log_rate,
    skip_gain,
    head_gain,
    cotangent,
):
    devices = lax.axis_size("ctx")
    count = tokens.shape[0]
    everyone = tokens.reshape(1, count)
    distance = 1
    while distance < devices:
        everyone = jnp.concatenate([everyone, exchange(everyone, "ctx", distance)], axis=0)
        distance *= 2
    tabs = tables(embedding, norm_gain, w_values, w_gates, w_states, w_steps)
    place = jnp.stack([lax.axis_index("ctx"), lax.axis_index("tp")]).astype(jnp.int32)
    scale = 1.0 / math.sqrt(count * devices * HEAD)
    encoded, grads = mixer(
        everyone,
        rc_map,
        place,
        skip_gain,
        tabs,
        conv_values,
        conv_states,
        step_bias,
        log_rate,
        head_gain,
        cotangent,
        scale,
    )
    for axis in ("tp", "ctx"):
        distance = 1
        while distance < lax.axis_size(axis):
            grads = grads + exchange(grads, axis, distance)
            distance *= 2
    head_total = log_rate.shape[0] * lax.axis_size("tp")
    return (encoded, grads[CONV, :head_total], grads[CONV + 1, :head_total], grads[:CONV])


def solution(mesh):
    placed = (
        P("ctx"),
        P(),
        P(),
        P(),
        P(None, "tp"),
        P(None, "tp"),
        P(),
        P(None, "tp"),
        P(None, "tp"),
        P(),
        P("tp"),
        P("tp"),
        P("tp"),
        P("tp"),
        P("ctx", "tp"),
    )
    return jax.shard_map(
        on_device,
        mesh=mesh,
        in_specs=placed,
        out_specs=(P("ctx", "tp"), P(), P(), P()),
        check_vma=False,
    )
```

```python
import functools
import math

import jax
import jax.numpy as jnp
from jax import lax
from jax.experimental import pallas as pl
from jax.experimental.pallas import tpu as pltpu
from jax.sharding import PartitionSpec as P

HEAD = 128
STATE = 128
CONV = 4
IDS = 4
WINDOWS = IDS**CONV
ROWS = WINDOWS + 16
EPSILON = 1e-05

f32 = jnp.float32
bf16 = jnp.bfloat16
NN = (((1,), (0,)), ((), ()))
NT = (((1,), (1,)), ((), ()))
TN = (((0,), (0,)), ((), ()))


def iota(shape, dim):
    return lax.broadcasted_iota(jnp.int32, shape, dim)


def mm(a, b, dims=NN):
    return lax.dot_general(a, b, dims, preferred_element_type=f32)


def split(x):
    high = x.astype(bf16)
    return high, (x - high.astype(f32)).astype(bf16)


def mm3(a, b, dims=NN):
    return mm(a[0], b[0], dims) + (mm(a[0], b[1], dims) + mm(a[1], b[0], dims))


def sigmoid(v):
    return 1.0 / (1.0 + jnp.exp(-v))


def windows(pick, table, taps):
    product = jnp.concatenate([taps[k : k + 1, :] * table for k in range(CONV)], axis=0)
    p1 = product.astype(bf16)
    rest = product - p1.astype(f32)
    p2 = rest.astype(bf16)
    p3 = (rest - p2.astype(f32)).astype(bf16)
    return mm(pick, jnp.concatenate([p1, p2, p3, jnp.zeros_like(p1)], axis=0))


def tables_kernel(
    emb_ref,
    gain_ref,
    wt_ref,
    cv_ref,
    cs_ref,
    wv_ref,
    wg_ref,
    ws_ref,
    tv_ref,
    tz_ref,
    tbc_ref,
    dt_ref,
    x_ref,
    x2_ref,
    bc_ref,
    slope_ref,
    held_v,
    held_g,
    held_s,
    sems,
):
    chunks = held_v.shape[0]
    size = held_v.shape[2]
    copies = [pltpu.make_async_copy(ws_ref, held_s, sems.at[0])]
    for i in range(chunks):
        columns = pl.ds(i * size, size)
        copies.append(pltpu.make_async_copy(wv_ref.at[:, columns], held_v.at[i], sems.at[1 + i]))
    for i in range(chunks):
        columns = pl.ds(i * size, size)
        copies.append(pltpu.make_async_copy(wg_ref.at[:, columns], held_g.at[i], sems.at[1 + chunks + i]))
    for copy in copies:
        copy.start()
    embedded = emb_ref[...].astype(f32)
    mean = jnp.mean(embedded * embedded, axis=1, keepdims=True)
    normed = (embedded * lax.rsqrt(mean + EPSILON) * gain_ref[...]).astype(bf16)
    dt_ref[...] = mm(wt_ref[...], normed, NT)
    lane = iota((WINDOWS, 128), 1)
    digit = (iota((WINDOWS, 128), 0) >> (2 * ((lane >> 3) & 3))) & 3
    pick = ((digit == (lane & 7)) & (lane < 96)).astype(f32).astype(bf16)

    def rows(weights):
        product = mm(normed, weights)
        return jnp.concatenate([product, jnp.zeros((8 - IDS, product.shape[1]), f32)], axis=0)

    copies[0].wait()
    table = rows(held_s[...])
    tbc_ref[...] = table
    summed = windows(pick, table, cs_ref[...])
    sig = sigmoid(summed)
    bc_ref[...] = summed * sig
    slope_ref[...] = sig * (1.0 + summed * (1.0 - sig))
    for i in range(chunks):
        copies[1 + i].wait()
        columns = slice(i * size, (i + 1) * size)
        table = rows(held_v[i])
        tv_ref[:, columns] = table
        summed = windows(pick, table, cv_ref[:, columns])
        x = summed * sigmoid(summed)
        x_ref[:, columns] = x
        high, low = split(x)
        for h in range(size // HEAD):
            at = (i * (size // HEAD) + h) * 2 * HEAD
            own = slice(h * HEAD, (h + 1) * HEAD)
            x2_ref[:, at : at + HEAD] = high[:, own]
            x2_ref[:, at + HEAD : at + 2 * HEAD] = low[:, own]
    for i in range(chunks):
        copies[1 + chunks + i].wait()
        table = rows(held_g[i])
        tz_ref[:, i * size : (i + 1) * size] = table * sigmoid(table)


def tables(embedding, norm_gain, w_values, w_gates, w_states, w_steps, conv_values, conv_states):
    depth, width = w_values.shape
    heads = w_steps.shape[1]
    size = 256
    chunks = width // size
    vmem = pl.BlockSpec(memory_space=pltpu.VMEM)
    hbm = pl.BlockSpec(memory_space=pl.ANY)
    shapes = [
        ((8, width), f32),
        ((8, width), f32),
        ((8, 2 * STATE), f32),
        ((heads, IDS), f32),
        ((WINDOWS, width), f32),
        ((WINDOWS, 2 * width), bf16),
        ((WINDOWS, 2 * STATE), f32),
        ((WINDOWS, 2 * STATE), f32),
    ]
    return pl.pallas_call(
        tables_kernel,
        in_specs=[vmem] * 5 + [hbm] * 3,
        out_specs=[vmem] * len(shapes),
        out_shape=[jax.ShapeDtypeStruct(shape, kind) for shape, kind in shapes],
        scratch_shapes=[
            pltpu.VMEM((chunks, depth, size), bf16),
            pltpu.VMEM((chunks, depth, size), bf16),
            pltpu.VMEM((depth, 2 * STATE), bf16),
            pltpu.SemaphoreType.DMA((1 + 2 * chunks,)),
        ],
        compiler_params=pltpu.CompilerParams(vmem_limit_bytes=56 * 2**20),
        name="tables",
    )(embedding, norm_gain.reshape(1, depth), w_steps.T, conv_values, conv_states, w_values, w_gates, w_states)


def mixer_kernel(
    scale,
    tok_ref,
    rc_ref,
    place_ref,
    skip_ref,
    tv_ref,
    tbc_ref,
    tz_ref,
    dt_ref,
    xw_ref,
    x2w_ref,
    bc_ref,
    slope_ref,
    cv_ref,
    cs_ref,
    bias_ref,
    rate_ref,
    gain_ref,
    cot_ref,
    enc_ref,
    grad_ref,
    tok_s,
    ids_s,
    count_s,
    onehot_s,
    weight_s,
    edge_s,
    wh_s,
    wl_s,
    x_s,
    x2_s,
    far_s,
    dh_s,
    dl_s,
    row_s,
    lcol_s,
    acol_s,
    tcol_s,
    gate_s,
    score_s,
    q_s,
    acc_s,
):
    devices, count = tok_ref.shape
    width = tv_ref.shape[1]
    heads = width // HEAD
    here = place_ref[0]
    tp_place = place_ref[1]

    for r in range(devices):
        tok_s[pl.ds(jnp.bitwise_xor(here, r), 1), :] = tok_ref[r : r + 1, :]
    tok = tok_s[...]
    rc = [rc_ref[t] for t in range(IDS)]
    rtok = jnp.zeros_like(tok)
    for t in range(IDS):
        rtok = jnp.where(tok == t, rc[t], rtok)
    lane = iota((devices, count), 1)
    row = iota((devices, count), 0)

    def before(ids, shift):
        turned = pltpu.roll(ids, shift, 1)
        return jnp.where(lane < shift, pltpu.roll(turned, 1, 0), turned)

    def after(ids, shift):
        turned = pltpu.roll(ids, count - shift, 1)
        return jnp.where(lane >= count - shift, pltpu.roll(turned, devices - 1, 0), turned)

    kf = before(tok, 3) + IDS * before(tok, 2) + IDS**2 * before(tok, 1) + IDS**3 * tok
    kr = after(rtok, 3) + IDS * after(rtok, 2) + IDS**2 * after(rtok, 1) + IDS**3 * rtok
    first = row * count + lane
    last = devices * count - 1 - first
    kf = jnp.where(first < CONV - 1, WINDOWS + first, kf)
    kr = jnp.where(last < CONV - 1, WINDOWS + CONV - 1 + last, kr)
    ids_s[0] = kf
    ids_s[1] = kr

    eye = iota((heads, heads), 0) == iota((heads, heads), 1)
    column = lambda ref: jnp.sum(jnp.where(eye, ref[...], 0.0), axis=1, keepdims=True)
    raw = dt_ref[...] + column(bias_ref)
    rate = jnp.exp(column(rate_ref))
    step = jnp.maximum(raw, 0.0) + jnp.log1p(jnp.exp(-jnp.abs(raw)))
    slope = sigmoid(raw)
    ratio = jnp.where(step > 1e-37, slope / jnp.maximum(step, 1e-37), 1.0)

    def per_strand(table):
        own = [table[:, t : t + 1] for t in range(IDS)]
        mapped = []
        for t in range(IDS):
            picked = own[0]
            for other in range(1, IDS):
                picked = jnp.where(rc[t] == other, own[other], picked)
            mapped.append(picked)
        return own, mapped

    step_of, slope_of, ratio_of = per_strand(step), per_strand(slope), per_strand(ratio)
    log_of, alog_of = per_strand(-rate * step), per_strand(-rate * slope)

    masks = [(tok == t).astype(f32) for t in range(IDS)]
    upper = (iota((count, count), 0) <= iota((count, count), 1)).astype(bf16)
    for t in range(IDS):
        count_s[t] = mm(masks[t].astype(bf16), upper)
    totals = [jnp.sum(m, axis=1, keepdims=True) for m in masks]
    row1 = iota((devices, 1), 0)
    far_counts = []
    for t in range(IDS):
        between = jnp.zeros((devices, 1), f32)
        for j in range(devices):
            inside = ((row1 < j) & (j < here)) | ((row1 > j) & (j > here))
            between = between + jnp.where(inside, totals[t][j : j + 1, :], 0.0)
        inclusive = count_s[t]
        far_counts.append(
            jnp.where(row < here, totals[t] - inclusive, inclusive - masks[t]) + between
        )

    window_rows = iota((ROWS, count), 0)
    for j in range(devices):
        forward = j < here
        reverse = j > here
        choose = lambda pair, t: jnp.where(forward, pair[0][t], pair[1][t])
        tok_j = tok[j : j + 1, :]
        log_sum = jnp.zeros((heads, count), f32)
        alog_sum = jnp.zeros((heads, count), f32)
        step_j = jnp.zeros((heads, count), f32)
        slope_j = jnp.zeros((heads, count), f32)
        for t in range(IDS):
            number = far_counts[t][j : j + 1, :]
            log_sum = log_sum + choose(log_of, t) * number
            alog_sum = alog_sum + choose(alog_of, t) * number
            step_j = jnp.where(tok_j == t, choose(step_of, t), step_j)
            slope_j = jnp.where(tok_j == t, choose(slope_of, t), slope_j)
        decay = jnp.exp(log_sum)
        weight = decay * step_j
        terms = jnp.concatenate([weight, weight * log_sum, decay * (slope_j + step_j * alog_sum)], axis=0)
        both = jnp.concatenate(
            [
                jnp.where(forward, terms, 0.0),
                jnp.where(reverse, terms, 0.0),
                jnp.zeros((64 - 6 * heads, count), f32),
            ],
            axis=0,
        )
        high, low = split(both)
        weight_s[0:64, j * count : (j + 1) * count] = high
        weight_s[64:128, j * count : (j + 1) * count] = low
        window_j = jnp.where(forward, kf[j : j + 1, :], kr[j : j + 1, :])
        onehot_s[:, j * count : (j + 1) * count] = (window_rows == window_j).astype(bf16)
    weights = mm(onehot_s[...], weight_s[...], NT)
    weights = weights + pltpu.roll(weights, 64, 1)

    lane_e = iota((16, 128), 1)
    row_e = iota((16, 128), 0)
    tap_e = (lane_e >> 3) & 3
    edge = jnp.full((16, 128), IDS, jnp.int32)
    for u in range(CONV - 1):
        for k in range(CONV - 1 - u, CONV):
            at = u - (CONV - 1) + k
            edge = jnp.where((row_e == u) & (tap_e == k), tok[0:1, at : at + 1], edge)
            edge = jnp.where(
                (row_e == CONV - 1 + u) & (tap_e == k),
                rtok[devices - 1 : devices, count - 1 - at : count - at],
                edge,
            )
    edge_pick = ((edge == (lane_e & 7)) & (lane_e < 96)).astype(f32).astype(bf16)
    summed = windows(edge_pick, tv_ref[...], cv_ref[...])
    edge_x = summed * sigmoid(summed)
    edge_s[...] = edge_x
    edge_high, edge_low = split(edge_x)
    edge_x2 = []
    for h in range(heads):
        edge_x2 += [edge_high[:, h * HEAD : (h + 1) * HEAD], edge_low[:, h * HEAD : (h + 1) * HEAD]]
    edge_x2 = jnp.concatenate(edge_x2, axis=1)
    table_bc = tbc_ref[...]
    summed = windows(edge_pick, table_bc, cs_ref[...])
    sig = sigmoid(summed)
    bc_all = jnp.concatenate([bc_ref[...], summed * sig], axis=0)
    bc_slope = jnp.concatenate([slope_ref[...], sig * (1.0 + summed * (1.0 - sig))], axis=0)
    bc = split(bc_all)
    b_all = (bc[0][:, :STATE], bc[1][:, :STATE])

    own_tok = tok_s[pl.ds(here, 1), :]
    own_masks = [(own_tok == t).astype(f32) for t in range(IDS)]
    own_counts = [[], []]
    for t in range(IDS):
        inclusive = count_s[t, pl.ds(here, 1), :]
        total = jnp.sum(own_masks[t], axis=1, keepdims=True)
        own_counts[0].append(inclusive)
        own_counts[1].append(total - inclusive + own_masks[t])
    turned = []
    for s in range(2):
        logs = sum(log_of[s][t] * own_counts[s][t] for t in range(IDS))
        alogs = sum(alog_of[s][t] * own_counts[s][t] for t in range(IDS))
        row_s[s, 0] = logs
        row_s[s, 1] = sum(step_of[s][t] * own_masks[t] for t in range(IDS))
        row_s[s, 2] = sum(ratio_of[s][t] * own_masks[t] for t in range(IDS)) - alogs
        turned += [logs, alogs]
    own_ids = [ids_s[s, pl.ds(here, 1), :] for s in range(2)]
    extra = jnp.concatenate(
        [own_ids[0].astype(f32), own_ids[1].astype(f32), own_tok.astype(f32), jnp.zeros((5, count), f32)],
        axis=0,
    )
    turned = jnp.concatenate(turned + [extra, jnp.zeros((120 - 4 * heads, count), f32)], axis=0).T
    for s in range(2):
        for h in range(heads):
            at = 2 * s * heads + h
            lcol_s[s, h] = jnp.broadcast_to(turned[:, at : at + 1], (count, 128))
            acol_s[s, h] = jnp.broadcast_to(turned[:, at + heads : at + heads + 1], (count, 128))
    base = 4 * heads
    tcol_s[...] = jnp.broadcast_to(turned[:, base + 2 : base + 3], (count, 128))
    gates = tz_ref[...]
    gate_s[0] = gates
    for t in range(IDS):
        picked = gates[0:1, :]
        for other in range(1, IDS):
            picked = jnp.where(rc[t] == other, gates[other : other + 1, :], picked)
        gate_s[1, t : t + 1, :] = picked

    own_onehot = []
    own_bc = []
    states = []
    lane_k = iota((count, ROWS), 1).astype(f32)
    for s in range(2):
        picks = (lane_k == turned[:, base + s : base + s + 1]).astype(f32).astype(bf16)
        own_onehot.append((window_rows == own_ids[s]).astype(f32).astype(bf16))
        ends = slice(0, 16) if s == 0 else slice(count - 16, count)
        pieces = []
        for table, extra in ((x2w_ref[...], edge_x2), (bc[0][:WINDOWS], bc[0][WINDOWS:]), (bc[1][:WINDOWS], bc[1][WINDOWS:])):
            got = mm(picks[:, :WINDOWS], table)
            more = mm(picks[ends, WINDOWS:], extra)
            if s == 0:
                got = jnp.concatenate([got[:16] + more, got[16:]], axis=0)
            else:
                got = jnp.concatenate([got[: count - 16], got[count - 16 :] + more], axis=0)
            pieces.append(got)
        x2_s[s] = pieces[0].astype(bf16)
        for h in range(heads):
            at = 2 * h * HEAD
            x_s[s, :, h * HEAD : (h + 1) * HEAD] = pieces[0][:, at : at + HEAD] + pieces[0][:, at + HEAD : at + 2 * HEAD]
        own_bc.append((pieces[1].astype(bf16), pieces[2].astype(bf16)))
        own_b = tuple(part[:, :STATE] for part in own_bc[s])
        own_c = tuple(part[:, STATE:] for part in own_bc[s])
        twice_c = jnp.concatenate([own_c[0], own_c[0]], axis=1)
        score_s[s] = mm(twice_c, jnp.concatenate(own_b, axis=1), NT) + mm(own_c[1], own_b[0], NT)
        for h in range(heads):
            at = 3 * s * heads + h
            columns = slice(h * HEAD, (h + 1) * HEAD)
            weighted = split(xw_ref[:, columns] * weights[:WINDOWS, at : at + 1])
            wh_s[s, :WINDOWS, columns], wl_s[s, :WINDOWS, columns] = weighted
            weighted = split(edge_s[:, columns] * weights[WINDOWS:, at : at + 1])
            wh_s[s, WINDOWS:, columns], wl_s[s, WINDOWS:, columns] = weighted
        regular, edges = slice(0, WINDOWS), slice(WINDOWS, ROWS)
        state = mm3(tuple(part[regular] for part in b_all), (wh_s[s, regular], wl_s[s, regular]), TN)
        state = state + mm(
            jnp.concatenate([b_all[0][edges], b_all[0][edges], b_all[1][edges]], axis=0),
            jnp.concatenate([wh_s[s, edges], wl_s[s, edges], wh_s[s, edges]], axis=0),
            TN,
        )
        states.append(jnp.concatenate(split(state), axis=0))
        far_s[s] = mm(twice_c, states[s]) + mm(own_c[1], states[s][:STATE])

    q_s[...] = jnp.zeros_like(q_s)
    tiles = count // 128
    triangle = [iota((128, 128), 0) >= iota((128, 128), 1), iota((128, 128), 0) <= iota((128, 128), 1)]

    def one_head(h, _):
        columns = pl.ds(pl.multiple_of(h * HEAD, HEAD), HEAD)
        columns2 = pl.ds(pl.multiple_of(h * 2 * HEAD, 2 * HEAD), 2 * HEAD)
        gain = gain_ref[:, columns]
        skip = skip_ref[h]
        outs = [None] * tiles
        rate_row = jnp.zeros((1, 128), f32)
        bias_row = jnp.zeros((1, 128), f32)
        for s in range(2):
            column_sums = [jnp.zeros((1, 128), f32) for _ in range(tiles)]
            part = lambda j: slice(j * 128, (j + 1) * 128)
            log_row = row_s[s, 0, pl.ds(h, 1), :]
            step_row = row_s[s, 1, pl.ds(h, 1), :]
            mixed_row = row_s[s, 2, pl.ds(h, 1), :]
            for i in range(tiles):
                near = range(0, i + 1) if s == 0 else range(i, tiles)
                span = slice(near[0] * 128, (near[-1] + 1) * 128)
                lcol = lcol_s[s, h, part(i), :]
                factors = []
                for j in near:
                    gap = lcol - log_row[:, part(j)]
                    if j == i:
                        gap = jnp.where(triangle[s], gap, -1e30)
                    factors.append(jnp.exp(gap) * step_row[:, part(j)])
                factor = jnp.concatenate(factors, axis=1)
                high, low = split(score_s[s, part(i), span] * factor)
                x2 = x2_s[s, span, columns2]
                y = mm(high, x2)
                y = y[:, :HEAD] + (y[:, HEAD:] + mm(low, x2[:, :HEAD]))
                grown = jnp.exp(lcol)
                y = y + grown * far_s[s, part(i), columns]
                tcol = tcol_s[part(i), :]
                gate = gate_s[s, 0:1, columns]
                for t in range(1, IDS):
                    gate = jnp.where(tcol == t, gate_s[s, t : t + 1, columns], gate)
                gated = (y + skip * x_s[s, part(i), columns]) * gate
                inverse = lax.rsqrt(jnp.mean(gated * gated, axis=1, keepdims=True) + EPSILON)
                normal = gated * inverse
                outs[i] = normal if outs[i] is None else outs[i] + normal
                cot = cot_ref[part(i), columns].astype(f32) * gain
                shared = jnp.mean(cot * normal, axis=1, keepdims=True)
                dy = (cot - normal * shared) * (inverse * gate)
                high, low = split(dy)
                e = mm(jnp.concatenate([high, high], axis=1), x2, NT) + mm(low, x2[:, :HEAD], NT)
                e = e * factor
                q_s[s, part(i), span] += e
                e = e * score_s[s, part(i), span]
                for n, j in enumerate(near):
                    column_sums[j] = column_sums[j] + jnp.sum(e[:, part(n)], axis=0, keepdims=True)
                row_terms = dy * y
                rate_row += jnp.sum(lcol * row_terms, axis=0, keepdims=True)
                bias_row += jnp.sum(acol_s[s, h, part(i), :] * row_terms, axis=0, keepdims=True)
                dh_s[s, part(i), columns], dl_s[s, part(i), columns] = split(grown * dy)
            for j in range(tiles):
                rate_row -= log_row[:, part(j)] * column_sums[j]
                bias_row += mixed_row[:, part(j)] * column_sums[j]
        for i in range(tiles):
            enc_ref[i * 128 : (i + 1) * 128, columns] = (outs[i] * gain).astype(enc_ref.dtype)
        acc_s[0, pl.ds(h, 1), :] = rate_row
        acc_s[1, pl.ds(h, 1), :] = bias_row
        return 0

    lax.fori_loop(0, heads, one_head, 0)

    db_all = jnp.zeros((ROWS, STATE), f32)
    dc_all = jnp.zeros((ROWS, STATE), f32)
    twice_b = jnp.concatenate([b_all[0], b_all[0]], axis=1)
    for s in range(2):
        own_b = tuple(part[:, :STATE] for part in own_bc[s])
        own_c = tuple(part[:, STATE:] for part in own_bc[s])
        q = split(q_s[s])
        grown = (dh_s[s], dl_s[s])
        far = mm(grown[0], states[s], NT)
        far = far[:, :STATE] + (far[:, STATE:] + mm(grown[1], states[s][:STATE], NT))
        dc_own = split(mm3(q, own_b) + far)
        db_own = split(mm3(q, own_c, TN))
        back = jnp.concatenate(split(mm3(own_c, grown, TN)), axis=0)
        dc_all = dc_all + (mm(own_onehot[s], dc_own[0]) + mm(own_onehot[s], dc_own[1]))
        db_all = db_all + (mm(own_onehot[s], db_own[0]) + mm(own_onehot[s], db_own[1]))
        far = mm(wh_s[s], back, NT)
        db_all = db_all + (far[:, :STATE] + (far[:, STATE:] + mm(wl_s[s], back[:STATE], NT)))
        reach = mm(twice_b, back) + mm(b_all[1], back[:STATE])
        for h in range(heads):
            at = 3 * s * heads + heads + h
            columns = slice(h * HEAD, (h + 1) * HEAD)
            x = jnp.concatenate([xw_ref[:, columns], edge_s[:, columns]], axis=0)
            terms = reach[:, columns] * x
            acc_s[0, h : h + 1, :] += jnp.sum(terms * weights[:, at : at + 1], axis=0, keepdims=True)
            acc_s[1, h : h + 1, :] += jnp.sum(
                terms * weights[:, at + heads : at + heads + 1], axis=0, keepdims=True
            )
    d_summed = split(jnp.concatenate([db_all, dc_all], axis=1) * bc_slope)
    lane_w = iota((WINDOWS, 128), 1)
    digit = (iota((WINDOWS, 128), 0) >> (2 * ((lane_w >> 3) & 3))) & 3
    pick = ((digit == (lane_w & 7)) & (lane_w < 32)).astype(f32).astype(bf16)
    pick = jnp.concatenate([pick, edge_pick], axis=0)
    by_tap = mm(pick, d_summed[0], TN) + mm(pick, d_summed[1], TN)
    grad_ref[...] = jnp.zeros_like(grad_ref)
    for k in range(CONV):
        grad_ref[k : k + 1, :] = scale * jnp.sum(by_tap[8 * k : 8 * k + 8, :] * table_bc, axis=0, keepdims=True)
    place = iota((heads, 128), 1) == iota((heads, 128), 0) + tp_place * heads
    for i in range(2):
        sums = scale * jnp.sum(acc_s[i], axis=1, keepdims=True)
        grad_ref[CONV + i : CONV + i + 1, 0:128] = jnp.sum(jnp.where(place, sums, 0.0), axis=0, keepdims=True)


def mixer(tokens, rc_map, place, skip, tabs, conv_values, conv_states, bias, rate, gain, cotangent, scale):
    devices, count = tokens.shape
    width = conv_values.shape[1]
    heads = width // HEAD
    tv, tz, tbc, dt, x, x2, bc, slope = tabs
    vmem = pl.BlockSpec(memory_space=pltpu.VMEM)
    smem = pl.BlockSpec(memory_space=pltpu.SMEM)
    scratch = [
        ((devices, count), jnp.int32),
        ((2, devices, count), jnp.int32),
        ((IDS, devices, count), f32),
        ((ROWS, devices * count), bf16),
        ((128, devices * count), bf16),
        ((16, width), f32),
        ((2, ROWS, width), bf16),
        ((2, ROWS, width), bf16),
        ((2, count, width), f32),
        ((2, count, 2 * width), bf16),
        ((2, count, width), f32),
        ((2, count, width), bf16),
        ((2, count, width), bf16),
        ((2, 3, heads, count), f32),
        ((2, heads, count, 128), f32),
        ((2, heads, count, 128), f32),
        ((count, 128), f32),
        ((2, 8, width), f32),
        ((2, count, count), f32),
        ((2, count, count), f32),
        ((2, heads, 128), f32),
    ]
    return pl.pallas_call(
        functools.partial(mixer_kernel, scale),
        in_specs=[vmem, smem, smem, smem] + [vmem] * 14,
        out_specs=[vmem, vmem],
        out_shape=[
            jax.ShapeDtypeStruct((count, width), bf16),
            jax.ShapeDtypeStruct((8, 2 * STATE), f32),
        ],
        scratch_shapes=[pltpu.VMEM(shape, kind) for shape, kind in scratch],
        compiler_params=pltpu.CompilerParams(vmem_limit_bytes=52 * 2**20),
        name="mixer",
    )(
        tokens,
        rc_map,
        place,
        skip,
        tv,
        tbc,
        tz,
        dt,
        x,
        x2,
        bc,
        slope,
        conv_values,
        conv_states,
        bias.reshape(1, heads),
        rate.reshape(1, heads),
        gain.reshape(1, width),
        cotangent,
    )


def exchange(value, axis, distance):
    size = lax.axis_size(axis)
    return lax.ppermute(value, axis, [(i, i ^ distance) for i in range(size)])


def on_device(
    tokens,
    rc_map,
    embedding,
    norm_gain,
    w_values,
    w_gates,
    w_states,
    w_steps,
    conv_values,
    conv_states,
    step_bias,
    log_rate,
    skip_gain,
    head_gain,
    cotangent,
):
    devices = lax.axis_size("ctx")
    count = tokens.shape[0]
    everyone = jnp.minimum(tokens, IDS - 1).reshape(1, count)
    distance = 1
    while distance < devices:
        everyone = jnp.concatenate([everyone, exchange(everyone, "ctx", distance)], axis=0)
        distance *= 2
    tabs = tables(embedding, norm_gain, w_values, w_gates, w_states, w_steps, conv_values, conv_states)
    place = jnp.stack([lax.axis_index("ctx"), lax.axis_index("tp")]).astype(jnp.int32)
    scale = 1.0 / math.sqrt(count * devices * HEAD)
    encoded, grads = mixer(
        everyone,
        rc_map,
        place,
        skip_gain,
        tabs,
        conv_values,
        conv_states,
        step_bias,
        log_rate,
        head_gain,
        cotangent,
        scale,
    )
    for axis in ("tp", "ctx"):
        distance = 1
        while distance < lax.axis_size(axis):
            grads = grads + exchange(grads, axis, distance)
            distance *= 2
    head_total = log_rate.shape[0] * lax.axis_size("tp")
    return (encoded, grads[CONV, :head_total], grads[CONV + 1, :head_total], grads[:CONV])


def solution(mesh):
    placed = (
        P("ctx"),
        P(),
        P(),
        P(),
        P(None, "tp"),
        P(None, "tp"),
        P(),
        P(None, "tp"),
        P(None, "tp"),
        P(),
        P("tp"),
        P("tp"),
        P("tp"),
        P("tp"),
        P("ctx", "tp"),
    )
    return jax.shard_map(
        on_device,
        mesh=mesh,
        in_specs=placed,
        out_specs=(P("ctx", "tp"), P(), P(), P()),
        check_vma=False,
    )
```

```python
import functools
import math

import jax
import jax.numpy as jnp
from jax import lax
from jax.experimental import pallas as pl
from jax.experimental.pallas import tpu as pltpu
from jax.sharding import PartitionSpec as P

HEAD = 128
STATE = 128
CONV = 4
IDS = 4
WINDOWS = IDS**CONV
ROWS = WINDOWS + 16
UNROLL = 2
EPSILON = 1e-05

f32 = jnp.float32
bf16 = jnp.bfloat16
NN = (((1,), (0,)), ((), ()))
NT = (((1,), (1,)), ((), ()))
TN = (((0,), (0,)), ((), ()))


def iota(shape, dim):
    return lax.broadcasted_iota(jnp.int32, shape, dim)


def mm(a, b, dims=NN):
    return lax.dot_general(a, b, dims, preferred_element_type=f32)


def split(x):
    high = x.astype(bf16)
    return high, (x - high.astype(f32)).astype(bf16)


def mm3(a, b, dims=NN):
    return mm(a[0], b[0], dims) + (mm(a[0], b[1], dims) + mm(a[1], b[0], dims))


def rows_of(parts):
    return jnp.concatenate(parts, axis=0)


def lanes_of(parts):
    return jnp.concatenate(parts, axis=1)


def stacked(a, b2, dims=NN):
    count = a[0].shape[0]
    both = mm(rows_of([lanes_of([a[0], a[0]]), lanes_of([a[1], a[1]])]), b2, dims)
    return both[:count] + both[count:]


def stacked_out(a, b2, width, dims=NN):
    count = a[0].shape[0]
    both = mm(rows_of([a[0], a[1]]), b2, dims)
    both = both[:count] + both[count:]
    return both[:, :width] + both[:, width:]


def sigmoid(v):
    return 1.0 / (1.0 + jnp.exp(-v))


def tap_parts(table, taps):
    product = rows_of([taps[k : k + 1, :] * table for k in range(CONV)])
    p1 = product.astype(bf16)
    rest = product - p1.astype(f32)
    p2 = rest.astype(bf16)
    p3 = (rest - p2.astype(f32)).astype(bf16)
    return rows_of([p1, p2, p3, jnp.zeros_like(p1)])


def mixer_kernel(
    scale,
    near_ref,
    far_ref,
    rc_ref,
    skip_ref,
    emb_ref,
    norm_gain_ref,
    wt_ref,
    cv_ref,
    cs_ref,
    bias_ref,
    rate_ref,
    gain_ref,
    wv_hbm,
    wg_hbm,
    ws_hbm,
    cot_hbm,
    enc_hbm,
    grad_ref,
    held_v,
    held_g,
    held_s,
    sems,
    enc_ref,
    enc_sem,
    tok_s,
    ids_s,
    count_s,
    onehot_s,
    weight_s,
    cot_s,
    cot_sem,
    xw_s,
    x2w_s,
    edge_s,
    wh_s,
    wl_s,
    x_s,
    x2_s,
    far_s,
    dh_s,
    dl_s,
    row_s,
    lcol_s,
    acol_s,
    tcol_s,
    gate_s,
    score_s,
    q_s,
    acc_s,
):
    devices, count = tok_s.shape
    width = cv_ref.shape[1]
    heads = width // HEAD
    here = lax.axis_index("ctx")
    tp_place = lax.axis_index("tp")
    chunks, size, _ = held_v.shape
    rows_at = lambda i: pl.ds(i * size, size)
    copies = [pltpu.make_async_copy(ws_hbm, held_s, sems.at[0])]
    for i in range(chunks):
        copies.append(pltpu.make_async_copy(wv_hbm.at[rows_at(i), :], held_v.at[i], sems.at[1 + i]))
    for i in range(chunks):
        copies.append(pltpu.make_async_copy(wg_hbm.at[rows_at(i), :], held_g.at[i], sems.at[1 + chunks + i]))
    for copy in copies:
        copy.start()

    cot_copy = pltpu.make_async_copy(cot_hbm, cot_s, cot_sem)
    cot_copy.start()

    half = near_ref.shape[0]
    for r in range(devices):
        own = near_ref[r : r + 1, :] if r < half else far_ref[r - half : r - half + 1, :]
        tok_s[pl.ds(jnp.bitwise_xor(here, r), 1), :] = own
    tok = tok_s[...]
    rc = [rc_ref[t] for t in range(IDS)]
    rtok = jnp.zeros_like(tok)
    for t in range(IDS):
        rtok = jnp.where(tok == t, rc[t], rtok)
    lane = iota((devices, count), 1)
    row = iota((devices, count), 0)

    def before(ids, shift):
        turned = pltpu.roll(ids, shift, 1)
        return jnp.where(lane < shift, pltpu.roll(turned, 1, 0), turned)

    def after(ids, shift):
        turned = pltpu.roll(ids, count - shift, 1)
        return jnp.where(lane >= count - shift, pltpu.roll(turned, devices - 1, 0), turned)

    kf = before(tok, 3) + IDS * before(tok, 2) + IDS**2 * before(tok, 1) + IDS**3 * tok
    kr = after(rtok, 3) + IDS * after(rtok, 2) + IDS**2 * after(rtok, 1) + IDS**3 * rtok
    first = row * count + lane
    last = devices * count - 1 - first
    kf = jnp.where(first < CONV - 1, WINDOWS + first, kf)
    kr = jnp.where(last < CONV - 1, WINDOWS + CONV - 1 + last, kr)
    ids_s[0] = kf
    ids_s[1] = kr

    embedded = emb_ref[...].astype(f32)
    mean = jnp.mean(embedded * embedded, axis=1, keepdims=True)
    normed = (embedded * lax.rsqrt(mean + EPSILON) * norm_gain_ref[...]).astype(bf16)
    eye = iota((heads, heads), 0) == iota((heads, heads), 1)
    column = lambda ref: jnp.sum(jnp.where(eye, ref[...], 0.0), axis=1, keepdims=True)
    raw = mm(wt_ref[...], normed, NT) + column(bias_ref)
    rate = jnp.exp(column(rate_ref))
    step = jnp.maximum(raw, 0.0) + jnp.log1p(jnp.exp(-jnp.abs(raw)))
    slope = sigmoid(raw)
    ratio = jnp.where(step > 1e-37, slope / jnp.maximum(step, 1e-37), 1.0)

    def per_strand(table):
        own = [table[:, t : t + 1] for t in range(IDS)]
        mapped = []
        for t in range(IDS):
            picked = own[0]
            for other in range(1, IDS):
                picked = jnp.where(rc[t] == other, own[other], picked)
            mapped.append(picked)
        return own, mapped

    step_of, slope_of, ratio_of = per_strand(step), per_strand(slope), per_strand(ratio)
    log_of, alog_of = per_strand(-rate * step), per_strand(-rate * slope)

    masks = [(tok == t).astype(f32) for t in range(IDS)]
    upper = (iota((count, count), 0) <= iota((count, count), 1)).astype(bf16)
    for t in range(IDS):
        count_s[t] = mm(masks[t].astype(bf16), upper)
    totals = [jnp.sum(m, axis=1, keepdims=True) for m in masks]
    row1 = iota((devices, 1), 0)
    far_counts = []
    for t in range(IDS):
        between = jnp.zeros((devices, 1), f32)
        for j in range(devices):
            inside = ((row1 < j) & (j < here)) | ((row1 > j) & (j > here))
            between = between + jnp.where(inside, totals[t][j : j + 1, :], 0.0)
        inclusive = count_s[t]
        far_counts.append(
            jnp.where(row < here, totals[t] - inclusive, inclusive - masks[t]) + between
        )

    window_rows = iota((ROWS, count), 0)
    def earlier(j):
        forward = j < here
        reverse = j > here
        choose = lambda pair, t: jnp.where(forward, pair[0][t], pair[1][t])
        tok_j = tok[j : j + 1, :]
        log_sum = jnp.zeros((heads, count), f32)
        alog_sum = jnp.zeros((heads, count), f32)
        step_j = jnp.zeros((heads, count), f32)
        slope_j = jnp.zeros((heads, count), f32)
        for t in range(IDS):
            number = far_counts[t][j : j + 1, :]
            log_sum = log_sum + choose(log_of, t) * number
            alog_sum = alog_sum + choose(alog_of, t) * number
            step_j = jnp.where(tok_j == t, choose(step_of, t), step_j)
            slope_j = jnp.where(tok_j == t, choose(slope_of, t), slope_j)
        decay = jnp.exp(log_sum)
        weight = decay * step_j
        terms = jnp.concatenate([weight, weight * log_sum, decay * (slope_j + step_j * alog_sum)], axis=0)
        both = jnp.concatenate(
            [
                jnp.where(forward, terms, 0.0),
                jnp.where(reverse, terms, 0.0),
                jnp.zeros((64 - 6 * heads, count), f32),
            ],
            axis=0,
        )
        high, low = split(both)
        weight_s[0:64, j * count : (j + 1) * count] = high
        weight_s[64:128, j * count : (j + 1) * count] = low
        window_j = jnp.where(forward, kf[j : j + 1, :], kr[j : j + 1, :])
        onehot_s[:, j * count : (j + 1) * count] = (window_rows == window_j).astype(bf16)

    blank = lambda size: jnp.zeros((8 - IDS, size), f32)
    copies[0].wait()
    product = mm(normed, held_s[...])
    table_bc = rows_of([product, blank(product.shape[1])])
    product = None
    for i in range(chunks):
        copies[1 + i].wait()
        term = mm(normed[:, i * size : (i + 1) * size], held_v[i])
        product = term if product is None else product + term
        for j in range(i * devices // chunks, (i + 1) * devices // chunks):
            earlier(j)
    taps_v = tap_parts(rows_of([product, blank(width)]), cv_ref[...])
    taps_s = tap_parts(table_bc, cs_ref[...])
    product = None
    for i in range(chunks):
        copies[1 + chunks + i].wait()
        term = mm(normed[:, i * size : (i + 1) * size], held_g[i])
        product = term if product is None else product + term
    gates = rows_of([product, blank(width)])
    gates = gates * sigmoid(gates)

    weights = mm(onehot_s[...], weight_s[...], NT)
    weights = weights + pltpu.roll(weights, 64, 1)

    lane_w = iota((WINDOWS, 128), 1)
    digit = (iota((WINDOWS, 128), 0) >> (2 * ((lane_w >> 3) & 3))) & 3
    pick = ((digit == (lane_w & 7)) & (lane_w < 96)).astype(f32).astype(bf16)
    for h in range(0, heads, 2):
        columns = slice(h * HEAD, (h + 2) * HEAD)
        summed = mm(pick, taps_v[:, columns])
        x = summed * sigmoid(summed)
        xw_s[:, columns] = x
        high, low = split(x)
        for i in range(2):
            at = 2 * (h + i) * HEAD
            own = slice(i * HEAD, (i + 1) * HEAD)
            x2w_s[:, at : at + HEAD] = high[:, own]
            x2w_s[:, at + HEAD : at + 2 * HEAD] = low[:, own]

    lane_e = iota((16, 128), 1)
    row_e = iota((16, 128), 0)
    tap_e = (lane_e >> 3) & 3
    edge = jnp.full((16, 128), IDS, jnp.int32)
    for u in range(CONV - 1):
        for k in range(CONV - 1 - u, CONV):
            at = u - (CONV - 1) + k
            edge = jnp.where((row_e == u) & (tap_e == k), tok[0:1, at : at + 1], edge)
            edge = jnp.where(
                (row_e == CONV - 1 + u) & (tap_e == k),
                rtok[devices - 1 : devices, count - 1 - at : count - at],
                edge,
            )
    edge_pick = ((edge == (lane_e & 7)) & (lane_e < 96)).astype(f32).astype(bf16)
    summed = mm(edge_pick, taps_v)
    edge_x = summed * sigmoid(summed)
    edge_s[...] = edge_x
    edge_high, edge_low = split(edge_x)
    edge_x2 = []
    for h in range(heads):
        edge_x2 += [edge_high[:, h * HEAD : (h + 1) * HEAD], edge_low[:, h * HEAD : (h + 1) * HEAD]]
    edge_x2 = jnp.concatenate(edge_x2, axis=1)
    pick = rows_of([pick, edge_pick])
    summed = mm(pick, taps_s)
    sig = sigmoid(summed)
    bc_all = summed * sig
    bc_slope = sig * (1.0 + summed * (1.0 - sig))
    bc = split(bc_all)
    b_all = (bc[0][:, :STATE], bc[1][:, :STATE])

    own_tok = tok_s[pl.ds(here, 1), :]
    own_masks = [(own_tok == t).astype(f32) for t in range(IDS)]
    own_counts = [[], []]
    for t in range(IDS):
        inclusive = count_s[t, pl.ds(here, 1), :]
        total = jnp.sum(own_masks[t], axis=1, keepdims=True)
        own_counts[0].append(inclusive)
        own_counts[1].append(total - inclusive + own_masks[t])
    turned = []
    for s in range(2):
        logs = sum(log_of[s][t] * own_counts[s][t] for t in range(IDS))
        alogs = sum(alog_of[s][t] * own_counts[s][t] for t in range(IDS))
        row_s[s, 0] = logs
        row_s[s, 1] = sum(step_of[s][t] * own_masks[t] for t in range(IDS))
        row_s[s, 2] = sum(ratio_of[s][t] * own_masks[t] for t in range(IDS)) - alogs
        turned += [logs, alogs]
    own_ids = [ids_s[s, pl.ds(here, 1), :] for s in range(2)]
    extra = jnp.concatenate(
        [own_ids[0].astype(f32), own_ids[1].astype(f32), own_tok.astype(f32), jnp.zeros((5, count), f32)],
        axis=0,
    )
    turned = jnp.concatenate(turned + [extra, jnp.zeros((120 - 4 * heads, count), f32)], axis=0).T
    for s in range(2):
        for h in range(heads):
            at = 2 * s * heads + h
            lcol_s[s, h] = jnp.broadcast_to(turned[:, at : at + 1], (count, 128))
            acol_s[s, h] = jnp.broadcast_to(turned[:, at + heads : at + heads + 1], (count, 128))
    base = 4 * heads
    tcol_s[...] = jnp.broadcast_to(turned[:, base + 2 : base + 3], (count, 128))
    gate_s[0] = gates
    for t in range(IDS):
        picked = gates[0:1, :]
        for other in range(1, IDS):
            picked = jnp.where(rc[t] == other, gates[other : other + 1, :], picked)
        gate_s[1, t : t + 1, :] = picked

    own_onehot = []
    lane_k = iota((count, ROWS), 1).astype(f32)
    picks = []
    for s in range(2):
        picks.append((lane_k == turned[:, base + s : base + s + 1]).astype(f32).astype(bf16))
        own_onehot.append((window_rows == own_ids[s]).astype(f32).astype(bf16))
    regular, edges = slice(0, WINDOWS), slice(WINDOWS, ROWS)
    both_picks = rows_of([picks[0][:, regular], picks[1][:, regular]])
    edge_picks = rows_of([picks[0][:16, edges], picks[1][count - 16 :, edges]])

    def gather(table, extra):
        got = mm(both_picks, table)
        more = mm(edge_picks, extra)
        return [
            rows_of([got[:16] + more[:16], got[16:count]]),
            rows_of([got[count : 2 * count - 16], got[2 * count - 16 :] + more[16:]]),
        ]

    for h in range(heads):
        columns = slice(2 * h * HEAD, 2 * (h + 1) * HEAD)
        for s, got in enumerate(gather(x2w_s[:, columns], edge_x2[:, columns])):
            x2_s[s, :, columns] = got.astype(bf16)
            x_s[s, :, h * HEAD : (h + 1) * HEAD] = got[:, :HEAD] + got[:, HEAD:]
    bc_high = gather(bc[0][regular], bc[0][edges])
    bc_low = gather(bc[1][regular], bc[1][edges])
    own_b, own_c, states = [], [], []
    for s in range(2):
        high, low = bc_high[s].astype(bf16), bc_low[s].astype(bf16)
        own_b.append((high[:, :STATE], low[:, :STATE]))
        own_c.append((high[:, STATE:], low[:, STATE:]))
        score_s[s] = stacked(own_c[s], lanes_of(own_b[s]), NT)
        for h in range(heads):
            at = 3 * s * heads + h
            columns = slice(h * HEAD, (h + 1) * HEAD)
            weighted = split(xw_s[:, columns] * weights[:WINDOWS, at : at + 1])
            wh_s[s, :WINDOWS, columns], wl_s[s, :WINDOWS, columns] = weighted
            weighted = split(edge_s[:, columns] * weights[WINDOWS:, at : at + 1])
            wh_s[s, WINDOWS:, columns], wl_s[s, WINDOWS:, columns] = weighted
        b2 = lanes_of([part[regular] for part in b_all])
        state = mm(b2, wh_s[s, regular], TN)
        state = state[:STATE] + state[STATE:] + mm(b2[:, :STATE], wl_s[s, regular], TN)
        state = state + mm(
            rows_of([b_all[0][edges], b_all[0][edges], b_all[1][edges]]),
            rows_of([wh_s[s, edges], wl_s[s, edges], wh_s[s, edges]]),
            TN,
        )
        states.append(rows_of(split(state)))
        far_s[s] = stacked(own_c[s], states[s])

    cot_copy.wait()
    q_s[...] = jnp.zeros_like(q_s)
    tiles = count // 128
    triangle = [iota((128, 128), 0) >= iota((128, 128), 1), iota((128, 128), 0) <= iota((128, 128), 1)]

    nothing = jnp.zeros((128, 128), bf16)
    part = lambda j: slice(j * 128, (j + 1) * 128)

    def one_head(h, _):
        columns = pl.ds(pl.multiple_of(h * HEAD, HEAD), HEAD)
        columns2 = pl.ds(pl.multiple_of(h * 2 * HEAD, 2 * HEAD), 2 * HEAD)
        gain = gain_ref[:, columns]
        skip = skip_ref[h]
        outs = [None] * tiles
        rate_row = jnp.zeros((1, 128), f32)
        bias_row = jnp.zeros((1, 128), f32)
        factors, ys = [], []
        for s in range(2):
            log_row = row_s[s, 0, pl.ds(h, 1), :]
            step_row = row_s[s, 1, pl.ds(h, 1), :]
            highs, lows, own = [], [], {}
            for i in range(tiles):
                lcol = lcol_s[s, h, part(i), :]
                high_row, low_row = [], []
                for j in range(tiles):
                    if (j > i) if s == 0 else (j < i):
                        high, low = nothing, nothing
                    else:
                        gap = lcol - log_row[:, part(j)]
                        if j == i:
                            gap = jnp.where(triangle[s], gap, -1e30)
                        own[i, j] = jnp.exp(gap) * step_row[:, part(j)]
                        high, low = split(score_s[s, part(i), part(j)] * own[i, j])
                    high_row.append(high)
                    low_row.append(low)
                highs.append(lanes_of(high_row))
                lows.append(lanes_of(low_row))
            factors.append(own)
            both = mm(rows_of(highs + lows), x2_s[s, :, columns2])
            both = both[:count] + both[count:]
            ys.append(both[:, :HEAD] + both[:, HEAD:])
        for s in range(2):
            column_sums = [jnp.zeros((1, 128), f32) for _ in range(tiles)]
            log_row = row_s[s, 0, pl.ds(h, 1), :]
            mixed_row = row_s[s, 2, pl.ds(h, 1), :]
            highs, lows = [], []
            for i in range(tiles):
                lcol = lcol_s[s, h, part(i), :]
                grown = jnp.exp(lcol)
                y = ys[s][part(i)] + grown * far_s[s, part(i), columns]
                tcol = tcol_s[part(i), :]
                gate = gate_s[s, 0:1, columns]
                for t in range(1, IDS):
                    gate = jnp.where(tcol == t, gate_s[s, t : t + 1, columns], gate)
                gated = (y + skip * x_s[s, part(i), columns]) * gate
                inverse = lax.rsqrt(jnp.mean(gated * gated, axis=1, keepdims=True) + EPSILON)
                normal = gated * inverse
                outs[i] = normal if outs[i] is None else outs[i] + normal
                cot = cot_s[part(i), columns].astype(f32) * gain
                shared = jnp.mean(cot * normal, axis=1, keepdims=True)
                dy = (cot - normal * shared) * (inverse * gate)
                high, low = split(dy)
                highs.append(lanes_of([high, high]))
                lows.append(lanes_of([low, low]))
                row_terms = dy * y
                rate_row += jnp.sum(lcol * row_terms, axis=0, keepdims=True)
                bias_row += jnp.sum(acol_s[s, h, part(i), :] * row_terms, axis=0, keepdims=True)
                dh_s[s, part(i), columns], dl_s[s, part(i), columns] = split(grown * dy)
            both = mm(rows_of(highs + lows), x2_s[s, :, columns2], NT)
            for i, j in factors[s]:
                e = both[part(i), part(j)] + both[part(tiles + i), part(j)]
                e = e * factors[s][i, j]
                q_s[s, part(i), part(j)] += e
                column_sums[j] = column_sums[j] + jnp.sum(e * score_s[s, part(i), part(j)], axis=0, keepdims=True)
            for j in range(tiles):
                rate_row -= log_row[:, part(j)] * column_sums[j]
                bias_row += mixed_row[:, part(j)] * column_sums[j]
        for i in range(tiles):
            enc_ref[i * 128 : (i + 1) * 128, columns] = (outs[i] * gain).astype(enc_ref.dtype)
        acc_s[0, pl.ds(h, 1), :] = rate_row
        acc_s[1, pl.ds(h, 1), :] = bias_row

    def some_heads(g, _):
        for i in range(UNROLL):
            one_head(g * UNROLL + i, 0)
        return 0

    lax.fori_loop(0, heads // UNROLL, some_heads, 0)

    enc_copy = pltpu.make_async_copy(enc_ref, enc_hbm, enc_sem)
    enc_copy.start()

    db_all = jnp.zeros((ROWS, STATE), f32)
    dc_all = jnp.zeros((ROWS, STATE), f32)
    for s in range(2):
        q = split(q_s[s])
        grown = (dh_s[s], dl_s[s])
        far = stacked_out(grown, states[s], STATE, NT)
        dc_own = split(stacked_out(q, lanes_of(own_b[s]), STATE) + far)
        db_own = split(mm3(q, own_c[s], TN))
        c2 = lanes_of(own_c[s])
        back = mm(c2, grown[0], TN)
        back = back[:STATE] + back[STATE:] + mm(own_c[s][0], grown[1], TN)
        back = rows_of(split(back))
        both = mm(own_onehot[s], lanes_of([db_own[0], dc_own[0]])) + mm(own_onehot[s], lanes_of([db_own[1], dc_own[1]]))
        dc_all = dc_all + both[:, STATE:]
        db_all = db_all + both[:, :STATE] + stacked_out((wh_s[s], wl_s[s]), back, STATE, NT)
        reach = stacked(b_all, back)
        for h in range(heads):
            at = 3 * s * heads + heads + h
            columns = slice(h * HEAD, (h + 1) * HEAD)
            x = rows_of([xw_s[:, columns], edge_s[:, columns]])
            terms = reach[:, columns] * x
            acc_s[0, h : h + 1, :] += jnp.sum(terms * weights[:, at : at + 1], axis=0, keepdims=True)
            acc_s[1, h : h + 1, :] += jnp.sum(
                terms * weights[:, at + heads : at + heads + 1], axis=0, keepdims=True
            )
    d_summed = split(jnp.concatenate([db_all, dc_all], axis=1) * bc_slope)
    by_tap = mm(pick, d_summed[0], TN) + mm(pick, d_summed[1], TN)
    grad_ref[...] = jnp.zeros_like(grad_ref)
    for k in range(CONV):
        grad_ref[k : k + 1, :] = scale * jnp.sum(by_tap[8 * k : 8 * k + 8, :] * table_bc, axis=0, keepdims=True)
    place = iota((heads, 128), 1) == iota((heads, 128), 0) + tp_place * heads
    for i in range(2):
        sums = scale * jnp.sum(acc_s[i], axis=1, keepdims=True)
        grad_ref[CONV + i : CONV + i + 1, 0:128] = jnp.sum(jnp.where(place, sums, 0.0), axis=0, keepdims=True)
    enc_copy.wait()


def mixer(near, far, rc_map, skip, small, large, scale):
    devices, count = near.shape[0] + far.shape[0], near.shape[1]
    depth, width = large[0].shape
    heads = width // HEAD
    chunks = 4
    vmem = pl.BlockSpec(memory_space=pltpu.VMEM)
    smem = pl.BlockSpec(memory_space=pltpu.SMEM)
    hbm = pl.BlockSpec(memory_space=pl.ANY)
    scratch = [
        ((chunks, depth // chunks, width), bf16),
        ((chunks, depth // chunks, width), bf16),
        ((depth, 2 * STATE), bf16),
        1 + 2 * chunks,
        ((count, width), bf16),
        None,
        ((devices, count), jnp.int32),
        ((2, devices, count), jnp.int32),
        ((IDS, devices, count), f32),
        ((ROWS, devices * count), bf16),
        ((128, devices * count), bf16),
        ((count, width), bf16),
        None,
        ((WINDOWS, width), f32),
        ((WINDOWS, 2 * width), bf16),
        ((16, width), f32),
        ((2, ROWS, width), bf16),
        ((2, ROWS, width), bf16),
        ((2, count, width), f32),
        ((2, count, 2 * width), bf16),
        ((2, count, width), f32),
        ((2, count, width), bf16),
        ((2, count, width), bf16),
        ((2, 3, heads, count), f32),
        ((2, heads, count, 128), f32),
        ((2, heads, count, 128), f32),
        ((count, 128), f32),
        ((2, 8, width), f32),
        ((2, count, count), f32),
        ((2, count, count), f32),
        ((2, heads, 128), f32),
    ]

    def space(item):
        if isinstance(item, tuple):
            return pltpu.VMEM(*item)
        return pltpu.SemaphoreType.DMA((item,)) if item else pltpu.SemaphoreType.DMA

    return pl.pallas_call(
        functools.partial(mixer_kernel, scale),
        in_specs=[vmem, vmem, smem, smem] + [vmem] * len(small) + [hbm] * len(large),
        out_specs=[hbm, vmem],
        out_shape=[
            jax.ShapeDtypeStruct((count, width), bf16),
            jax.ShapeDtypeStruct((8, 2 * STATE), f32),
        ],
        scratch_shapes=[space(item) for item in scratch],
        compiler_params=pltpu.CompilerParams(vmem_limit_bytes=56 * 2**20),
        name="mixer",
    )(
        near,
        far,
        rc_map,
        skip,
        *small,
        *large,
    )


def exchange(value, axis, distance):
    size = lax.axis_size(axis)
    return lax.ppermute(value, axis, [(i, i ^ distance) for i in range(size)])


def on_device(
    tokens,
    rc_map,
    embedding,
    norm_gain,
    w_values,
    w_gates,
    w_states,
    w_steps,
    conv_values,
    conv_states,
    step_bias,
    log_rate,
    skip_gain,
    head_gain,
    cotangent,
):
    devices = lax.axis_size("ctx")
    count = tokens.shape[0]
    near = jnp.minimum(tokens, IDS - 1).reshape(1, count)
    far = exchange(near, "ctx", 1)
    distance = 2
    while distance < devices:
        near = jnp.concatenate([near, far], axis=0)
        far = exchange(near, "ctx", distance)
        distance *= 2
    scale = 1.0 / math.sqrt(count * devices * HEAD)
    small = [
        embedding,
        norm_gain.reshape(1, -1),
        w_steps.T,
        conv_values,
        conv_states,
        step_bias.reshape(1, -1),
        log_rate.reshape(1, -1),
        head_gain.reshape(1, -1),
    ]
    large = [w_values, w_gates, w_states, cotangent]
    encoded, grads = mixer(near, far, rc_map, skip_gain, small, large, scale)
    for axis in ("tp", "ctx"):
        distance = 1
        while distance < lax.axis_size(axis):
            grads = grads + exchange(grads, axis, distance)
            distance *= 2
    head_total = log_rate.shape[0] * lax.axis_size("tp")
    return (encoded, grads[CONV, :head_total], grads[CONV + 1, :head_total], grads[:CONV])


def solution(mesh):
    placed = (
        P("ctx"),
        P(),
        P(),
        P(),
        P(None, "tp"),
        P(None, "tp"),
        P(),
        P(None, "tp"),
        P(None, "tp"),
        P(),
        P("tp"),
        P("tp"),
        P("tp"),
        P("tp"),
        P("ctx", "tp"),
    )
    return jax.shard_map(
        on_device,
        mesh=mesh,
        in_specs=placed,
        out_specs=(P("ctx", "tp"), P(), P(), P()),
        check_vma=False,
    )
```

```python
import functools
import math

import jax
import jax.numpy as jnp
from jax import lax
from jax.experimental import pallas as pl
from jax.experimental.pallas import tpu as pltpu
from jax.sharding import PartitionSpec as P

HEAD = 128
STATE = 128
CONV = 4
IDS = 4
WINDOWS = IDS**CONV
ROWS = WINDOWS + 16
UNROLL = 2
TABLES_VMEM = 53 * 2**20
MIXER_VMEM = 53 * 2**20
EPSILON = 1e-05

f32 = jnp.float32
bf16 = jnp.bfloat16
NN = (((1,), (0,)), ((), ()))
NT = (((1,), (1,)), ((), ()))
TN = (((0,), (0,)), ((), ()))


def iota(shape, dim):
    return lax.broadcasted_iota(jnp.int32, shape, dim)


def mm(a, b, dims=NN):
    return lax.dot_general(a, b, dims, preferred_element_type=f32)


def split(x):
    high = x.astype(bf16)
    return high, (x - high.astype(f32)).astype(bf16)


def mm3(a, b, dims=NN):
    return mm(a[0], b[0], dims) + (mm(a[0], b[1], dims) + mm(a[1], b[0], dims))


def rows_of(parts):
    return jnp.concatenate(parts, axis=0)


def lanes_of(parts):
    return jnp.concatenate(parts, axis=1)


def stacked(a, b2, dims=NN):
    count = a[0].shape[0]
    both = mm(rows_of([lanes_of([a[0], a[0]]), lanes_of([a[1], a[1]])]), b2, dims)
    return both[:count] + both[count:]


def stacked_out(a, b2, width, dims=NN):
    count = a[0].shape[0]
    both = mm(rows_of([a[0], a[1]]), b2, dims)
    both = both[:count] + both[count:]
    return both[:, :width] + both[:, width:]


def sigmoid(v):
    return 1.0 / (1.0 + jnp.exp(-v))


def tap_parts(table, taps):
    product = rows_of([taps[k : k + 1, :] * table for k in range(CONV)])
    p1 = product.astype(bf16)
    rest = product - p1.astype(f32)
    p2 = rest.astype(bf16)
    p3 = (rest - p2.astype(f32)).astype(bf16)
    return rows_of([p1, p2, p3, jnp.zeros_like(p1)])


def tables_kernel(normed_ref, wv_hbm, ws_hbm, tv_ref, ts_ref, held_v, held_s, sems):
    chunks, size, _ = held_v.shape
    copies = [pltpu.make_async_copy(ws_hbm, held_s, sems.at[chunks])]
    for i in range(chunks):
        copies.append(pltpu.make_async_copy(wv_hbm.at[pl.ds(i * size, size), :], held_v.at[i], sems.at[i]))
    for copy in copies:
        copy.start()
    normed = normed_ref[...]
    copies[0].wait()
    ts_ref[0:IDS, :] = mm(normed, held_s[...])
    ts_ref[IDS:, :] = jnp.zeros((8 - IDS, ts_ref.shape[1]), f32)
    product = None
    for i in range(chunks):
        copies[1 + i].wait()
        term = mm(normed[:, i * size : (i + 1) * size], held_v[i])
        product = term if product is None else product + term
    tv_ref[0:IDS, :] = product
    tv_ref[IDS:, :] = jnp.zeros((8 - IDS, tv_ref.shape[1]), f32)


def tables(normed, w_values, w_states):
    depth, width = w_values.shape
    chunks = 4
    vmem = pl.BlockSpec(memory_space=pltpu.VMEM)
    hbm = pl.BlockSpec(memory_space=pl.ANY)
    return pl.pallas_call(
        tables_kernel,
        in_specs=[vmem, hbm, hbm],
        out_specs=[vmem, vmem],
        out_shape=[
            jax.ShapeDtypeStruct((8, width), f32),
            jax.ShapeDtypeStruct((8, w_states.shape[1]), f32),
        ],
        scratch_shapes=[
            pltpu.VMEM((chunks, depth // chunks, width), bf16),
            pltpu.VMEM(w_states.shape, bf16),
            pltpu.SemaphoreType.DMA((1 + chunks,)),
        ],
        compiler_params=pltpu.CompilerParams(vmem_limit_bytes=TABLES_VMEM),
        name="tables",
    )(normed, w_values, w_states)


def mixer_kernel(
    scale,
    near_ref,
    far_ref,
    rc_ref,
    skip_ref,
    normed_ref,
    tv_ref,
    tbc_ref,
    dt_ref,
    cv_ref,
    cs_ref,
    bias_ref,
    rate_ref,
    gain_ref,
    cot_ref,
    wg_hbm,
    enc_hbm,
    grad_ref,
    held_g,
    sems,
    enc_ref,
    enc_sem,
    tok_s,
    ids_s,
    count_s,
    onehot_s,
    weight_s,
    xw_s,
    x2w_s,
    edge_s,
    wh_s,
    wl_s,
    x_s,
    x2_s,
    far_s,
    dh_s,
    dl_s,
    row_s,
    lcol_s,
    acol_s,
    tcol_s,
    gate_s,
    score_s,
    q_s,
    acc_s,
):
    devices, count = tok_s.shape
    width = cv_ref.shape[1]
    heads = width // HEAD
    here = lax.axis_index("ctx")
    tp_place = lax.axis_index("tp")
    chunks, size, _ = held_g.shape
    copies = []
    for i in range(chunks):
        copies.append(pltpu.make_async_copy(wg_hbm.at[pl.ds(i * size, size), :], held_g.at[i], sems.at[i]))
    for copy in copies:
        copy.start()

    half = near_ref.shape[0]
    for r in range(devices):
        own = near_ref[r : r + 1, :] if r < half else far_ref[r - half : r - half + 1, :]
        tok_s[pl.ds(jnp.bitwise_xor(here, r), 1), :] = own
    tok = tok_s[...]
    rc = [rc_ref[t] for t in range(IDS)]
    rtok = jnp.zeros_like(tok)
    for t in range(IDS):
        rtok = jnp.where(tok == t, rc[t], rtok)
    lane = iota((devices, count), 1)
    row = iota((devices, count), 0)

    def before(ids, shift):
        turned = pltpu.roll(ids, shift, 1)
        return jnp.where(lane < shift, pltpu.roll(turned, 1, 0), turned)

    def after(ids, shift):
        turned = pltpu.roll(ids, count - shift, 1)
        return jnp.where(lane >= count - shift, pltpu.roll(turned, devices - 1, 0), turned)

    kf = before(tok, 3) + IDS * before(tok, 2) + IDS**2 * before(tok, 1) + IDS**3 * tok
    kr = after(rtok, 3) + IDS * after(rtok, 2) + IDS**2 * after(rtok, 1) + IDS**3 * rtok
    first = row * count + lane
    last = devices * count - 1 - first
    kf = jnp.where(first < CONV - 1, WINDOWS + first, kf)
    kr = jnp.where(last < CONV - 1, WINDOWS + CONV - 1 + last, kr)
    ids_s[0] = kf
    ids_s[1] = kr

    eye = iota((heads, heads), 0) == iota((heads, heads), 1)
    column = lambda ref: jnp.sum(jnp.where(eye, ref[...], 0.0), axis=1, keepdims=True)
    raw = dt_ref[...] + column(bias_ref)
    rate = jnp.exp(column(rate_ref))
    step = jnp.maximum(raw, 0.0) + jnp.log1p(jnp.exp(-jnp.abs(raw)))
    slope = sigmoid(raw)
    ratio = jnp.where(step > 1e-37, slope / jnp.maximum(step, 1e-37), 1.0)

    def per_strand(table):
        own = [table[:, t : t + 1] for t in range(IDS)]
        mapped = []
        for t in range(IDS):
            picked = own[0]
            for other in range(1, IDS):
                picked = jnp.where(rc[t] == other, own[other], picked)
            mapped.append(picked)
        return own, mapped

    step_of, slope_of, ratio_of = per_strand(step), per_strand(slope), per_strand(ratio)
    log_of, alog_of = per_strand(-rate * step), per_strand(-rate * slope)

    masks = [(tok == t).astype(f32) for t in range(IDS)]
    upper = (iota((count, count), 0) <= iota((count, count), 1)).astype(bf16)
    for t in range(IDS):
        count_s[t] = mm(masks[t].astype(bf16), upper)
    totals = [jnp.sum(m, axis=1, keepdims=True) for m in masks]
    row1 = iota((devices, 1), 0)
    far_counts = []
    for t in range(IDS):
        between = jnp.zeros((devices, 1), f32)
        for j in range(devices):
            inside = ((row1 < j) & (j < here)) | ((row1 > j) & (j > here))
            between = between + jnp.where(inside, totals[t][j : j + 1, :], 0.0)
        inclusive = count_s[t]
        far_counts.append(
            jnp.where(row < here, totals[t] - inclusive, inclusive - masks[t]) + between
        )

    window_rows = iota((ROWS, count), 0)
    def earlier(j):
        forward = j < here
        reverse = j > here
        choose = lambda pair, t: jnp.where(forward, pair[0][t], pair[1][t])
        tok_j = tok[j : j + 1, :]
        log_sum = jnp.zeros((heads, count), f32)
        alog_sum = jnp.zeros((heads, count), f32)
        step_j = jnp.zeros((heads, count), f32)
        slope_j = jnp.zeros((heads, count), f32)
        for t in range(IDS):
            number = far_counts[t][j : j + 1, :]
            log_sum = log_sum + choose(log_of, t) * number
            alog_sum = alog_sum + choose(alog_of, t) * number
            step_j = jnp.where(tok_j == t, choose(step_of, t), step_j)
            slope_j = jnp.where(tok_j == t, choose(slope_of, t), slope_j)
        decay = jnp.exp(log_sum)
        weight = decay * step_j
        terms = jnp.concatenate([weight, weight * log_sum, decay * (slope_j + step_j * alog_sum)], axis=0)
        both = jnp.concatenate(
            [
                jnp.where(forward, terms, 0.0),
                jnp.where(reverse, terms, 0.0),
                jnp.zeros((64 - 6 * heads, count), f32),
            ],
            axis=0,
        )
        high, low = split(both)
        weight_s[0:64, j * count : (j + 1) * count] = high
        weight_s[64:128, j * count : (j + 1) * count] = low
        window_j = jnp.where(forward, kf[j : j + 1, :], kr[j : j + 1, :])
        onehot_s[:, j * count : (j + 1) * count] = (window_rows == window_j).astype(bf16)

    for j in range(devices):
        earlier(j)

    table_bc = tbc_ref[...]
    taps_v = tap_parts(tv_ref[...], cv_ref[...])
    taps_s = tap_parts(table_bc, cs_ref[...])
    product = None
    for i in range(chunks):
        copies[i].wait()
        term = mm(normed_ref[:, i * size : (i + 1) * size], held_g[i])
        product = term if product is None else product + term
    gates = rows_of([product, jnp.zeros((8 - IDS, width), f32)])
    gates = gates * sigmoid(gates)

    weights = mm(onehot_s[...], weight_s[...], NT)
    weights = weights + pltpu.roll(weights, 64, 1)

    lane_w = iota((WINDOWS, 128), 1)
    digit = (iota((WINDOWS, 128), 0) >> (2 * ((lane_w >> 3) & 3))) & 3
    pick = ((digit == (lane_w & 7)) & (lane_w < 96)).astype(f32).astype(bf16)
    for h in range(0, heads, 2):
        columns = slice(h * HEAD, (h + 2) * HEAD)
        summed = mm(pick, taps_v[:, columns])
        x = summed * sigmoid(summed)
        xw_s[:, columns] = x
        high, low = split(x)
        for i in range(2):
            at = 2 * (h + i) * HEAD
            own = slice(i * HEAD, (i + 1) * HEAD)
            x2w_s[:, at : at + HEAD] = high[:, own]
            x2w_s[:, at + HEAD : at + 2 * HEAD] = low[:, own]

    lane_e = iota((16, 128), 1)
    row_e = iota((16, 128), 0)
    tap_e = (lane_e >> 3) & 3
    edge = jnp.full((16, 128), IDS, jnp.int32)
    for u in range(CONV - 1):
        for k in range(CONV - 1 - u, CONV):
            at = u - (CONV - 1) + k
            edge = jnp.where((row_e == u) & (tap_e == k), tok[0:1, at : at + 1], edge)
            edge = jnp.where(
                (row_e == CONV - 1 + u) & (tap_e == k),
                rtok[devices - 1 : devices, count - 1 - at : count - at],
                edge,
            )
    edge_pick = ((edge == (lane_e & 7)) & (lane_e < 96)).astype(f32).astype(bf16)
    summed = mm(edge_pick, taps_v)
    edge_x = summed * sigmoid(summed)
    edge_s[...] = edge_x
    edge_high, edge_low = split(edge_x)
    edge_x2 = []
    for h in range(heads):
        edge_x2 += [edge_high[:, h * HEAD : (h + 1) * HEAD], edge_low[:, h * HEAD : (h + 1) * HEAD]]
    edge_x2 = jnp.concatenate(edge_x2, axis=1)
    pick = rows_of([pick, edge_pick])
    summed = mm(pick, taps_s)
    sig = sigmoid(summed)
    bc_all = summed * sig
    bc_slope = sig * (1.0 + summed * (1.0 - sig))
    bc = split(bc_all)
    b_all = (bc[0][:, :STATE], bc[1][:, :STATE])

    own_tok = tok_s[pl.ds(here, 1), :]
    own_masks = [(own_tok == t).astype(f32) for t in range(IDS)]
    own_counts = [[], []]
    for t in range(IDS):
        inclusive = count_s[t, pl.ds(here, 1), :]
        total = jnp.sum(own_masks[t], axis=1, keepdims=True)
        own_counts[0].append(inclusive)
        own_counts[1].append(total - inclusive + own_masks[t])
    turned = []
    for s in range(2):
        logs = sum(log_of[s][t] * own_counts[s][t] for t in range(IDS))
        alogs = sum(alog_of[s][t] * own_counts[s][t] for t in range(IDS))
        row_s[s, 0] = logs
        row_s[s, 1] = sum(step_of[s][t] * own_masks[t] for t in range(IDS))
        row_s[s, 2] = sum(ratio_of[s][t] * own_masks[t] for t in range(IDS)) - alogs
        turned += [logs, alogs]
    own_ids = [ids_s[s, pl.ds(here, 1), :] for s in range(2)]
    extra = jnp.concatenate(
        [own_ids[0].astype(f32), own_ids[1].astype(f32), own_tok.astype(f32), jnp.zeros((5, count), f32)],
        axis=0,
    )
    turned = jnp.concatenate(turned + [extra, jnp.zeros((120 - 4 * heads, count), f32)], axis=0).T
    for s in range(2):
        for h in range(heads):
            at = 2 * s * heads + h
            lcol_s[s, h] = jnp.broadcast_to(turned[:, at : at + 1], (count, 128))
            acol_s[s, h] = jnp.broadcast_to(turned[:, at + heads : at + heads + 1], (count, 128))
    base = 4 * heads
    tcol_s[...] = jnp.broadcast_to(turned[:, base + 2 : base + 3], (count, 128))
    gate_s[0] = gates
    for t in range(IDS):
        picked = gates[0:1, :]
        for other in range(1, IDS):
            picked = jnp.where(rc[t] == other, gates[other : other + 1, :], picked)
        gate_s[1, t : t + 1, :] = picked

    own_onehot = []
    lane_k = iota((count, ROWS), 1).astype(f32)
    picks = []
    for s in range(2):
        picks.append((lane_k == turned[:, base + s : base + s + 1]).astype(f32).astype(bf16))
        own_onehot.append((window_rows == own_ids[s]).astype(f32).astype(bf16))
    regular, edges = slice(0, WINDOWS), slice(WINDOWS, ROWS)
    both_picks = rows_of([picks[0][:, regular], picks[1][:, regular]])
    edge_picks = rows_of([picks[0][:16, edges], picks[1][count - 16 :, edges]])

    def gather(table, extra):
        got = mm(both_picks, table)
        more = mm(edge_picks, extra)
        return [
            rows_of([got[:16] + more[:16], got[16:count]]),
            rows_of([got[count : 2 * count - 16], got[2 * count - 16 :] + more[16:]]),
        ]

    for h in range(heads):
        columns = slice(2 * h * HEAD, 2 * (h + 1) * HEAD)
        for s, got in enumerate(gather(x2w_s[:, columns], edge_x2[:, columns])):
            x2_s[s, :, columns] = got.astype(bf16)
            x_s[s, :, h * HEAD : (h + 1) * HEAD] = got[:, :HEAD] + got[:, HEAD:]
    bc_high = gather(bc[0][regular], bc[0][edges])
    bc_low = gather(bc[1][regular], bc[1][edges])
    own_b, own_c, states = [], [], []
    for s in range(2):
        high, low = bc_high[s].astype(bf16), bc_low[s].astype(bf16)
        own_b.append((high[:, :STATE], low[:, :STATE]))
        own_c.append((high[:, STATE:], low[:, STATE:]))
        score_s[s] = stacked(own_c[s], lanes_of(own_b[s]), NT)
        for h in range(heads):
            at = 3 * s * heads + h
            columns = slice(h * HEAD, (h + 1) * HEAD)
            weighted = split(xw_s[:, columns] * weights[:WINDOWS, at : at + 1])
            wh_s[s, :WINDOWS, columns], wl_s[s, :WINDOWS, columns] = weighted
            weighted = split(edge_s[:, columns] * weights[WINDOWS:, at : at + 1])
            wh_s[s, WINDOWS:, columns], wl_s[s, WINDOWS:, columns] = weighted
        b2 = lanes_of([part[regular] for part in b_all])
        state = mm(b2, wh_s[s, regular], TN)
        state = state[:STATE] + state[STATE:] + mm(b2[:, :STATE], wl_s[s, regular], TN)
        state = state + mm(
            rows_of([b_all[0][edges], b_all[0][edges], b_all[1][edges]]),
            rows_of([wh_s[s, edges], wl_s[s, edges], wh_s[s, edges]]),
            TN,
        )
        states.append(rows_of(split(state)))
        far_s[s] = stacked(own_c[s], states[s])

    q_s[...] = jnp.zeros_like(q_s)
    tiles = count // 128
    triangle = [iota((128, 128), 0) >= iota((128, 128), 1), iota((128, 128), 0) <= iota((128, 128), 1)]

    nothing = jnp.zeros((128, 128), bf16)
    part = lambda j: slice(j * 128, (j + 1) * 128)

    def one_head(h, _):
        columns = pl.ds(pl.multiple_of(h * HEAD, HEAD), HEAD)
        columns2 = pl.ds(pl.multiple_of(h * 2 * HEAD, 2 * HEAD), 2 * HEAD)
        gain = gain_ref[:, columns]
        skip = skip_ref[h]
        outs = [None] * tiles
        rate_row = jnp.zeros((1, 128), f32)
        bias_row = jnp.zeros((1, 128), f32)
        factors, ys = [], []
        for s in range(2):
            log_row = row_s[s, 0, pl.ds(h, 1), :]
            step_row = row_s[s, 1, pl.ds(h, 1), :]
            highs, lows, own = [], [], {}
            for i in range(tiles):
                lcol = lcol_s[s, h, part(i), :]
                high_row, low_row = [], []
                for j in range(tiles):
                    if (j > i) if s == 0 else (j < i):
                        high, low = nothing, nothing
                    else:
                        gap = lcol - log_row[:, part(j)]
                        if j == i:
                            gap = jnp.where(triangle[s], gap, -1e30)
                        own[i, j] = jnp.exp(gap) * step_row[:, part(j)]
                        high, low = split(score_s[s, part(i), part(j)] * own[i, j])
                    high_row.append(high)
                    low_row.append(low)
                highs.append(lanes_of(high_row))
                lows.append(lanes_of(low_row))
            factors.append(own)
            both = mm(rows_of(highs + lows), x2_s[s, :, columns2])
            both = both[:count] + both[count:]
            ys.append(both[:, :HEAD] + both[:, HEAD:])
        for s in range(2):
            column_sums = [jnp.zeros((1, 128), f32) for _ in range(tiles)]
            log_row = row_s[s, 0, pl.ds(h, 1), :]
            mixed_row = row_s[s, 2, pl.ds(h, 1), :]
            highs, lows = [], []
            for i in range(tiles):
                lcol = lcol_s[s, h, part(i), :]
                grown = jnp.exp(lcol)
                y = ys[s][part(i)] + grown * far_s[s, part(i), columns]
                tcol = tcol_s[part(i), :]
                gate = gate_s[s, 0:1, columns]
                for t in range(1, IDS):
                    gate = jnp.where(tcol == t, gate_s[s, t : t + 1, columns], gate)
                gated = (y + skip * x_s[s, part(i), columns]) * gate
                inverse = lax.rsqrt(jnp.mean(gated * gated, axis=1, keepdims=True) + EPSILON)
                normal = gated * inverse
                outs[i] = normal if outs[i] is None else outs[i] + normal
                cot = cot_ref[part(i), columns].astype(f32) * gain
                shared = jnp.mean(cot * normal, axis=1, keepdims=True)
                dy = (cot - normal * shared) * (inverse * gate)
                high, low = split(dy)
                highs.append(lanes_of([high, high]))
                lows.append(lanes_of([low, low]))
                row_terms = dy * y
                rate_row += jnp.sum(lcol * row_terms, axis=0, keepdims=True)
                bias_row += jnp.sum(acol_s[s, h, part(i), :] * row_terms, axis=0, keepdims=True)
                dh_s[s, part(i), columns], dl_s[s, part(i), columns] = split(grown * dy)
            both = mm(rows_of(highs + lows), x2_s[s, :, columns2], NT)
            for i, j in factors[s]:
                e = both[part(i), part(j)] + both[part(tiles + i), part(j)]
                e = e * factors[s][i, j]
                q_s[s, part(i), part(j)] += e
                column_sums[j] = column_sums[j] + jnp.sum(e * score_s[s, part(i), part(j)], axis=0, keepdims=True)
            for j in range(tiles):
                rate_row -= log_row[:, part(j)] * column_sums[j]
                bias_row += mixed_row[:, part(j)] * column_sums[j]
        for i in range(tiles):
            enc_ref[i * 128 : (i + 1) * 128, columns] = (outs[i] * gain).astype(enc_ref.dtype)
        acc_s[0, pl.ds(h, 1), :] = rate_row
        acc_s[1, pl.ds(h, 1), :] = bias_row

    def some_heads(g, _):
        for i in range(UNROLL):
            one_head(g * UNROLL + i, 0)
        return 0

    lax.fori_loop(0, heads // UNROLL, some_heads, 0)

    enc_copy = pltpu.make_async_copy(enc_ref, enc_hbm, enc_sem)
    enc_copy.start()

    db_all = jnp.zeros((ROWS, STATE), f32)
    dc_all = jnp.zeros((ROWS, STATE), f32)
    for s in range(2):
        q = split(q_s[s])
        grown = (dh_s[s], dl_s[s])
        far = stacked_out(grown, states[s], STATE, NT)
        dc_own = split(stacked_out(q, lanes_of(own_b[s]), STATE) + far)
        db_own = split(mm3(q, own_c[s], TN))
        c2 = lanes_of(own_c[s])
        back = mm(c2, grown[0], TN)
        back = back[:STATE] + back[STATE:] + mm(own_c[s][0], grown[1], TN)
        back = rows_of(split(back))
        both = mm(own_onehot[s], lanes_of([db_own[0], dc_own[0]])) + mm(own_onehot[s], lanes_of([db_own[1], dc_own[1]]))
        dc_all = dc_all + both[:, STATE:]
        db_all = db_all + both[:, :STATE] + stacked_out((wh_s[s], wl_s[s]), back, STATE, NT)
        reach = stacked(b_all, back)
        for h in range(heads):
            at = 3 * s * heads + heads + h
            columns = slice(h * HEAD, (h + 1) * HEAD)
            x = rows_of([xw_s[:, columns], edge_s[:, columns]])
            terms = reach[:, columns] * x
            acc_s[0, h : h + 1, :] += jnp.sum(terms * weights[:, at : at + 1], axis=0, keepdims=True)
            acc_s[1, h : h + 1, :] += jnp.sum(
                terms * weights[:, at + heads : at + heads + 1], axis=0, keepdims=True
            )
    d_summed = split(jnp.concatenate([db_all, dc_all], axis=1) * bc_slope)
    by_tap = mm(pick, d_summed[0], TN) + mm(pick, d_summed[1], TN)
    grad_ref[...] = jnp.zeros_like(grad_ref)
    for k in range(CONV):
        grad_ref[k : k + 1, :] = scale * jnp.sum(by_tap[8 * k : 8 * k + 8, :] * table_bc, axis=0, keepdims=True)
    place = iota((heads, 128), 1) == iota((heads, 128), 0) + tp_place * heads
    for i in range(2):
        sums = scale * jnp.sum(acc_s[i], axis=1, keepdims=True)
        grad_ref[CONV + i : CONV + i + 1, 0:128] = jnp.sum(jnp.where(place, sums, 0.0), axis=0, keepdims=True)
    enc_copy.wait()


def mixer(near, far, rc_map, skip, small, w_gates, scale):
    devices, count = near.shape[0] + far.shape[0], near.shape[1]
    depth, width = w_gates.shape
    heads = width // HEAD
    chunks = 4
    vmem = pl.BlockSpec(memory_space=pltpu.VMEM)
    smem = pl.BlockSpec(memory_space=pltpu.SMEM)
    hbm = pl.BlockSpec(memory_space=pl.ANY)
    scratch = [
        ((chunks, depth // chunks, width), bf16),
        chunks,
        ((count, width), bf16),
        None,
        ((devices, count), jnp.int32),
        ((2, devices, count), jnp.int32),
        ((IDS, devices, count), f32),
        ((ROWS, devices * count), bf16),
        ((128, devices * count), bf16),
        ((WINDOWS, width), f32),
        ((WINDOWS, 2 * width), bf16),
        ((16, width), f32),
        ((2, ROWS, width), bf16),
        ((2, ROWS, width), bf16),
        ((2, count, width), f32),
        ((2, count, 2 * width), bf16),
        ((2, count, width), f32),
        ((2, count, width), bf16),
        ((2, count, width), bf16),
        ((2, 3, heads, count), f32),
        ((2, heads, count, 128), f32),
        ((2, heads, count, 128), f32),
        ((count, 128), f32),
        ((2, 8, width), f32),
        ((2, count, count), f32),
        ((2, count, count), f32),
        ((2, heads, 128), f32),
    ]

    def space(item):
        if isinstance(item, tuple):
            return pltpu.VMEM(*item)
        return pltpu.SemaphoreType.DMA((item,)) if item else pltpu.SemaphoreType.DMA

    return pl.pallas_call(
        functools.partial(mixer_kernel, scale),
        in_specs=[vmem, vmem, smem, smem] + [vmem] * len(small) + [hbm],
        out_specs=[hbm, vmem],
        out_shape=[
            jax.ShapeDtypeStruct((count, width), bf16),
            jax.ShapeDtypeStruct((8, 2 * STATE), f32),
        ],
        scratch_shapes=[space(item) for item in scratch],
        compiler_params=pltpu.CompilerParams(vmem_limit_bytes=MIXER_VMEM),
        name="mixer",
    )(
        near,
        far,
        rc_map,
        skip,
        *small,
        w_gates,
    )


def exchange(value, axis, distance):
    size = lax.axis_size(axis)
    return lax.ppermute(value, axis, [(i, i ^ distance) for i in range(size)])


def on_device(
    tokens,
    rc_map,
    embedding,
    norm_gain,
    w_values,
    w_gates,
    w_states,
    w_steps,
    conv_values,
    conv_states,
    step_bias,
    log_rate,
    skip_gain,
    head_gain,
    cotangent,
):
    devices = lax.axis_size("ctx")
    count = tokens.shape[0]
    near = jnp.minimum(tokens, IDS - 1).reshape(1, count)
    far = exchange(near, "ctx", 1)
    distance = 2
    while distance < devices:
        near = jnp.concatenate([near, far], axis=0)
        far = exchange(near, "ctx", distance)
        distance *= 2
    scale = 1.0 / math.sqrt(count * devices * HEAD)
    embedded = embedding.astype(f32)
    mean = jnp.mean(embedded * embedded, axis=1, keepdims=True)
    normed = (embedded * lax.rsqrt(mean + EPSILON) * norm_gain).astype(bf16)
    tv, tbc = tables(normed, w_values, w_states)
    dt = lax.dot_general(w_steps, normed, (((0,), (1,)), ((), ())), preferred_element_type=f32)
    small = [
        normed,
        tv,
        tbc,
        dt,
        conv_values,
        conv_states,
        step_bias.reshape(1, -1),
        log_rate.reshape(1, -1),
        head_gain.reshape(1, -1),
        cotangent,
    ]
    encoded, grads = mixer(near, far, rc_map, skip_gain, small, w_gates, scale)
    for axis in ("tp", "ctx"):
        distance = 1
        while distance < lax.axis_size(axis):
            grads = grads + exchange(grads, axis, distance)
            distance *= 2
    head_total = log_rate.shape[0] * lax.axis_size("tp")
    return (encoded, grads[CONV, :head_total], grads[CONV + 1, :head_total], grads[:CONV])


def solution(mesh):
    placed = (
        P("ctx"),
        P(),
        P(),
        P(),
        P(None, "tp"),
        P(None, "tp"),
        P(),
        P(None, "tp"),
        P(None, "tp"),
        P(),
        P("tp"),
        P("tp"),
        P("tp"),
        P("tp"),
        P("ctx", "tp"),
    )
    return jax.shard_map(
        on_device,
        mesh=mesh,
        in_specs=placed,
        out_specs=(P("ctx", "tp"), P(), P(), P()),
        check_vma=False,
    )
```

```python
import functools
import math

import jax
import jax.numpy as jnp
from jax import lax
from jax.experimental import pallas as pl
from jax.experimental.pallas import tpu as pltpu
from jax.sharding import PartitionSpec as P

HEAD = 128
STATE = 128
CONV = 4
IDS = 4
WINDOWS = IDS**CONV
ROWS = WINDOWS + 16
TABLES_VMEM = 53 * 2**20
MIXER_VMEM = 53 * 2**20
EPSILON = 1e-05

f32 = jnp.float32
bf16 = jnp.bfloat16
NN = (((1,), (0,)), ((), ()))
NT = (((1,), (1,)), ((), ()))
TN = (((0,), (0,)), ((), ()))


def iota(shape, dim):
    return lax.broadcasted_iota(jnp.int32, shape, dim)


def mm(a, b, dims=NN):
    return lax.dot_general(a, b, dims, preferred_element_type=f32)


def split(x):
    high = x.astype(bf16)
    return high, (x - high.astype(f32)).astype(bf16)


def mm3(a, b, dims=NN):
    return mm(a[0], b[0], dims) + (mm(a[0], b[1], dims) + mm(a[1], b[0], dims))


def rows_of(parts):
    return jnp.concatenate(parts, axis=0)


def lanes_of(parts):
    return jnp.concatenate(parts, axis=1)


def stacked(a, b2, dims=NN):
    count = a[0].shape[0]
    both = mm(rows_of([lanes_of([a[0], a[0]]), lanes_of([a[1], a[1]])]), b2, dims)
    return both[:count] + both[count:]


def stacked_out(a, b2, width, dims=NN):
    count = a[0].shape[0]
    both = mm(rows_of([a[0], a[1]]), b2, dims)
    both = both[:count] + both[count:]
    return both[:, :width] + both[:, width:]


def sigmoid(v):
    return 1.0 / (1.0 + jnp.exp(-v))


def tap_parts(table, taps):
    product = rows_of([taps[k : k + 1, :] * table for k in range(CONV)])
    p1 = product.astype(bf16)
    rest = product - p1.astype(f32)
    p2 = rest.astype(bf16)
    p3 = (rest - p2.astype(f32)).astype(bf16)
    return rows_of([p1, p2, p3, jnp.zeros_like(p1)])


def tables_kernel(count, normed_ref, *refs):
    weights, outs, held, sems = refs[:count], refs[count : 2 * count], refs[2 * count : 3 * count], refs[-1]
    copies = []
    for k in range(count):
        chunks, size, _ = held[k].shape
        for i in range(chunks):
            part = weights[k].at[pl.ds(i * size, size), :]
            copies.append(pltpu.make_async_copy(part, held[k].at[i], sems.at[len(copies)]))
    for copy in copies:
        copy.start()
    normed = normed_ref[...]
    done = 0
    for k in range(count):
        chunks, size, _ = held[k].shape
        product = None
        for i in range(chunks):
            copies[done].wait()
            done += 1
            term = mm(normed[:, i * size : (i + 1) * size], held[k][i])
            product = term if product is None else product + term
        outs[k][0:IDS, :] = product
        outs[k][IDS:, :] = jnp.zeros((8 - IDS, product.shape[1]), f32)


def tables(normed, weights, chunks):
    vmem = pl.BlockSpec(memory_space=pltpu.VMEM)
    hbm = pl.BlockSpec(memory_space=pl.ANY)
    depth = normed.shape[1]
    return pl.pallas_call(
        functools.partial(tables_kernel, len(weights)),
        in_specs=[vmem] + [hbm] * len(weights),
        out_specs=[vmem] * len(weights),
        out_shape=[jax.ShapeDtypeStruct((8, weight.shape[1]), f32) for weight in weights],
        scratch_shapes=[
            pltpu.VMEM((parts, depth // parts, weight.shape[1]), bf16) for weight, parts in zip(weights, chunks)
        ]
        + [pltpu.SemaphoreType.DMA((sum(chunks),))],
        compiler_params=pltpu.CompilerParams(vmem_limit_bytes=TABLES_VMEM),
        name="tables",
    )(normed, *weights)


def mixer_kernel(
    scale,
    near_ref,
    far_ref,
    rc_ref,
    skip_ref,
    tv_ref,
    tbc_ref,
    tz_ref,
    dt_ref,
    cv_ref,
    cs_ref,
    bias_ref,
    rate_ref,
    gain_ref,
    cot_ref,
    enc_hbm,
    grad_ref,
    enc_ref,
    enc_sem,
    tok_s,
    ids_s,
    count_s,
    onehot_s,
    weight_s,
    xw_s,
    x2w_s,
    edge_s,
    wh_s,
    wl_s,
    x_s,
    x2_s,
    far_s,
    dh_s,
    dl_s,
    row_s,
    lcol_s,
    acol_s,
    tcol_s,
    gate_s,
    score_s,
    q_s,
    acc_s,
):
    devices, count = tok_s.shape
    width = cv_ref.shape[1]
    heads = width // HEAD
    here = lax.axis_index("ctx")
    tp_place = lax.axis_index("tp")
    half = near_ref.shape[0]
    for r in range(devices):
        own = near_ref[r : r + 1, :] if r < half else far_ref[r - half : r - half + 1, :]
        tok_s[pl.ds(jnp.bitwise_xor(here, r), 1), :] = own
    tok = tok_s[...]
    rc = [rc_ref[:, t : t + 1] for t in range(IDS)]
    rtok = jnp.zeros_like(tok)
    for t in range(IDS):
        rtok = jnp.where(tok == t, rc[t], rtok)
    lane = iota((devices, count), 1)
    row = iota((devices, count), 0)

    def before(ids, shift):
        turned = pltpu.roll(ids, shift, 1)
        return jnp.where(lane < shift, pltpu.roll(turned, 1, 0), turned)

    def after(ids, shift):
        turned = pltpu.roll(ids, count - shift, 1)
        return jnp.where(lane >= count - shift, pltpu.roll(turned, devices - 1, 0), turned)

    kf = before(tok, 3) + IDS * before(tok, 2) + IDS**2 * before(tok, 1) + IDS**3 * tok
    kr = after(rtok, 3) + IDS * after(rtok, 2) + IDS**2 * after(rtok, 1) + IDS**3 * rtok
    first = row * count + lane
    last = devices * count - 1 - first
    kf = jnp.where(first < CONV - 1, WINDOWS + first, kf)
    kr = jnp.where(last < CONV - 1, WINDOWS + CONV - 1 + last, kr)
    ids_s[0] = kf
    ids_s[1] = kr

    eye = iota((heads, heads), 0) == iota((heads, heads), 1)
    column = lambda ref: jnp.sum(jnp.where(eye, ref[...], 0.0), axis=1, keepdims=True)
    raw = dt_ref[...] + column(bias_ref)
    rate = jnp.exp(column(rate_ref))
    step = jnp.maximum(raw, 0.0) + jnp.log1p(jnp.exp(-jnp.abs(raw)))
    slope = sigmoid(raw)
    ratio = jnp.where(step > 1e-37, slope / jnp.maximum(step, 1e-37), 1.0)

    def per_strand(table):
        own = [table[:, t : t + 1] for t in range(IDS)]
        mapped = []
        for t in range(IDS):
            picked = own[0]
            for other in range(1, IDS):
                picked = jnp.where(rc[t] == other, own[other], picked)
            mapped.append(picked)
        return own, mapped

    step_of, slope_of, ratio_of = per_strand(step), per_strand(slope), per_strand(ratio)
    log_of, alog_of = per_strand(-rate * step), per_strand(-rate * slope)

    masks = [(tok == t).astype(f32) for t in range(IDS)]
    upper = (iota((count, count), 0) <= iota((count, count), 1)).astype(bf16)
    for t in range(IDS):
        count_s[t] = mm(masks[t].astype(bf16), upper)
    totals = [jnp.sum(m, axis=1, keepdims=True) for m in masks]
    row1 = iota((devices, 1), 0)
    far_counts = []
    for t in range(IDS):
        between = jnp.zeros((devices, 1), f32)
        for j in range(devices):
            inside = ((row1 < j) & (j < here)) | ((row1 > j) & (j > here))
            between = between + jnp.where(inside, totals[t][j : j + 1, :], 0.0)
        inclusive = count_s[t]
        far_counts.append(
            jnp.where(row < here, totals[t] - inclusive, inclusive - masks[t]) + between
        )

    window_rows = iota((ROWS, count), 0)
    def earlier(j):
        forward = j < here
        reverse = j > here
        choose = lambda pair, t: jnp.where(forward, pair[0][t], pair[1][t])
        tok_j = tok[j : j + 1, :]
        log_sum = jnp.zeros((heads, count), f32)
        alog_sum = jnp.zeros((heads, count), f32)
        step_j = jnp.zeros((heads, count), f32)
        slope_j = jnp.zeros((heads, count), f32)
        for t in range(IDS):
            number = far_counts[t][j : j + 1, :]
            log_sum = log_sum + choose(log_of, t) * number
            alog_sum = alog_sum + choose(alog_of, t) * number
            step_j = jnp.where(tok_j == t, choose(step_of, t), step_j)
            slope_j = jnp.where(tok_j == t, choose(slope_of, t), slope_j)
        decay = jnp.exp(log_sum)
        weight = decay * step_j
        terms = jnp.concatenate([weight, weight * log_sum, decay * (slope_j + step_j * alog_sum)], axis=0)
        both = jnp.concatenate(
            [
                jnp.where(forward, terms, 0.0),
                jnp.where(reverse, terms, 0.0),
                jnp.zeros((64 - 6 * heads, count), f32),
            ],
            axis=0,
        )
        high, low = split(both)
        weight_s[0:64, j * count : (j + 1) * count] = high
        weight_s[64:128, j * count : (j + 1) * count] = low
        window_j = jnp.where(forward, kf[j : j + 1, :], kr[j : j + 1, :])
        onehot_s[:, j * count : (j + 1) * count] = (window_rows == window_j).astype(bf16)

    for j in range(devices):
        earlier(j)

    table_bc = tbc_ref[...]
    taps_v = tap_parts(tv_ref[...], cv_ref[...])
    taps_s = tap_parts(table_bc, cs_ref[...])
    weights = mm(onehot_s[...], weight_s[...], NT)
    weights = weights + pltpu.roll(weights, 64, 1)

    lane_w = iota((WINDOWS, 128), 1)
    digit = (iota((WINDOWS, 128), 0) >> (2 * ((lane_w >> 3) & 3))) & 3
    pick = ((digit == (lane_w & 7)) & (lane_w < 96)).astype(f32).astype(bf16)
    for h in range(0, heads, 2):
        columns = slice(h * HEAD, (h + 2) * HEAD)
        summed = mm(pick, taps_v[:, columns])
        x = summed * sigmoid(summed)
        xw_s[:, columns] = x
        high, low = split(x)
        for i in range(2):
            at = 2 * (h + i) * HEAD
            own = slice(i * HEAD, (i + 1) * HEAD)
            x2w_s[:, at : at + HEAD] = high[:, own]
            x2w_s[:, at + HEAD : at + 2 * HEAD] = low[:, own]

    lane_e = iota((16, 128), 1)
    row_e = iota((16, 128), 0)
    tap_e = (lane_e >> 3) & 3
    edge = jnp.full((16, 128), IDS, jnp.int32)
    for u in range(CONV - 1):
        for k in range(CONV - 1 - u, CONV):
            at = u - (CONV - 1) + k
            edge = jnp.where((row_e == u) & (tap_e == k), tok[0:1, at : at + 1], edge)
            edge = jnp.where(
                (row_e == CONV - 1 + u) & (tap_e == k),
                rtok[devices - 1 : devices, count - 1 - at : count - at],
                edge,
            )
    edge_pick = ((edge == (lane_e & 7)) & (lane_e < 96)).astype(f32).astype(bf16)
    summed = mm(edge_pick, taps_v)
    edge_x = summed * sigmoid(summed)
    edge_s[...] = edge_x
    edge_high, edge_low = split(edge_x)
    edge_x2 = []
    for h in range(heads):
        edge_x2 += [edge_high[:, h * HEAD : (h + 1) * HEAD], edge_low[:, h * HEAD : (h + 1) * HEAD]]
    edge_x2 = jnp.concatenate(edge_x2, axis=1)
    pick = rows_of([pick, edge_pick])
    summed = mm(pick, taps_s)
    sig = sigmoid(summed)
    bc_all = summed * sig
    bc_slope = sig * (1.0 + summed * (1.0 - sig))
    bc = split(bc_all)
    b_all = (bc[0][:, :STATE], bc[1][:, :STATE])

    own_tok = tok_s[pl.ds(here, 1), :]
    own_masks = [(own_tok == t).astype(f32) for t in range(IDS)]
    own_counts = [[], []]
    for t in range(IDS):
        inclusive = count_s[t, pl.ds(here, 1), :]
        total = jnp.sum(own_masks[t], axis=1, keepdims=True)
        own_counts[0].append(inclusive)
        own_counts[1].append(total - inclusive + own_masks[t])
    turned = []
    for s in range(2):
        logs = sum(log_of[s][t] * own_counts[s][t] for t in range(IDS))
        alogs = sum(alog_of[s][t] * own_counts[s][t] for t in range(IDS))
        row_s[s, 0] = logs
        row_s[s, 1] = sum(step_of[s][t] * own_masks[t] for t in range(IDS))
        row_s[s, 2] = sum(ratio_of[s][t] * own_masks[t] for t in range(IDS)) - alogs
        turned += [logs, alogs]
    own_ids = [ids_s[s, pl.ds(here, 1), :] for s in range(2)]
    extra = jnp.concatenate(
        [own_ids[0].astype(f32), own_ids[1].astype(f32), own_tok.astype(f32), jnp.zeros((5, count), f32)],
        axis=0,
    )
    turned = jnp.concatenate(turned + [extra, jnp.zeros((120 - 4 * heads, count), f32)], axis=0).T
    for s in range(2):
        for h in range(heads):
            at = 2 * s * heads + h
            lcol_s[s, h] = jnp.broadcast_to(turned[:, at : at + 1], (count, 128))
            acol_s[s, h] = jnp.broadcast_to(turned[:, at + heads : at + heads + 1], (count, 128))
    base = 4 * heads
    tcol_s[...] = jnp.broadcast_to(turned[:, base + 2 : base + 3], (count, 128))
    own_onehot = []
    lane_k = iota((count, ROWS), 1).astype(f32)
    picks = []
    for s in range(2):
        picks.append((lane_k == turned[:, base + s : base + s + 1]).astype(f32).astype(bf16))
        own_onehot.append((window_rows == own_ids[s]).astype(f32).astype(bf16))
    regular, edges = slice(0, WINDOWS), slice(WINDOWS, ROWS)
    both_picks = rows_of([picks[0][:, regular], picks[1][:, regular]])
    edge_picks = rows_of([picks[0][:16, edges], picks[1][count - 16 :, edges]])

    def gather(table, extra):
        got = mm(both_picks, table)
        more = mm(edge_picks, extra)
        return [
            rows_of([got[:16] + more[:16], got[16:count]]),
            rows_of([got[count : 2 * count - 16], got[2 * count - 16 :] + more[16:]]),
        ]

    for h in range(heads):
        columns = slice(2 * h * HEAD, 2 * (h + 1) * HEAD)
        for s, got in enumerate(gather(x2w_s[:, columns], edge_x2[:, columns])):
            x2_s[s, :, columns] = got.astype(bf16)
            x_s[s, :, h * HEAD : (h + 1) * HEAD] = got[:, :HEAD] + got[:, HEAD:]
    bc_high = gather(bc[0][regular], bc[0][edges])
    bc_low = gather(bc[1][regular], bc[1][edges])
    own_b, own_c, states = [], [], []
    for s in range(2):
        high, low = bc_high[s].astype(bf16), bc_low[s].astype(bf16)
        own_b.append((high[:, :STATE], low[:, :STATE]))
        own_c.append((high[:, STATE:], low[:, STATE:]))
        score_s[s] = stacked(own_c[s], lanes_of(own_b[s]), NT)
        for h in range(heads):
            at = 3 * s * heads + h
            columns = slice(h * HEAD, (h + 1) * HEAD)
            weighted = split(xw_s[:, columns] * weights[:WINDOWS, at : at + 1])
            wh_s[s, :WINDOWS, columns], wl_s[s, :WINDOWS, columns] = weighted
            weighted = split(edge_s[:, columns] * weights[WINDOWS:, at : at + 1])
            wh_s[s, WINDOWS:, columns], wl_s[s, WINDOWS:, columns] = weighted
        b2 = lanes_of([part[regular] for part in b_all])
        state = mm(b2, wh_s[s, regular], TN)
        state = state[:STATE] + state[STATE:] + mm(b2[:, :STATE], wl_s[s, regular], TN)
        state = state + mm(
            rows_of([b_all[0][edges], b_all[0][edges], b_all[1][edges]]),
            rows_of([wh_s[s, edges], wl_s[s, edges], wh_s[s, edges]]),
            TN,
        )
        states.append(rows_of(split(state)))
        far_s[s] = stacked(own_c[s], states[s])

    gates = tz_ref[...]
    gates = gates * sigmoid(gates)

    gate_s[0] = gates
    for t in range(IDS):
        picked = gates[0:1, :]
        for other in range(1, IDS):
            picked = jnp.where(rc[t] == other, gates[other : other + 1, :], picked)
        gate_s[1, t : t + 1, :] = picked


    q_s[...] = jnp.zeros_like(q_s)
    tiles = count // 128
    triangle = [iota((128, 128), 0) >= iota((128, 128), 1), iota((128, 128), 0) <= iota((128, 128), 1)]

    nothing = jnp.zeros((128, 128), bf16)
    part = lambda j: slice(j * 128, (j + 1) * 128)

    def one_head(h):
        columns = slice(h * HEAD, (h + 1) * HEAD)
        columns2 = slice(h * 2 * HEAD, (h + 1) * 2 * HEAD)
        gain = gain_ref[:, columns]
        skip = skip_ref[:, h : h + 1]
        outs = [None] * tiles
        rate_row = jnp.zeros((1, 128), f32)
        bias_row = jnp.zeros((1, 128), f32)
        factors, ys = [], []
        for s in range(2):
            log_row = row_s[s, 0, h : h + 1, :]
            step_row = row_s[s, 1, h : h + 1, :]
            highs, lows, own = [], [], {}
            for i in range(tiles):
                lcol = lcol_s[s, h, part(i), :]
                high_row, low_row = [], []
                for j in range(tiles):
                    if (j > i) if s == 0 else (j < i):
                        high, low = nothing, nothing
                    else:
                        gap = lcol - log_row[:, part(j)]
                        if j == i:
                            gap = jnp.where(triangle[s], gap, -1e30)
                        own[i, j] = jnp.exp(gap) * step_row[:, part(j)]
                        high, low = split(score_s[s, part(i), part(j)] * own[i, j])
                    high_row.append(high)
                    low_row.append(low)
                highs.append(lanes_of(high_row))
                lows.append(lanes_of(low_row))
            factors.append(own)
            both = mm(rows_of(highs + lows), x2_s[s, :, columns2])
            both = both[:count] + both[count:]
            ys.append(both[:, :HEAD] + both[:, HEAD:])
        for s in range(2):
            column_sums = [jnp.zeros((1, 128), f32) for _ in range(tiles)]
            log_row = row_s[s, 0, h : h + 1, :]
            mixed_row = row_s[s, 2, h : h + 1, :]
            highs, lows = [], []
            for i in range(tiles):
                lcol = lcol_s[s, h, part(i), :]
                grown = jnp.exp(lcol)
                y = ys[s][part(i)] + grown * far_s[s, part(i), columns]
                tcol = tcol_s[part(i), :]
                gate = gate_s[s, 0:1, columns]
                for t in range(1, IDS):
                    gate = jnp.where(tcol == t, gate_s[s, t : t + 1, columns], gate)
                gated = (y + skip * x_s[s, part(i), columns]) * gate
                inverse = lax.rsqrt(jnp.mean(gated * gated, axis=1, keepdims=True) + EPSILON)
                normal = gated * inverse
                outs[i] = normal if outs[i] is None else outs[i] + normal
                cot = cot_ref[part(i), columns].astype(f32) * gain
                shared = jnp.mean(cot * normal, axis=1, keepdims=True)
                dy = (cot - normal * shared) * (inverse * gate)
                high, low = split(dy)
                highs.append(lanes_of([high, high]))
                lows.append(lanes_of([low, low]))
                row_terms = dy * y
                rate_row += jnp.sum(lcol * row_terms, axis=0, keepdims=True)
                bias_row += jnp.sum(acol_s[s, h, part(i), :] * row_terms, axis=0, keepdims=True)
                dh_s[s, part(i), columns], dl_s[s, part(i), columns] = split(grown * dy)
            both = mm(rows_of(highs + lows), x2_s[s, :, columns2], NT)
            for i, j in factors[s]:
                e = both[part(i), part(j)] + both[part(tiles + i), part(j)]
                e = e * factors[s][i, j]
                q_s[s, part(i), part(j)] += e
                column_sums[j] = column_sums[j] + jnp.sum(e * score_s[s, part(i), part(j)], axis=0, keepdims=True)
            for j in range(tiles):
                rate_row -= log_row[:, part(j)] * column_sums[j]
                bias_row += mixed_row[:, part(j)] * column_sums[j]
        for i in range(tiles):
            enc_ref[i * 128 : (i + 1) * 128, columns] = (outs[i] * gain).astype(enc_ref.dtype)
        acc_s[0, h : h + 1, :] = rate_row
        acc_s[1, h : h + 1, :] = bias_row

    for h in range(heads):
        one_head(h)

    enc_copy = pltpu.make_async_copy(enc_ref, enc_hbm, enc_sem)
    enc_copy.start()

    db_all = jnp.zeros((ROWS, STATE), f32)
    dc_all = jnp.zeros((ROWS, STATE), f32)
    for s in range(2):
        q = split(q_s[s])
        grown = (dh_s[s], dl_s[s])
        far = stacked_out(grown, states[s], STATE, NT)
        dc_own = split(stacked_out(q, lanes_of(own_b[s]), STATE) + far)
        db_own = split(mm3(q, own_c[s], TN))
        c2 = lanes_of(own_c[s])
        back = mm(c2, grown[0], TN)
        back = back[:STATE] + back[STATE:] + mm(own_c[s][0], grown[1], TN)
        back = rows_of(split(back))
        both = mm(own_onehot[s], lanes_of([db_own[0], dc_own[0]])) + mm(own_onehot[s], lanes_of([db_own[1], dc_own[1]]))
        dc_all = dc_all + both[:, STATE:]
        db_all = db_all + both[:, :STATE] + stacked_out((wh_s[s], wl_s[s]), back, STATE, NT)
        reach = stacked(b_all, back)
        for h in range(heads):
            at = 3 * s * heads + heads + h
            columns = slice(h * HEAD, (h + 1) * HEAD)
            x = rows_of([xw_s[:, columns], edge_s[:, columns]])
            terms = reach[:, columns] * x
            acc_s[0, h : h + 1, :] += jnp.sum(terms * weights[:, at : at + 1], axis=0, keepdims=True)
            acc_s[1, h : h + 1, :] += jnp.sum(
                terms * weights[:, at + heads : at + heads + 1], axis=0, keepdims=True
            )
    d_summed = split(jnp.concatenate([db_all, dc_all], axis=1) * bc_slope)
    by_tap = mm(pick, d_summed[0], TN) + mm(pick, d_summed[1], TN)
    grad_ref[...] = jnp.zeros_like(grad_ref)
    for k in range(CONV):
        grad_ref[k : k + 1, :] = scale * jnp.sum(by_tap[8 * k : 8 * k + 8, :] * table_bc, axis=0, keepdims=True)
    place = iota((heads, 128), 1) == iota((heads, 128), 0) + tp_place * heads
    for i in range(2):
        sums = scale * jnp.sum(acc_s[i], axis=1, keepdims=True)
        grad_ref[CONV + i : CONV + i + 1, 0:128] = jnp.sum(jnp.where(place, sums, 0.0), axis=0, keepdims=True)
    enc_copy.wait()


def mixer(near, far, rc_map, skip, small, scale):
    devices, count = near.shape[0] + far.shape[0], near.shape[1]
    width = small[0].shape[1]
    heads = width // HEAD
    vmem = pl.BlockSpec(memory_space=pltpu.VMEM)
    hbm = pl.BlockSpec(memory_space=pl.ANY)
    scratch = [
        ((count, width), bf16),
        None,
        ((devices, count), jnp.int32),
        ((2, devices, count), jnp.int32),
        ((IDS, devices, count), f32),
        ((ROWS, devices * count), bf16),
        ((128, devices * count), bf16),
        ((WINDOWS, width), f32),
        ((WINDOWS, 2 * width), bf16),
        ((16, width), f32),
        ((2, ROWS, width), bf16),
        ((2, ROWS, width), bf16),
        ((2, count, width), f32),
        ((2, count, 2 * width), bf16),
        ((2, count, width), f32),
        ((2, count, width), bf16),
        ((2, count, width), bf16),
        ((2, 3, heads, count), f32),
        ((2, heads, count, 128), f32),
        ((2, heads, count, 128), f32),
        ((count, 128), f32),
        ((2, 8, width), f32),
        ((2, count, count), f32),
        ((2, count, count), f32),
        ((2, heads, 128), f32),
    ]

    def space(item):
        if isinstance(item, tuple):
            return pltpu.VMEM(*item)
        return pltpu.SemaphoreType.DMA((item,)) if item else pltpu.SemaphoreType.DMA

    return pl.pallas_call(
        functools.partial(mixer_kernel, scale),
        in_specs=[vmem] * (4 + len(small)),
        out_specs=[hbm, vmem],
        out_shape=[
            jax.ShapeDtypeStruct((count, width), bf16),
            jax.ShapeDtypeStruct((8, 2 * STATE), f32),
        ],
        scratch_shapes=[space(item) for item in scratch],
        compiler_params=pltpu.CompilerParams(vmem_limit_bytes=MIXER_VMEM),
        name="mixer",
    )(
        near,
        far,
        rc_map.reshape(1, IDS),
        skip.reshape(1, heads),
        *small,
    )


def exchange(value, axis, distance):
    size = lax.axis_size(axis)
    return lax.ppermute(value, axis, [(i, i ^ distance) for i in range(size)])


def on_device(
    tokens,
    rc_map,
    embedding,
    norm_gain,
    w_values,
    w_gates,
    w_states,
    w_steps,
    conv_values,
    conv_states,
    step_bias,
    log_rate,
    skip_gain,
    head_gain,
    cotangent,
):
    devices = lax.axis_size("ctx")
    count = tokens.shape[0]
    scale = 1.0 / math.sqrt(count * devices * HEAD)
    embedded = embedding.astype(f32)
    mean = jnp.mean(embedded * embedded, axis=1, keepdims=True)
    normed = (embedded * lax.rsqrt(mean + EPSILON) * norm_gain).astype(bf16)
    near = jnp.minimum(tokens, IDS - 1).reshape(1, count)
    far = exchange(tokens.reshape(1, count), "ctx", 1)
    tv = tbc = None
    distance = 2
    while distance < devices:
        near = jnp.concatenate([near, far], axis=0)
        if distance == 2:
            near, normed = lax.optimization_barrier((near, normed))
        if distance * 2 >= devices:
            tbc, tv = tables(normed, [w_states, w_values], [1, 4])
            near, tbc, tv, normed = lax.optimization_barrier((near, tbc, tv, normed))
        far = exchange(near, "ctx", distance)
        distance *= 2
    if tv is None:
        tbc, tv = tables(normed, [w_states, w_values], [1, 4])
    (tz,) = tables(normed, [w_gates], [4])
    dt = lax.dot_general(w_steps, normed, (((0,), (1,)), ((), ())), preferred_element_type=f32)
    small = [
        tv,
        tbc,
        tz,
        dt,
        conv_values,
        conv_states,
        step_bias.reshape(1, -1),
        log_rate.reshape(1, -1),
        head_gain.reshape(1, -1),
        cotangent,
    ]
    encoded, grads = mixer(near, far, rc_map, skip_gain, small, scale)
    for axis in ("tp", "ctx"):
        distance = 1
        while distance < lax.axis_size(axis):
            grads = grads + exchange(grads, axis, distance)
            distance *= 2
    head_total = log_rate.shape[0] * lax.axis_size("tp")
    return (encoded, grads[CONV, :head_total], grads[CONV + 1, :head_total], grads[:CONV])


def solution(mesh):
    placed = (
        P("ctx"),
        P(),
        P(),
        P(),
        P(None, "tp"),
        P(None, "tp"),
        P(),
        P(None, "tp"),
        P(None, "tp"),
        P(),
        P("tp"),
        P("tp"),
        P("tp"),
        P("tp"),
        P("ctx", "tp"),
    )
    return jax.shard_map(
        on_device,
        mesh=mesh,
        in_specs=placed,
        out_specs=(P("ctx", "tp"), P(), P(), P()),
        check_vma=False,
    )
```

```python
import functools
import math

import jax
import jax.numpy as jnp
from jax import lax
from jax.experimental import pallas as pl
from jax.experimental.pallas import tpu as pltpu
from jax.sharding import PartitionSpec as P

HEAD = 128
STATE = 128
CONV = 4
IDS = 4
WINDOWS = IDS**CONV
ROWS = WINDOWS + 16
TABLES_VMEM = 53 * 2**20
MIXER_VMEM = 53 * 2**20
EPSILON = 1e-05

f32 = jnp.float32
bf16 = jnp.bfloat16
NN = (((1,), (0,)), ((), ()))
NT = (((1,), (1,)), ((), ()))
TN = (((0,), (0,)), ((), ()))


def iota(shape, dim):
    return lax.broadcasted_iota(jnp.int32, shape, dim)


def mm(a, b, dims=NN):
    return lax.dot_general(a, b, dims, preferred_element_type=f32)


def split(x):
    high = x.astype(bf16)
    return high, (x - high.astype(f32)).astype(bf16)


def mm3(a, b, dims=NN):
    return mm(a[0], b[0], dims) + (mm(a[0], b[1], dims) + mm(a[1], b[0], dims))


def rows_of(parts):
    return jnp.concatenate(parts, axis=0)


def lanes_of(parts):
    return jnp.concatenate(parts, axis=1)


def stacked(a, b2, dims=NN):
    count = a[0].shape[0]
    both = mm(rows_of([lanes_of([a[0], a[0]]), lanes_of([a[1], a[1]])]), b2, dims)
    return both[:count] + both[count:]


def stacked_out(a, b2, width, dims=NN):
    count = a[0].shape[0]
    both = mm(rows_of([a[0], a[1]]), b2, dims)
    both = both[:count] + both[count:]
    return both[:, :width] + both[:, width:]


def sigmoid(v):
    return 1.0 / (1.0 + jnp.exp(-v))


def tap_parts(table, taps):
    product = rows_of([taps[k : k + 1, :] * table for k in range(CONV)])
    p1 = product.astype(bf16)
    rest = product - p1.astype(f32)
    p2 = rest.astype(bf16)
    p3 = (rest - p2.astype(f32)).astype(bf16)
    return rows_of([p1, p2, p3, jnp.zeros_like(p1)])


def tables_kernel(count, normed_ref, *refs):
    weights, outs, held, sems = refs[:count], refs[count : 2 * count], refs[2 * count : 3 * count], refs[-1]
    copies = []
    for k in range(count):
        chunks, size, _ = held[k].shape
        for i in range(chunks):
            part = weights[k].at[pl.ds(i * size, size), :]
            copies.append(pltpu.make_async_copy(part, held[k].at[i], sems.at[len(copies)]))
    for copy in copies:
        copy.start()
    normed = normed_ref[...]
    done = 0
    for k in range(count):
        chunks, size, _ = held[k].shape
        product = None
        for i in range(chunks):
            copies[done].wait()
            done += 1
            term = mm(normed[:, i * size : (i + 1) * size], held[k][i])
            product = term if product is None else product + term
        outs[k][0:IDS, :] = product
        outs[k][IDS:, :] = jnp.zeros((8 - IDS, product.shape[1]), f32)


def tables(normed, weights, chunks):
    vmem = pl.BlockSpec(memory_space=pltpu.VMEM)
    hbm = pl.BlockSpec(memory_space=pl.ANY)
    depth = normed.shape[1]
    return pl.pallas_call(
        functools.partial(tables_kernel, len(weights)),
        in_specs=[vmem] + [hbm] * len(weights),
        out_specs=[vmem] * len(weights),
        out_shape=[jax.ShapeDtypeStruct((8, weight.shape[1]), f32) for weight in weights],
        scratch_shapes=[
            pltpu.VMEM((parts, depth // parts, weight.shape[1]), bf16) for weight, parts in zip(weights, chunks)
        ]
        + [pltpu.SemaphoreType.DMA((sum(chunks),))],
        compiler_params=pltpu.CompilerParams(vmem_limit_bytes=TABLES_VMEM),
        name="tables",
    )(normed, *weights)


def mixer_kernel(
    scale,
    near_ref,
    far_ref,
    rc_ref,
    skip_ref,
    tv_ref,
    tbc_ref,
    tz_ref,
    dt_ref,
    cv_ref,
    cs_ref,
    bias_ref,
    rate_ref,
    gain_ref,
    cot_ref,
    enc_hbm,
    grad_ref,
    enc_ref,
    enc_sem,
    tok_s,
    ids_s,
    count_s,
    onehot_s,
    weight_s,
    xw_s,
    x2w_s,
    edge_s,
    wh_s,
    wl_s,
    x_s,
    x2_s,
    far_s,
    dh_s,
    dl_s,
    row_s,
    lcol_s,
    acol_s,
    tcol_s,
    gate_s,
    score_s,
    q_s,
    acc_s,
    back_s,
):
    devices, count = tok_s.shape
    width = cv_ref.shape[1]
    heads = width // HEAD
    here = lax.axis_index("ctx")
    tp_place = lax.axis_index("tp")
    half = near_ref.shape[0]
    for r in range(devices):
        own = near_ref[r : r + 1, :] if r < half else far_ref[r - half : r - half + 1, :]
        tok_s[pl.ds(jnp.bitwise_xor(here, r), 1), :] = own
    tok = tok_s[...]
    rc = [rc_ref[:, t : t + 1] for t in range(IDS)]
    rtok = jnp.zeros_like(tok)
    for t in range(IDS):
        rtok = jnp.where(tok == t, rc[t], rtok)
    lane = iota((devices, count), 1)
    row = iota((devices, count), 0)

    def before(ids, shift):
        turned = pltpu.roll(ids, shift, 1)
        return jnp.where(lane < shift, pltpu.roll(turned, 1, 0), turned)

    def after(ids, shift):
        turned = pltpu.roll(ids, count - shift, 1)
        return jnp.where(lane >= count - shift, pltpu.roll(turned, devices - 1, 0), turned)

    kf = before(tok, 3) + IDS * before(tok, 2) + IDS**2 * before(tok, 1) + IDS**3 * tok
    kr = after(rtok, 3) + IDS * after(rtok, 2) + IDS**2 * after(rtok, 1) + IDS**3 * rtok
    first = row * count + lane
    last = devices * count - 1 - first
    kf = jnp.where(first < CONV - 1, WINDOWS + first, kf)
    kr = jnp.where(last < CONV - 1, WINDOWS + CONV - 1 + last, kr)
    ids_s[0] = kf
    ids_s[1] = kr

    eye = iota((heads, heads), 0) == iota((heads, heads), 1)
    column = lambda ref: jnp.sum(jnp.where(eye, ref[...], 0.0), axis=1, keepdims=True)
    raw = dt_ref[...] + column(bias_ref)
    rate = jnp.exp(column(rate_ref))
    step = jnp.maximum(raw, 0.0) + jnp.log1p(jnp.exp(-jnp.abs(raw)))
    slope = sigmoid(raw)
    ratio = jnp.where(step > 1e-37, slope / jnp.maximum(step, 1e-37), 1.0)

    def per_strand(table):
        own = [table[:, t : t + 1] for t in range(IDS)]
        mapped = []
        for t in range(IDS):
            picked = own[0]
            for other in range(1, IDS):
                picked = jnp.where(rc[t] == other, own[other], picked)
            mapped.append(picked)
        return own, mapped

    step_of, slope_of, ratio_of = per_strand(step), per_strand(slope), per_strand(ratio)
    log_of, alog_of = per_strand(-rate * step), per_strand(-rate * slope)

    masks = [(tok == t).astype(f32) for t in range(IDS)]
    upper = (iota((count, count), 0) <= iota((count, count), 1)).astype(bf16)
    for t in range(IDS):
        count_s[t] = mm(masks[t].astype(bf16), upper)
    totals = [jnp.sum(m, axis=1, keepdims=True) for m in masks]
    row1 = iota((devices, 1), 0)
    far_counts = []
    for t in range(IDS):
        between = jnp.zeros((devices, 1), f32)
        for j in range(devices):
            inside = ((row1 < j) & (j < here)) | ((row1 > j) & (j > here))
            between = between + jnp.where(inside, totals[t][j : j + 1, :], 0.0)
        inclusive = count_s[t]
        far_counts.append(
            jnp.where(row < here, totals[t] - inclusive, inclusive - masks[t]) + between
        )

    window_rows = iota((ROWS, count), 0)
    def earlier(j):
        forward = j < here
        reverse = j > here
        choose = lambda pair, t: jnp.where(forward, pair[0][t], pair[1][t])
        tok_j = tok[j : j + 1, :]
        log_sum = jnp.zeros((heads, count), f32)
        alog_sum = jnp.zeros((heads, count), f32)
        step_j = jnp.zeros((heads, count), f32)
        slope_j = jnp.zeros((heads, count), f32)
        for t in range(IDS):
            number = far_counts[t][j : j + 1, :]
            log_sum = log_sum + choose(log_of, t) * number
            alog_sum = alog_sum + choose(alog_of, t) * number
            step_j = jnp.where(tok_j == t, choose(step_of, t), step_j)
            slope_j = jnp.where(tok_j == t, choose(slope_of, t), slope_j)
        decay = jnp.exp(log_sum)
        weight = decay * step_j
        terms = jnp.concatenate([weight, weight * log_sum, decay * (slope_j + step_j * alog_sum)], axis=0)
        both = jnp.concatenate(
            [
                jnp.where(forward, terms, 0.0),
                jnp.where(reverse, terms, 0.0),
                jnp.zeros((64 - 6 * heads, count), f32),
            ],
            axis=0,
        )
        high, low = split(both)
        weight_s[0:64, j * count : (j + 1) * count] = high
        weight_s[64:128, j * count : (j + 1) * count] = low
        window_j = jnp.where(forward, kf[j : j + 1, :], kr[j : j + 1, :])
        onehot_s[:, j * count : (j + 1) * count] = (window_rows == window_j).astype(bf16)

    for j in range(devices):
        earlier(j)

    table_bc = tbc_ref[...]
    taps_v = tap_parts(tv_ref[...], cv_ref[...])
    taps_s = tap_parts(table_bc, cs_ref[...])
    weights = mm(onehot_s[...], weight_s[...], NT)
    weights = weights + pltpu.roll(weights, 64, 1)

    lane_w = iota((WINDOWS, 128), 1)
    digit = (iota((WINDOWS, 128), 0) >> (2 * ((lane_w >> 3) & 3))) & 3
    pick = ((digit == (lane_w & 7)) & (lane_w < 96)).astype(f32).astype(bf16)
    for h in range(0, heads, 2):
        columns = slice(h * HEAD, (h + 2) * HEAD)
        summed = mm(pick, taps_v[:, columns])
        x = summed * sigmoid(summed)
        xw_s[:, columns] = x
        high, low = split(x)
        for i in range(2):
            at = 2 * (h + i) * HEAD
            own = slice(i * HEAD, (i + 1) * HEAD)
            x2w_s[:, at : at + HEAD] = high[:, own]
            x2w_s[:, at + HEAD : at + 2 * HEAD] = low[:, own]

    lane_e = iota((16, 128), 1)
    row_e = iota((16, 128), 0)
    tap_e = (lane_e >> 3) & 3
    edge = jnp.full((16, 128), IDS, jnp.int32)
    for u in range(CONV - 1):
        for k in range(CONV - 1 - u, CONV):
            at = u - (CONV - 1) + k
            edge = jnp.where((row_e == u) & (tap_e == k), tok[0:1, at : at + 1], edge)
            edge = jnp.where(
                (row_e == CONV - 1 + u) & (tap_e == k),
                rtok[devices - 1 : devices, count - 1 - at : count - at],
                edge,
            )
    edge_pick = ((edge == (lane_e & 7)) & (lane_e < 96)).astype(f32).astype(bf16)
    summed = mm(edge_pick, taps_v)
    edge_x = summed * sigmoid(summed)
    edge_s[...] = edge_x
    edge_high, edge_low = split(edge_x)
    edge_x2 = []
    for h in range(heads):
        edge_x2 += [edge_high[:, h * HEAD : (h + 1) * HEAD], edge_low[:, h * HEAD : (h + 1) * HEAD]]
    edge_x2 = jnp.concatenate(edge_x2, axis=1)
    pick = rows_of([pick, edge_pick])
    summed = mm(pick, taps_s)
    sig = sigmoid(summed)
    bc_all = summed * sig
    bc_slope = sig * (1.0 + summed * (1.0 - sig))
    bc = split(bc_all)
    b_all = (bc[0][:, :STATE], bc[1][:, :STATE])

    own_tok = tok_s[pl.ds(here, 1), :]
    own_masks = [(own_tok == t).astype(f32) for t in range(IDS)]
    own_counts = [[], []]
    for t in range(IDS):
        inclusive = count_s[t, pl.ds(here, 1), :]
        total = jnp.sum(own_masks[t], axis=1, keepdims=True)
        own_counts[0].append(inclusive)
        own_counts[1].append(total - inclusive + own_masks[t])
    turned = []
    for s in range(2):
        logs = sum(log_of[s][t] * own_counts[s][t] for t in range(IDS))
        alogs = sum(alog_of[s][t] * own_counts[s][t] for t in range(IDS))
        row_s[s, 0] = logs
        row_s[s, 1] = sum(step_of[s][t] * own_masks[t] for t in range(IDS))
        row_s[s, 2] = sum(ratio_of[s][t] * own_masks[t] for t in range(IDS)) - alogs
        turned += [logs, alogs]
    own_ids = [ids_s[s, pl.ds(here, 1), :] for s in range(2)]
    extra = jnp.concatenate(
        [own_ids[0].astype(f32), own_ids[1].astype(f32), own_tok.astype(f32), jnp.zeros((5, count), f32)],
        axis=0,
    )
    turned = jnp.concatenate(turned + [extra, jnp.zeros((120 - 4 * heads, count), f32)], axis=0).T
    for s in range(2):
        for h in range(heads):
            at = 2 * s * heads + h
            lcol_s[s, h] = jnp.broadcast_to(turned[:, at : at + 1], (count, 128))
            acol_s[s, h] = jnp.broadcast_to(turned[:, at + heads : at + heads + 1], (count, 128))
    base = 4 * heads
    tcol_s[...] = jnp.broadcast_to(turned[:, base + 2 : base + 3], (count, 128))
    own_onehot = []
    lane_k = iota((count, ROWS), 1).astype(f32)
    picks = []
    for s in range(2):
        picks.append((lane_k == turned[:, base + s : base + s + 1]).astype(f32).astype(bf16))
        own_onehot.append((window_rows == own_ids[s]).astype(f32).astype(bf16))
    regular, edges = slice(0, WINDOWS), slice(WINDOWS, ROWS)
    both_picks = rows_of([picks[0][:, regular], picks[1][:, regular]])
    edge_picks = rows_of([picks[0][:16, edges], picks[1][count - 16 :, edges]])

    def gather(table, extra):
        got = mm(both_picks, table)
        more = mm(edge_picks, extra)
        return [
            rows_of([got[:16] + more[:16], got[16:count]]),
            rows_of([got[count : 2 * count - 16], got[2 * count - 16 :] + more[16:]]),
        ]

    for h in range(heads):
        columns = slice(2 * h * HEAD, 2 * (h + 1) * HEAD)
        for s, got in enumerate(gather(x2w_s[:, columns], edge_x2[:, columns])):
            x2_s[s, :, columns] = got.astype(bf16)
            x_s[s, :, h * HEAD : (h + 1) * HEAD] = got[:, :HEAD] + got[:, HEAD:]
    bc_high = gather(bc[0][regular], bc[0][edges])
    bc_low = gather(bc[1][regular], bc[1][edges])
    gates = tz_ref[...]
    gates = gates * sigmoid(gates)

    gate_s[0] = gates
    for t in range(IDS):
        picked = gates[0:1, :]
        for other in range(1, IDS):
            picked = jnp.where(rc[t] == other, gates[other : other + 1, :], picked)
        gate_s[1, t : t + 1, :] = picked
    own_b, own_c, states = [], [], [None, None]
    for s in range(2):
        high, low = bc_high[s].astype(bf16), bc_low[s].astype(bf16)
        own_b.append((high[:, :STATE], low[:, :STATE]))
        own_c.append((high[:, STATE:], low[:, STATE:]))
        score_s[s] = stacked(own_c[s], lanes_of(own_b[s]), NT)
    b2 = lanes_of([part[regular] for part in b_all])

    def enter(s):
        for h in range(heads):
            at = 3 * s * heads + h
            columns = slice(h * HEAD, (h + 1) * HEAD)
            weighted = split(xw_s[:, columns] * weights[:WINDOWS, at : at + 1])
            wh_s[s, :WINDOWS, columns], wl_s[s, :WINDOWS, columns] = weighted
            weighted = split(edge_s[:, columns] * weights[WINDOWS:, at : at + 1])
            wh_s[s, WINDOWS:, columns], wl_s[s, WINDOWS:, columns] = weighted
        state = mm(b2, wh_s[s, regular], TN)
        state = state[:STATE] + state[STATE:] + mm(b2[:, :STATE], wl_s[s, regular], TN)
        state = state + mm(
            rows_of([b_all[0][edges], b_all[0][edges], b_all[1][edges]]),
            rows_of([wh_s[s, edges], wl_s[s, edges], wh_s[s, edges]]),
            TN,
        )
        states[s] = rows_of(split(state))
        far_s[s] = stacked(own_c[s], states[s])

    q_s[...] = jnp.zeros_like(q_s)
    tiles = count // 128
    triangle = [iota((128, 128), 0) >= iota((128, 128), 1), iota((128, 128), 0) <= iota((128, 128), 1)]

    nothing = jnp.zeros((128, 128), bf16)
    part = lambda j: slice(j * 128, (j + 1) * 128)

    def mix(h):
        columns2 = slice(h * 2 * HEAD, (h + 1) * 2 * HEAD)
        factors, ys = [], []
        for s in range(2):
            log_row = row_s[s, 0, h : h + 1, :]
            step_row = row_s[s, 1, h : h + 1, :]
            highs, lows, own = [], [], {}
            for i in range(tiles):
                lcol = lcol_s[s, h, part(i), :]
                high_row, low_row = [], []
                for j in range(tiles):
                    if (j > i) if s == 0 else (j < i):
                        high, low = nothing, nothing
                    else:
                        gap = lcol - log_row[:, part(j)]
                        if j == i:
                            gap = jnp.where(triangle[s], gap, -1e30)
                        own[i, j] = jnp.exp(gap) * step_row[:, part(j)]
                        high, low = split(score_s[s, part(i), part(j)] * own[i, j])
                    high_row.append(high)
                    low_row.append(low)
                highs.append(lanes_of(high_row))
                lows.append(lanes_of(low_row))
            factors.append(own)
            both = mm(rows_of(highs + lows), x2_s[s, :, columns2])
            both = both[:count] + both[count:]
            ys.append(both[:, :HEAD] + both[:, HEAD:])
        return factors, ys

    def gate_rows(h, ys):
        columns = slice(h * HEAD, (h + 1) * HEAD)
        columns2 = slice(h * 2 * HEAD, (h + 1) * 2 * HEAD)
        gain = gain_ref[:, columns]
        skip = skip_ref[:, h : h + 1]
        outs = [None] * tiles
        rate_row = jnp.zeros((1, 128), f32)
        bias_row = jnp.zeros((1, 128), f32)
        pairs = []
        for s in range(2):
            highs, lows = [], []
            for i in range(tiles):
                lcol = lcol_s[s, h, part(i), :]
                grown = jnp.exp(lcol)
                y = ys[s][part(i)] + grown * far_s[s, part(i), columns]
                tcol = tcol_s[part(i), :]
                gate = gate_s[s, 0:1, columns]
                for t in range(1, IDS):
                    gate = jnp.where(tcol == t, gate_s[s, t : t + 1, columns], gate)
                gated = (y + skip * x_s[s, part(i), columns]) * gate
                inverse = lax.rsqrt(jnp.mean(gated * gated, axis=1, keepdims=True) + EPSILON)
                normal = gated * inverse
                outs[i] = normal if outs[i] is None else outs[i] + normal
                cot = cot_ref[part(i), columns].astype(f32) * gain
                shared = jnp.mean(cot * normal, axis=1, keepdims=True)
                dy = (cot - normal * shared) * (inverse * gate)
                high, low = split(dy)
                highs.append(lanes_of([high, high]))
                lows.append(lanes_of([low, low]))
                row_terms = dy * y
                rate_row += jnp.sum(lcol * row_terms, axis=0, keepdims=True)
                bias_row += jnp.sum(acol_s[s, h, part(i), :] * row_terms, axis=0, keepdims=True)
                dh_s[s, part(i), columns], dl_s[s, part(i), columns] = split(grown * dy)
            pairs.append(mm(rows_of(highs + lows), x2_s[s, :, columns2], NT))
        for i in range(tiles):
            enc_ref[i * 128 : (i + 1) * 128, columns] = (outs[i] * gain).astype(enc_ref.dtype)
        return pairs, rate_row, bias_row

    def settle(h, factors, pairs, rate_row, bias_row):
        for s in range(2):
            column_sums = [jnp.zeros((1, 128), f32) for _ in range(tiles)]
            log_row = row_s[s, 0, h : h + 1, :]
            mixed_row = row_s[s, 2, h : h + 1, :]
            for i, j in factors[s]:
                e = pairs[s][part(i), part(j)] + pairs[s][part(tiles + i), part(j)]
                e = e * factors[s][i, j]
                q_s[s, part(i), part(j)] += e
                column_sums[j] = column_sums[j] + jnp.sum(e * score_s[s, part(i), part(j)], axis=0, keepdims=True)
            for j in range(tiles):
                rate_row -= log_row[:, part(j)] * column_sums[j]
                bias_row += mixed_row[:, part(j)] * column_sums[j]
        acc_s[0, h : h + 1, :] = rate_row
        acc_s[1, h : h + 1, :] = bias_row

    def reach_back(first):
        columns = slice(first * HEAD, (first + 2) * HEAD)
        for s in range(2):
            back = mm(lanes_of(own_c[s]), dh_s[s, :, columns], TN)
            back = back[:STATE] + back[STATE:] + mm(own_c[s][0], dl_s[s, :, columns], TN)
            back = rows_of(split(back))
            back_s[s, :, columns] = back
            reach = stacked(b_all, back)
            for h in (first, first + 1):
                at = 3 * s * heads + heads + h
                own = slice((h - first) * HEAD, (h - first + 1) * HEAD)
                whole = slice(h * HEAD, (h + 1) * HEAD)
                terms = reach[:, own] * rows_of([xw_s[:, whole], edge_s[:, whole]])
                acc_s[0, h : h + 1, :] += jnp.sum(terms * weights[:, at : at + 1], axis=0, keepdims=True)
                acc_s[1, h : h + 1, :] += jnp.sum(
                    terms * weights[:, at + heads : at + heads + 1], axis=0, keepdims=True
                )

    mixed = {0: mix(0)}
    enter(0)
    mixed[1] = mix(1)
    enter(1)
    for h in range(heads):
        if 1 <= h < heads - 1:
            mixed[h + 1] = mix(h + 1)
        factors, ys = mixed.pop(h)
        settle(h, factors, *gate_rows(h, ys))
        if h % 2 == 1:
            reach_back(h - 1)

    enc_copy = pltpu.make_async_copy(enc_ref, enc_hbm, enc_sem)
    enc_copy.start()

    db_all = jnp.zeros((ROWS, STATE), f32)
    dc_all = jnp.zeros((ROWS, STATE), f32)
    for s in range(2):
        q = split(q_s[s])
        grown = (dh_s[s], dl_s[s])
        far = stacked_out(grown, states[s], STATE, NT)
        dc_own = split(stacked_out(q, lanes_of(own_b[s]), STATE) + far)
        db_own = split(mm3(q, own_c[s], TN))
        both = mm(own_onehot[s], lanes_of([db_own[0], dc_own[0]])) + mm(own_onehot[s], lanes_of([db_own[1], dc_own[1]]))
        dc_all = dc_all + both[:, STATE:]
        db_all = db_all + both[:, :STATE] + stacked_out((wh_s[s], wl_s[s]), back_s[s], STATE, NT)
    d_summed = split(jnp.concatenate([db_all, dc_all], axis=1) * bc_slope)
    by_tap = mm(pick, d_summed[0], TN) + mm(pick, d_summed[1], TN)
    grad_ref[...] = jnp.zeros_like(grad_ref)
    for k in range(CONV):
        grad_ref[k : k + 1, :] = scale * jnp.sum(by_tap[8 * k : 8 * k + 8, :] * table_bc, axis=0, keepdims=True)
    place = iota((heads, 128), 1) == iota((heads, 128), 0) + tp_place * heads
    for i in range(2):
        sums = scale * jnp.sum(acc_s[i], axis=1, keepdims=True)
        grad_ref[CONV + i : CONV + i + 1, 0:128] = jnp.sum(jnp.where(place, sums, 0.0), axis=0, keepdims=True)
    enc_copy.wait()


def mixer(near, far, rc_map, skip, small, scale):
    devices, count = near.shape[0] + far.shape[0], near.shape[1]
    width = small[0].shape[1]
    heads = width // HEAD
    vmem = pl.BlockSpec(memory_space=pltpu.VMEM)
    hbm = pl.BlockSpec(memory_space=pl.ANY)
    scratch = [
        ((count, width), bf16),
        None,
        ((devices, count), jnp.int32),
        ((2, devices, count), jnp.int32),
        ((IDS, devices, count), f32),
        ((ROWS, devices * count), bf16),
        ((128, devices * count), bf16),
        ((WINDOWS, width), f32),
        ((WINDOWS, 2 * width), bf16),
        ((16, width), f32),
        ((2, ROWS, width), bf16),
        ((2, ROWS, width), bf16),
        ((2, count, width), f32),
        ((2, count, 2 * width), bf16),
        ((2, count, width), f32),
        ((2, count, width), bf16),
        ((2, count, width), bf16),
        ((2, 3, heads, count), f32),
        ((2, heads, count, 128), f32),
        ((2, heads, count, 128), f32),
        ((count, 128), f32),
        ((2, 8, width), f32),
        ((2, count, count), f32),
        ((2, count, count), f32),
        ((2, heads, 128), f32),
        ((2, 2 * STATE, width), bf16),
    ]

    def space(item):
        if isinstance(item, tuple):
            return pltpu.VMEM(*item)
        return pltpu.SemaphoreType.DMA((item,)) if item else pltpu.SemaphoreType.DMA

    return pl.pallas_call(
        functools.partial(mixer_kernel, scale),
        in_specs=[vmem] * (4 + len(small)),
        out_specs=[hbm, vmem],
        out_shape=[
            jax.ShapeDtypeStruct((count, width), bf16),
            jax.ShapeDtypeStruct((8, 2 * STATE), f32),
        ],
        scratch_shapes=[space(item) for item in scratch],
        compiler_params=pltpu.CompilerParams(vmem_limit_bytes=MIXER_VMEM),
        name="mixer",
    )(
        near,
        far,
        rc_map.reshape(1, IDS),
        skip.reshape(1, heads),
        *small,
    )


def exchange(value, axis, distance):
    size = lax.axis_size(axis)
    return lax.ppermute(value, axis, [(i, i ^ distance) for i in range(size)])


def on_device(
    tokens,
    rc_map,
    embedding,
    norm_gain,
    w_values,
    w_gates,
    w_states,
    w_steps,
    conv_values,
    conv_states,
    step_bias,
    log_rate,
    skip_gain,
    head_gain,
    cotangent,
):
    devices = lax.axis_size("ctx")
    count = tokens.shape[0]
    scale = 1.0 / math.sqrt(count * devices * HEAD)
    embedded = embedding.astype(f32)
    mean = jnp.mean(embedded * embedded, axis=1, keepdims=True)
    normed = (embedded * lax.rsqrt(mean + EPSILON) * norm_gain).astype(bf16)
    near = jnp.minimum(tokens, IDS - 1).reshape(1, count)
    far = exchange(tokens.reshape(1, count), "ctx", 1)
    tv = tbc = None
    distance = 2
    while distance < devices:
        near = jnp.concatenate([near, far], axis=0)
        if distance == 2:
            near, normed = lax.optimization_barrier((near, normed))
        if distance * 2 >= devices:
            tbc, tv = tables(normed, [w_states, w_values], [1, 4])
            near, tbc, tv, normed = lax.optimization_barrier((near, tbc, tv, normed))
        far = exchange(near, "ctx", distance)
        distance *= 2
    if tv is None:
        tbc, tv = tables(normed, [w_states, w_values], [1, 4])
    (tz,) = tables(normed, [w_gates], [4])
    dt = lax.dot_general(w_steps, normed, (((0,), (1,)), ((), ())), preferred_element_type=f32)
    small = [
        tv,
        tbc,
        tz,
        dt,
        conv_values,
        conv_states,
        step_bias.reshape(1, -1),
        log_rate.reshape(1, -1),
        head_gain.reshape(1, -1),
        cotangent,
    ]
    encoded, grads = mixer(near, far, rc_map, skip_gain, small, scale)
    for axis in ("tp", "ctx"):
        distance = 1
        while distance < lax.axis_size(axis):
            grads = grads + exchange(grads, axis, distance)
            distance *= 2
    head_total = log_rate.shape[0] * lax.axis_size("tp")
    return (encoded, grads[CONV, :head_total], grads[CONV + 1, :head_total], grads[:CONV])


def solution(mesh):
    placed = (
        P("ctx"),
        P(),
        P(),
        P(),
        P(None, "tp"),
        P(None, "tp"),
        P(),
        P(None, "tp"),
        P(None, "tp"),
        P(),
        P("tp"),
        P("tp"),
        P("tp"),
        P("tp"),
        P("ctx", "tp"),
    )
    return jax.shard_map(
        on_device,
        mesh=mesh,
        in_specs=placed,
        out_specs=(P("ctx", "tp"), P(), P(), P()),
        check_vma=False,
    )
```

```python
import functools
import math

import jax
import jax.numpy as jnp
from jax import lax
from jax.experimental import pallas as pl
from jax.experimental.pallas import tpu as pltpu
from jax.sharding import PartitionSpec as P

HEAD = 128
STATE = 128
CONV = 4
IDS = 4
WINDOWS = IDS**CONV
ROWS = WINDOWS + 16
TABLES_VMEM = 53 * 2**20
MIXER_VMEM = 53 * 2**20
EPSILON = 1e-05

f32 = jnp.float32
bf16 = jnp.bfloat16
NN = (((1,), (0,)), ((), ()))
NT = (((1,), (1,)), ((), ()))
TN = (((0,), (0,)), ((), ()))


def iota(shape, dim):
    return lax.broadcasted_iota(jnp.int32, shape, dim)


def mm(a, b, dims=NN):
    return lax.dot_general(a, b, dims, preferred_element_type=f32)


def split(x):
    high = x.astype(bf16)
    return high, (x - high.astype(f32)).astype(bf16)


def mm3(a, b, dims=NN):
    return mm(a[0], b[0], dims) + (mm(a[0], b[1], dims) + mm(a[1], b[0], dims))


def rows_of(parts):
    return jnp.concatenate(parts, axis=0)


def lanes_of(parts):
    return jnp.concatenate(parts, axis=1)


def stacked(a, b2, dims=NN):
    count = a[0].shape[0]
    both = mm(rows_of([lanes_of([a[0], a[0]]), lanes_of([a[1], a[1]])]), b2, dims)
    return both[:count] + both[count:]


def stacked_out(a, b2, width, dims=NN):
    count = a[0].shape[0]
    both = mm(rows_of([a[0], a[1]]), b2, dims)
    both = both[:count] + both[count:]
    return both[:, :width] + both[:, width:]


def sigmoid(v):
    return 1.0 / (1.0 + jnp.exp(-v))


def tap_parts(table, taps):
    product = rows_of([taps[k : k + 1, :] * table for k in range(CONV)])
    p1 = product.astype(bf16)
    rest = product - p1.astype(f32)
    p2 = rest.astype(bf16)
    p3 = (rest - p2.astype(f32)).astype(bf16)
    return rows_of([p1, p2, p3, jnp.zeros_like(p1)])


def tables_kernel(count, normed_ref, *refs):
    weights, outs, held, sems = refs[:count], refs[count : 2 * count], refs[2 * count : 3 * count], refs[-1]
    copies = []
    for k in range(count):
        chunks, size, _ = held[k].shape
        for i in range(chunks):
            part = weights[k].at[pl.ds(i * size, size), :]
            copies.append(pltpu.make_async_copy(part, held[k].at[i], sems.at[len(copies)]))
    for copy in copies:
        copy.start()
    normed = normed_ref[...]
    done = 0
    for k in range(count):
        chunks, size, _ = held[k].shape
        product = None
        for i in range(chunks):
            copies[done].wait()
            done += 1
            term = mm(normed[:, i * size : (i + 1) * size], held[k][i])
            product = term if product is None else product + term
        outs[k][0:IDS, :] = product
        outs[k][IDS:, :] = jnp.zeros((8 - IDS, product.shape[1]), f32)


def tables(normed, weights, chunks):
    vmem = pl.BlockSpec(memory_space=pltpu.VMEM)
    hbm = pl.BlockSpec(memory_space=pl.ANY)
    depth = normed.shape[1]
    return pl.pallas_call(
        functools.partial(tables_kernel, len(weights)),
        in_specs=[vmem] + [hbm] * len(weights),
        out_specs=[vmem] * len(weights),
        out_shape=[jax.ShapeDtypeStruct((8, weight.shape[1]), f32) for weight in weights],
        scratch_shapes=[
            pltpu.VMEM((parts, depth // parts, weight.shape[1]), bf16) for weight, parts in zip(weights, chunks)
        ]
        + [pltpu.SemaphoreType.DMA((sum(chunks),))],
        compiler_params=pltpu.CompilerParams(vmem_limit_bytes=TABLES_VMEM),
        name="tables",
    )(normed, *weights)


def mixer_kernel(
    scale,
    near_ref,
    far_ref,
    rc_ref,
    skip_ref,
    tv_ref,
    tbc_ref,
    tz_ref,
    dt_ref,
    cv_ref,
    cs_ref,
    bias_ref,
    rate_ref,
    gain_ref,
    cot_ref,
    enc_hbm,
    grad_ref,
    enc_ref,
    enc_sem,
    tok_s,
    ids_s,
    count_s,
    onehot_s,
    weight_s,
    xw_s,
    x2w_s,
    edge_s,
    wh_s,
    wl_s,
    x_s,
    x2_s,
    far_s,
    dh_s,
    dl_s,
    row_s,
    lcol_s,
    acol_s,
    tcol_s,
    gate_s,
    score_s,
    q_s,
    acc_s,
    back_s,
):
    devices, count = tok_s.shape
    width = cv_ref.shape[1]
    heads = width // HEAD
    here = lax.axis_index("ctx")
    tp_place = lax.axis_index("tp")
    half = near_ref.shape[0]
    for r in range(devices):
        own = near_ref[r : r + 1, :] if r < half else far_ref[r - half : r - half + 1, :]
        tok_s[pl.ds(jnp.bitwise_xor(here, r), 1), :] = own
    tok = tok_s[...]
    rc = [rc_ref[:, t : t + 1] for t in range(IDS)]
    rtok = jnp.zeros_like(tok)
    for t in range(IDS):
        rtok = jnp.where(tok == t, rc[t], rtok)
    lane = iota((devices, count), 1)
    row = iota((devices, count), 0)

    def before(ids, shift):
        turned = pltpu.roll(ids, shift, 1)
        return jnp.where(lane < shift, pltpu.roll(turned, 1, 0), turned)

    def after(ids, shift):
        turned = pltpu.roll(ids, count - shift, 1)
        return jnp.where(lane >= count - shift, pltpu.roll(turned, devices - 1, 0), turned)

    kf = before(tok, 3) + IDS * before(tok, 2) + IDS**2 * before(tok, 1) + IDS**3 * tok
    kr = after(rtok, 3) + IDS * after(rtok, 2) + IDS**2 * after(rtok, 1) + IDS**3 * rtok
    first = row * count + lane
    last = devices * count - 1 - first
    kf = jnp.where(first < CONV - 1, WINDOWS + first, kf)
    kr = jnp.where(last < CONV - 1, WINDOWS + CONV - 1 + last, kr)
    ids_s[0] = kf
    ids_s[1] = kr

    eye = iota((heads, heads), 0) == iota((heads, heads), 1)
    column = lambda ref: jnp.sum(jnp.where(eye, ref[...], 0.0), axis=1, keepdims=True)
    raw = dt_ref[...] + column(bias_ref)
    rate = jnp.exp(column(rate_ref))
    step = jnp.maximum(raw, 0.0) + jnp.log1p(jnp.exp(-jnp.abs(raw)))
    slope = sigmoid(raw)
    ratio = jnp.where(step > 1e-37, slope / jnp.maximum(step, 1e-37), 1.0)

    def per_strand(table):
        own = [table[:, t : t + 1] for t in range(IDS)]
        mapped = []
        for t in range(IDS):
            picked = own[0]
            for other in range(1, IDS):
                picked = jnp.where(rc[t] == other, own[other], picked)
            mapped.append(picked)
        return own, mapped

    step_of, slope_of, ratio_of = per_strand(step), per_strand(slope), per_strand(ratio)
    log_of, alog_of = per_strand(-rate * step), per_strand(-rate * slope)

    masks = [(tok == t).astype(f32) for t in range(IDS)]
    upper = (iota((count, count), 0) <= iota((count, count), 1)).astype(bf16)
    for t in range(IDS):
        count_s[t] = mm(masks[t].astype(bf16), upper)
    totals = [jnp.sum(m, axis=1, keepdims=True) for m in masks]
    row1 = iota((devices, 1), 0)
    far_counts = []
    for t in range(IDS):
        between = jnp.zeros((devices, 1), f32)
        for j in range(devices):
            inside = ((row1 < j) & (j < here)) | ((row1 > j) & (j > here))
            between = between + jnp.where(inside, totals[t][j : j + 1, :], 0.0)
        inclusive = count_s[t]
        far_counts.append(
            jnp.where(row < here, totals[t] - inclusive, inclusive - masks[t]) + between
        )

    own_tok = tok_s[pl.ds(here, 1), :]
    own_masks = [(own_tok == t).astype(f32) for t in range(IDS)]
    own_counts = [[], []]
    for t in range(IDS):
        inclusive = count_s[t, pl.ds(here, 1), :]
        total = jnp.sum(own_masks[t], axis=1, keepdims=True)
        own_counts[0].append(inclusive)
        own_counts[1].append(total - inclusive + own_masks[t])
    turned = []
    for s in range(2):
        logs = sum(log_of[s][t] * own_counts[s][t] for t in range(IDS))
        alogs = sum(alog_of[s][t] * own_counts[s][t] for t in range(IDS))
        row_s[s, 0] = logs
        row_s[s, 1] = sum(step_of[s][t] * own_masks[t] for t in range(IDS))
        row_s[s, 2] = sum(ratio_of[s][t] * own_masks[t] for t in range(IDS)) - alogs
        turned += [logs, alogs]
    own_ids = [ids_s[s, pl.ds(here, 1), :] for s in range(2)]
    extra = jnp.concatenate(
        [own_ids[0].astype(f32), own_ids[1].astype(f32), own_tok.astype(f32), jnp.zeros((5, count), f32)],
        axis=0,
    )
    turned = jnp.concatenate(turned + [extra, jnp.zeros((120 - 4 * heads, count), f32)], axis=0).T
    base = 4 * heads
    tcol_s[...] = jnp.broadcast_to(turned[:, base + 2 : base + 3], (count, 128))
    window_rows = iota((ROWS, count), 0)
    def earlier(j):
        forward = j < here
        reverse = j > here
        choose = lambda pair, t: jnp.where(forward, pair[0][t], pair[1][t])
        tok_j = tok[j : j + 1, :]
        log_sum = jnp.zeros((heads, count), f32)
        alog_sum = jnp.zeros((heads, count), f32)
        step_j = jnp.zeros((heads, count), f32)
        slope_j = jnp.zeros((heads, count), f32)
        for t in range(IDS):
            number = far_counts[t][j : j + 1, :]
            log_sum = log_sum + choose(log_of, t) * number
            alog_sum = alog_sum + choose(alog_of, t) * number
            step_j = jnp.where(tok_j == t, choose(step_of, t), step_j)
            slope_j = jnp.where(tok_j == t, choose(slope_of, t), slope_j)
        decay = jnp.exp(log_sum)
        weight = decay * step_j
        terms = jnp.concatenate([weight, weight * log_sum, decay * (slope_j + step_j * alog_sum)], axis=0)
        both = jnp.concatenate(
            [
                jnp.where(forward, terms, 0.0),
                jnp.where(reverse, terms, 0.0),
                jnp.zeros((64 - 6 * heads, count), f32),
            ],
            axis=0,
        )
        high, low = split(both)
        weight_s[0:64, j * count : (j + 1) * count] = high
        weight_s[64:128, j * count : (j + 1) * count] = low
        window_j = jnp.where(forward, kf[j : j + 1, :], kr[j : j + 1, :])
        onehot_s[:, j * count : (j + 1) * count] = (window_rows == window_j).astype(bf16)

    for j in range(devices):
        earlier(j)

    table_bc = tbc_ref[...]
    taps_v = tap_parts(tv_ref[...], cv_ref[...])
    taps_s = tap_parts(table_bc, cs_ref[...])
    weights = mm(onehot_s[...], weight_s[...], NT)
    weights = weights + pltpu.roll(weights, 64, 1)

    lane_w = iota((WINDOWS, 128), 1)
    digit = (iota((WINDOWS, 128), 0) >> (2 * ((lane_w >> 3) & 3))) & 3
    pick = ((digit == (lane_w & 7)) & (lane_w < 96)).astype(f32).astype(bf16)
    for h in range(0, heads, 2):
        columns = slice(h * HEAD, (h + 2) * HEAD)
        summed = mm(pick, taps_v[:, columns])
        x = summed * sigmoid(summed)
        xw_s[:, columns] = x
        high, low = split(x)
        for i in range(2):
            at = 2 * (h + i) * HEAD
            own = slice(i * HEAD, (i + 1) * HEAD)
            x2w_s[:, at : at + HEAD] = high[:, own]
            x2w_s[:, at + HEAD : at + 2 * HEAD] = low[:, own]

    lane_e = iota((16, 128), 1)
    row_e = iota((16, 128), 0)
    tap_e = (lane_e >> 3) & 3
    edge = jnp.full((16, 128), IDS, jnp.int32)
    for u in range(CONV - 1):
        for k in range(CONV - 1 - u, CONV):
            at = u - (CONV - 1) + k
            edge = jnp.where((row_e == u) & (tap_e == k), tok[0:1, at : at + 1], edge)
            edge = jnp.where(
                (row_e == CONV - 1 + u) & (tap_e == k),
                rtok[devices - 1 : devices, count - 1 - at : count - at],
                edge,
            )
    edge_pick = ((edge == (lane_e & 7)) & (lane_e < 96)).astype(f32).astype(bf16)
    summed = mm(edge_pick, taps_v)
    edge_x = summed * sigmoid(summed)
    edge_s[...] = edge_x
    edge_high, edge_low = split(edge_x)
    edge_x2 = []
    for h in range(heads):
        edge_x2 += [edge_high[:, h * HEAD : (h + 1) * HEAD], edge_low[:, h * HEAD : (h + 1) * HEAD]]
    edge_x2 = jnp.concatenate(edge_x2, axis=1)
    pick = rows_of([pick, edge_pick])
    summed = mm(pick, taps_s)
    sig = sigmoid(summed)
    bc_all = summed * sig
    bc_slope = sig * (1.0 + summed * (1.0 - sig))
    bc = split(bc_all)
    b_all = (bc[0][:, :STATE], bc[1][:, :STATE])

    own_onehot = []
    lane_k = iota((count, ROWS), 1).astype(f32)
    picks = []
    for s in range(2):
        picks.append((lane_k == turned[:, base + s : base + s + 1]).astype(f32).astype(bf16))
        own_onehot.append((window_rows == own_ids[s]).astype(f32).astype(bf16))
    regular, edges = slice(0, WINDOWS), slice(WINDOWS, ROWS)
    both_picks = rows_of([picks[0][:, regular], picks[1][:, regular]])
    edge_picks = rows_of([picks[0][:16, edges], picks[1][count - 16 :, edges]])

    def gather(table, extra):
        got = mm(both_picks, table)
        more = mm(edge_picks, extra)
        return [
            rows_of([got[:16] + more[:16], got[16:count]]),
            rows_of([got[count : 2 * count - 16], got[2 * count - 16 :] + more[16:]]),
        ]

    for h in range(heads):
        columns = slice(2 * h * HEAD, 2 * (h + 1) * HEAD)
        for s, got in enumerate(gather(x2w_s[:, columns], edge_x2[:, columns])):
            x2_s[s, :, columns] = got.astype(bf16)
            x_s[s, :, h * HEAD : (h + 1) * HEAD] = got[:, :HEAD] + got[:, HEAD:]
    bc_high = gather(bc[0][regular], bc[0][edges])
    bc_low = gather(bc[1][regular], bc[1][edges])
    gates = tz_ref[...]
    gates = gates * sigmoid(gates)

    gate_s[0] = gates
    for t in range(IDS):
        picked = gates[0:1, :]
        for other in range(1, IDS):
            picked = jnp.where(rc[t] == other, gates[other : other + 1, :], picked)
        gate_s[1, t : t + 1, :] = picked
    own_b, own_c, states = [], [], [None, None]
    for s in range(2):
        high, low = bc_high[s].astype(bf16), bc_low[s].astype(bf16)
        own_b.append((high[:, :STATE], low[:, :STATE]))
        own_c.append((high[:, STATE:], low[:, STATE:]))
        score_s[s] = stacked(own_c[s], lanes_of(own_b[s]), NT)
    b2 = lanes_of([part[regular] for part in b_all])

    def enter(s):
        for h in range(heads):
            at = 3 * s * heads + h
            columns = slice(h * HEAD, (h + 1) * HEAD)
            weighted = split(xw_s[:, columns] * weights[:WINDOWS, at : at + 1])
            wh_s[s, :WINDOWS, columns], wl_s[s, :WINDOWS, columns] = weighted
            weighted = split(edge_s[:, columns] * weights[WINDOWS:, at : at + 1])
            wh_s[s, WINDOWS:, columns], wl_s[s, WINDOWS:, columns] = weighted
        state = mm(b2, wh_s[s, regular], TN)
        state = state[:STATE] + state[STATE:] + mm(b2[:, :STATE], wl_s[s, regular], TN)
        state = state + mm(
            rows_of([b_all[0][edges], b_all[0][edges], b_all[1][edges]]),
            rows_of([wh_s[s, edges], wl_s[s, edges], wh_s[s, edges]]),
            TN,
        )
        states[s] = rows_of(split(state))
        far_s[s] = stacked(own_c[s], states[s])

    q_s[...] = jnp.zeros_like(q_s)
    tiles = count // 128
    triangle = [iota((128, 128), 0) >= iota((128, 128), 1), iota((128, 128), 0) <= iota((128, 128), 1)]

    nothing = jnp.zeros((128, 128), bf16)
    part = lambda j: slice(j * 128, (j + 1) * 128)

    def mix(h):
        columns2 = slice(h * 2 * HEAD, (h + 1) * 2 * HEAD)
        for s in range(2):
            at = 2 * s * heads + h
            lcol_s[s, h] = jnp.broadcast_to(turned[:, at : at + 1], (count, 128))
            acol_s[s, h] = jnp.broadcast_to(turned[:, at + heads : at + heads + 1], (count, 128))
        factors, ys = [], []
        for s in range(2):
            log_row = row_s[s, 0, h : h + 1, :]
            step_row = row_s[s, 1, h : h + 1, :]
            highs, lows, own = [], [], {}
            for i in range(tiles):
                lcol = lcol_s[s, h, part(i), :]
                high_row, low_row = [], []
                for j in range(tiles):
                    if (j > i) if s == 0 else (j < i):
                        high, low = nothing, nothing
                    else:
                        gap = lcol - log_row[:, part(j)]
                        if j == i:
                            gap = jnp.where(triangle[s], gap, -1e30)
                        own[i, j] = jnp.exp(gap) * step_row[:, part(j)]
                        high, low = split(score_s[s, part(i), part(j)] * own[i, j])
                    high_row.append(high)
                    low_row.append(low)
                highs.append(lanes_of(high_row))
                lows.append(lanes_of(low_row))
            factors.append(own)
            both = mm(rows_of(highs + lows), x2_s[s, :, columns2])
            both = both[:count] + both[count:]
            ys.append(both[:, :HEAD] + both[:, HEAD:])
        return factors, ys

    def gate_rows(h, ys):
        columns = slice(h * HEAD, (h + 1) * HEAD)
        columns2 = slice(h * 2 * HEAD, (h + 1) * 2 * HEAD)
        gain = gain_ref[:, columns]
        skip = skip_ref[:, h : h + 1]
        outs = [None] * tiles
        rate_row = jnp.zeros((1, 128), f32)
        bias_row = jnp.zeros((1, 128), f32)
        pairs = []
        for s in range(2):
            highs, lows = [], []
            for i in range(tiles):
                lcol = lcol_s[s, h, part(i), :]
                grown = jnp.exp(lcol)
                y = ys[s][part(i)] + grown * far_s[s, part(i), columns]
                tcol = tcol_s[part(i), :]
                gate = gate_s[s, 0:1, columns]
                for t in range(1, IDS):
                    gate = jnp.where(tcol == t, gate_s[s, t : t + 1, columns], gate)
                gated = (y + skip * x_s[s, part(i), columns]) * gate
                inverse = lax.rsqrt(jnp.mean(gated * gated, axis=1, keepdims=True) + EPSILON)
                normal = gated * inverse
                outs[i] = normal if outs[i] is None else outs[i] + normal
                cot = cot_ref[part(i), columns].astype(f32) * gain
                shared = jnp.mean(cot * normal, axis=1, keepdims=True)
                dy = (cot - normal * shared) * (inverse * gate)
                high, low = split(dy)
                highs.append(lanes_of([high, high]))
                lows.append(lanes_of([low, low]))
                row_terms = dy * y
                rate_row += jnp.sum(lcol * row_terms, axis=0, keepdims=True)
                bias_row += jnp.sum(acol_s[s, h, part(i), :] * row_terms, axis=0, keepdims=True)
                dh_s[s, part(i), columns], dl_s[s, part(i), columns] = split(grown * dy)
            pairs.append(mm(rows_of(highs + lows), x2_s[s, :, columns2], NT))
        for i in range(tiles):
            enc_ref[i * 128 : (i + 1) * 128, columns] = (outs[i] * gain).astype(enc_ref.dtype)
        return pairs, rate_row, bias_row

    def settle(h, factors, pairs, rate_row, bias_row):
        for s in range(2):
            column_sums = [jnp.zeros((1, 128), f32) for _ in range(tiles)]
            log_row = row_s[s, 0, h : h + 1, :]
            mixed_row = row_s[s, 2, h : h + 1, :]
            for i, j in factors[s]:
                e = pairs[s][part(i), part(j)] + pairs[s][part(tiles + i), part(j)]
                e = e * factors[s][i, j]
                q_s[s, part(i), part(j)] += e
                column_sums[j] = column_sums[j] + jnp.sum(e * score_s[s, part(i), part(j)], axis=0, keepdims=True)
            for j in range(tiles):
                rate_row -= log_row[:, part(j)] * column_sums[j]
                bias_row += mixed_row[:, part(j)] * column_sums[j]
        acc_s[0, h : h + 1, :] = rate_row
        acc_s[1, h : h + 1, :] = bias_row

    def reach_back(first):
        columns = slice(first * HEAD, (first + 2) * HEAD)
        for s in range(2):
            back = mm(lanes_of(own_c[s]), dh_s[s, :, columns], TN)
            back = back[:STATE] + back[STATE:] + mm(own_c[s][0], dl_s[s, :, columns], TN)
            back = rows_of(split(back))
            back_s[s, :, columns] = back
            reach = stacked(b_all, back)
            for h in (first, first + 1):
                at = 3 * s * heads + heads + h
                own = slice((h - first) * HEAD, (h - first + 1) * HEAD)
                whole = slice(h * HEAD, (h + 1) * HEAD)
                terms = reach[:, own] * rows_of([xw_s[:, whole], edge_s[:, whole]])
                acc_s[0, h : h + 1, :] += jnp.sum(terms * weights[:, at : at + 1], axis=0, keepdims=True)
                acc_s[1, h : h + 1, :] += jnp.sum(
                    terms * weights[:, at + heads : at + heads + 1], axis=0, keepdims=True
                )

    mixed = {0: mix(0)}
    enter(0)
    mixed[1] = mix(1)
    enter(1)
    for h in range(heads):
        if 1 <= h < heads - 1:
            mixed[h + 1] = mix(h + 1)
        factors, ys = mixed.pop(h)
        settle(h, factors, *gate_rows(h, ys))
        if h % 2 == 1:
            reach_back(h - 1)

    enc_copy = pltpu.make_async_copy(enc_ref, enc_hbm, enc_sem)
    enc_copy.start()

    db_all = jnp.zeros((ROWS, STATE), f32)
    dc_all = jnp.zeros((ROWS, STATE), f32)
    for s in range(2):
        q = split(q_s[s])
        grown = (dh_s[s], dl_s[s])
        far = stacked_out(grown, states[s], STATE, NT)
        dc_own = split(stacked_out(q, lanes_of(own_b[s]), STATE) + far)
        db_own = split(mm3(q, own_c[s], TN))
        both = mm(own_onehot[s], lanes_of([db_own[0], dc_own[0]])) + mm(own_onehot[s], lanes_of([db_own[1], dc_own[1]]))
        dc_all = dc_all + both[:, STATE:]
        db_all = db_all + both[:, :STATE] + stacked_out((wh_s[s], wl_s[s]), back_s[s], STATE, NT)
    d_summed = split(jnp.concatenate([db_all, dc_all], axis=1) * bc_slope)
    by_tap = mm(pick, d_summed[0], TN) + mm(pick, d_summed[1], TN)
    grad_ref[...] = jnp.zeros_like(grad_ref)
    for k in range(CONV):
        grad_ref[k : k + 1, :] = scale * jnp.sum(by_tap[8 * k : 8 * k + 8, :] * table_bc, axis=0, keepdims=True)
    place = iota((heads, 128), 1) == iota((heads, 128), 0) + tp_place * heads
    for i in range(2):
        sums = scale * jnp.sum(acc_s[i], axis=1, keepdims=True)
        grad_ref[CONV + i : CONV + i + 1, 0:128] = jnp.sum(jnp.where(place, sums, 0.0), axis=0, keepdims=True)
    enc_copy.wait()


def mixer(near, far, rc_map, skip, small, scale):
    devices, count = near.shape[0] + far.shape[0], near.shape[1]
    width = small[0].shape[1]
    heads = width // HEAD
    vmem = pl.BlockSpec(memory_space=pltpu.VMEM)
    hbm = pl.BlockSpec(memory_space=pl.ANY)
    scratch = [
        ((count, width), bf16),
        None,
        ((devices, count), jnp.int32),
        ((2, devices, count), jnp.int32),
        ((IDS, devices, count), f32),
        ((ROWS, devices * count), bf16),
        ((128, devices * count), bf16),
        ((WINDOWS, width), f32),
        ((WINDOWS, 2 * width), bf16),
        ((16, width), f32),
        ((2, ROWS, width), bf16),
        ((2, ROWS, width), bf16),
        ((2, count, width), f32),
        ((2, count, 2 * width), bf16),
        ((2, count, width), f32),
        ((2, count, width), bf16),
        ((2, count, width), bf16),
        ((2, 3, heads, count), f32),
        ((2, heads, count, 128), f32),
        ((2, heads, count, 128), f32),
        ((count, 128), f32),
        ((2, 8, width), f32),
        ((2, count, count), f32),
        ((2, count, count), f32),
        ((2, heads, 128), f32),
        ((2, 2 * STATE, width), bf16),
    ]

    def space(item):
        if isinstance(item, tuple):
            return pltpu.VMEM(*item)
        return pltpu.SemaphoreType.DMA((item,)) if item else pltpu.SemaphoreType.DMA

    return pl.pallas_call(
        functools.partial(mixer_kernel, scale),
        in_specs=[vmem] * (4 + len(small)),
        out_specs=[hbm, vmem],
        out_shape=[
            jax.ShapeDtypeStruct((count, width), bf16),
            jax.ShapeDtypeStruct((8, 2 * STATE), f32),
        ],
        scratch_shapes=[space(item) for item in scratch],
        compiler_params=pltpu.CompilerParams(vmem_limit_bytes=MIXER_VMEM),
        name="mixer",
    )(
        near,
        far,
        rc_map.reshape(1, IDS),
        skip.reshape(1, heads),
        *small,
    )


def exchange(value, axis, distance):
    size = lax.axis_size(axis)
    return lax.ppermute(value, axis, [(i, i ^ distance) for i in range(size)])


def on_device(
    tokens,
    rc_map,
    embedding,
    norm_gain,
    w_values,
    w_gates,
    w_states,
    w_steps,
    conv_values,
    conv_states,
    step_bias,
    log_rate,
    skip_gain,
    head_gain,
    cotangent,
):
    devices = lax.axis_size("ctx")
    count = tokens.shape[0]
    scale = 1.0 / math.sqrt(count * devices * HEAD)
    embedded = embedding.astype(f32)
    mean = jnp.mean(embedded * embedded, axis=1, keepdims=True)
    normed = (embedded * lax.rsqrt(mean + EPSILON) * norm_gain).astype(bf16)
    near = jnp.minimum(tokens, IDS - 1).reshape(1, count)
    far = exchange(tokens.reshape(1, count), "ctx", 1)
    tv = tbc = None
    distance = 2
    while distance < devices:
        near = jnp.concatenate([near, far], axis=0)
        if distance == 2:
            near, normed = lax.optimization_barrier((near, normed))
        if distance * 2 >= devices:
            tbc, tv = tables(normed, [w_states, w_values], [2, 8])
            near, tbc, tv, normed = lax.optimization_barrier((near, tbc, tv, normed))
        far = exchange(near, "ctx", distance)
        distance *= 2
    if tv is None:
        tbc, tv = tables(normed, [w_states, w_values], [2, 8])
    (tz,) = tables(normed, [w_gates], [8])
    dt = lax.dot_general(w_steps, normed, (((0,), (1,)), ((), ())), preferred_element_type=f32)
    small = [
        tv,
        tbc,
        tz,
        dt,
        conv_values,
        conv_states,
        step_bias.reshape(1, -1),
        log_rate.reshape(1, -1),
        head_gain.reshape(1, -1),
        cotangent,
    ]
    encoded, grads = mixer(near, far, rc_map, skip_gain, small, scale)
    for axis in ("tp", "ctx"):
        distance = 1
        while distance < lax.axis_size(axis):
            grads = grads + exchange(grads, axis, distance)
            distance *= 2
    head_total = log_rate.shape[0] * lax.axis_size("tp")
    return (encoded, grads[CONV, :head_total], grads[CONV + 1, :head_total], grads[:CONV])


def solution(mesh):
    placed = (
        P("ctx"),
        P(),
        P(),
        P(),
        P(None, "tp"),
        P(None, "tp"),
        P(),
        P(None, "tp"),
        P(None, "tp"),
        P(),
        P("tp"),
        P("tp"),
        P("tp"),
        P("tp"),
        P("ctx", "tp"),
    )
    return jax.shard_map(
        on_device,
        mesh=mesh,
        in_specs=placed,
        out_specs=(P("ctx", "tp"), P(), P(), P()),
        check_vma=False,
    )
```
